32 devices in a mesh: parts: 2 (over y), dp: 4 (over z), tensor: 2 (over x), sub: 2 (over core).
Axes of the slice: x: 2, y: 2, z: 4, core: 2. Of those that a mesh axis runs over, the one named last changes fastest.
Arguments:
- tokens: bfloat16 [8, 8, 128, 8192], P(('parts', 'dp'), None, 'sub', 'tensor'), parts along dimension 0, may hold values from -6 to 6
- cotangent: bfloat16 [8, 8, 128, 1024], P(('parts', 'dp'), None, 'sub', 'tensor'), parts along dimension 0, may hold values from -6 to 6
- frozen_value_weight: bfloat16 [8192, 1024], P('tensor', 'dp'), may hold values from -0.0625 to 0.0625
- adapter_down: bfloat16 [8, 16, 8192], P(('parts', 'dp'), None, 'tensor'), parts along dimension 0, may hold values from -0.25 to 0.25
- adapter_up: bfloat16 [8, 16, 1024], P(('parts', 'dp'), None, 'tensor'), parts along dimension 0, may hold values from -0.375 to 0.375
- tokens_per_job: int32 [8], P('parts'), parts along dimension 0, may hold values from 1 to 1920, as said below
- packed_block_slots: int32 [8, 8], P('parts'), parts along dimension 0, may hold values from 0 to 31, as said below
Outputs:
- layer_output: bfloat16 [8, 8, 128, 1024], P(('parts', 'dp'), None, 'sub', 'tensor'), parts along dimension 0
- token_gradient: bfloat16 [8, 8, 128, 8192], P(('parts', 'dp'), None, 'sub', 'tensor'), parts along dimension 0
- grad_down: float32 [8, 16, 8192], P(('parts', 'dp'), None, 'tensor'), parts along dimension 0
- grad_up: float32 [8, 16, 1024], P(('parts', 'dp'), None, 'tensor'), parts along dimension 0
The draws below stay inside these ranges and needn't reach their ends.
There are 2 independent parts, one for each index of `parts`. The reference program is written for one: setup_inputs(seed, part) draws one part's arguments, and reference() takes and returns one part's arrays. A program takes and returns all parts, laid end to end along the dimension named above; an argument that names none is the same for every part. Nothing has to cross between parts.
Inputs may be any that keep to these rules, and one draw needn't show every extreme that they name: The block counts ceil(tokens_per_job[j] / 128) add up to 32. `packed_block_slots`: A permutation of the packed slots 0 to 31. Every index of dp receives 8 blocks, and no index of dp sends more than 2 of its blocks to one index of dp.
All inputs are finite; a program needn't handle non-finite values.
Results may differ from the reference program's by a relative error of at most 0.015.
Values may be sent and summed in bfloat16 or wider, within the bound.
No kernel may reach another device: no remote copies, remote signals or barrier semaphores. Data moves between devices by JAX's collectives and lax.ppermute only.
A program may use at most 64 MiB of HBM per device.

```python
import jax
import jax.numpy as jnp
from jax import lax

MODEL_WIDTH = 8192
VALUE_WIDTH = 1024
ADAPTER_RANK = 16
BLOCK = 128
BLK_DEV = 8
JOB_DEV = 1
JOB_TOTAL_SIZE = 4
N_DP = 4
N_TENSOR = 2


def mixed_rows(key, shape):
    key_noise = jax.random.fold_in(key, 1)
    noise = jax.random.normal(key_noise, shape, jnp.float32)
    return jnp.clip(noise, -6.0, 6.0)


def draw_tokens(key, part):
    key = jax.random.fold_in(key, 31)
    values = mixed_rows(key, (N_DP, BLK_DEV, BLOCK, MODEL_WIDTH))
    return values.astype(jnp.bfloat16)


def draw_cotangent(key, part):
    key = jax.random.fold_in(key, 37)
    values = mixed_rows(key, (N_DP, BLK_DEV, BLOCK, VALUE_WIDTH))
    return values.astype(jnp.bfloat16)


def draw_tokens_per_job(key, part):
    key = jax.random.fold_in(key, 11)
    job_total = JOB_DEV * N_DP
    spare_blocks = N_DP * BLK_DEV - job_total
    heavy_extra = (spare_blocks + 1) // 2
    other_spare = spare_blocks - heavy_extra
    key_one, key_two, key_three, key_four = jax.random.split(key, 4)
    pick_one = jax.random.randint(key_one, (other_spare,), 0, job_total - 2)
    pick_two = jax.random.randint(key_two, (other_spare,), 0, job_total - 2)
    favored = jnp.minimum(pick_one, pick_two) + 1
    shuffle = jax.random.permutation(key_three, job_total)
    target = shuffle[favored]
    job_range = jnp.arange(job_total, dtype=jnp.int32)
    extra_blocks = jnp.sum((target[:, None] == job_range[None, :]).astype(jnp.int32), axis=0)
    extra_blocks = extra_blocks + jnp.where(job_range == shuffle[0], heavy_extra, 0)
    last_fill = jax.random.randint(key_four, (job_total,), 1, BLOCK + 1)
    last_fill = jnp.where(job_range == shuffle[0], BLOCK, last_fill)
    last_fill = jnp.where(job_range == shuffle[job_total - 1], 1, last_fill)
    return (BLOCK * extra_blocks + last_fill).astype(jnp.int32)


def permutations(key, count, length):
    key_list = jax.random.split(key, count)
    return jax.vmap(partial_permutation, in_axes=(0, None))(key_list, length)


def partial_permutation(key, length):
    return jax.random.permutation(key, length)


def draw_packed_block_slots(key, part):
    key = jax.random.fold_in(key, 23)
    key_list = jax.random.split(key, 5)
    spans = (BLK_DEV + N_DP - 1) // N_DP
    offset_src = jax.random.permutation(key_list[0], N_DP)
    relabel = jax.random.permutation(key_list[1], N_DP)
    offset_pos = permutations(key_list[2], spans, N_DP).reshape(-1)[:BLK_DEV]
    position = permutations(key_list[3], N_DP, BLK_DEV)
    summed = (offset_pos[position] + offset_src[:, None]) % N_DP
    dest_group = relabel[summed]
    slot_perm = permutations(key_list[4], N_DP, BLK_DEV)
    dest_slot = slot_perm[dest_group, position]
    return (dest_group * BLK_DEV + dest_slot).astype(jnp.int32)


def level_of(own_key, dims, cuts, least, largest):
    loudness, own = 1.0, jax.random.fold_in(own_key, 6)
    for axis_at, shards_of in cuts:
        steps = jnp.exp(jax.random.uniform(jax.random.fold_in(own, axis_at), (shards_of,), jnp.float32, least / len(cuts), largest / len(cuts)))
        loudness = loudness * jnp.repeat(steps, dims[axis_at] // shards_of).reshape([-1 if axis == axis_at else 1 for axis in range(len(dims))])
    return loudness


def gaussian(key, dims, scale, reach, cuts=(), kind=jnp.bfloat16):
    result = jax.random.normal(key, dims, jnp.float32) * scale
    if len(cuts) > 0:
        result = level_of(key, dims, cuts, -0.22, 0.18) * result
    return jnp.clip(result, min=-reach, max=reach).astype(kind)


def setup_inputs(seed: int = 0, part: int = 0) -> dict:
    splits = jax.random.split(jax.random.key(seed), 8)
    own_keys = jax.random.split(jax.random.fold_in(splits[7], part), 8)
    tokens = draw_tokens(jax.random.fold_in(jax.random.fold_in(splits[7], part), 71), part)
    cotangent = draw_cotangent(jax.random.fold_in(jax.random.fold_in(splits[7], part), 71), part)
    frozen_value_weight = gaussian(splits[2], (MODEL_WIDTH, VALUE_WIDTH), MODEL_WIDTH ** -0.5, 0.0625, ((0, 2), (1, 4)))
    adapter_down = gaussian(own_keys[3], (JOB_TOTAL_SIZE, ADAPTER_RANK, MODEL_WIDTH), (4.0 / MODEL_WIDTH ** 0.5), 0.25, ((0, 4), (2, 2)))
    adapter_up = gaussian(own_keys[4], (JOB_TOTAL_SIZE, ADAPTER_RANK, VALUE_WIDTH), (0.25 / ADAPTER_RANK ** 0.5), 0.375, ((0, 4), (2, 2)))
    tokens_per_job = draw_tokens_per_job(jax.random.fold_in(jax.random.fold_in(splits[7], part), 71), part)
    packed_block_slots = draw_packed_block_slots(jax.random.fold_in(jax.random.fold_in(splits[7], part), 71), part)
    return dict(tokens=tokens, cotangent=cotangent, frozen_value_weight=frozen_value_weight, adapter_down=adapter_down, adapter_up=adapter_up, tokens_per_job=tokens_per_job, packed_block_slots=packed_block_slots)


adapter_scale = 2.0


def block_facts(tokens_per_job, block_ids, block_rows):
    job_total = tokens_per_job.shape[0]
    blocks = (tokens_per_job + (block_rows - 1)) // block_rows
    block_ends = jnp.cumsum(blocks, dtype=jnp.int32)
    starts = block_ends - blocks
    job_index = jnp.sum((block_ends[None, :] <= block_ids[:, None]).astype(jnp.int32), axis=1, dtype=jnp.int32)
    chosen = job_index[:, None] == jnp.arange(job_total, dtype=jnp.int32)[None, :]
    job_count = jnp.sum(jnp.where(chosen, tokens_per_job[None, :], 0), axis=1, dtype=jnp.int32)
    first_block = jnp.sum(jnp.where(chosen, starts[None, :], 0), axis=1, dtype=jnp.int32)
    valid_rows = jnp.clip(job_count - block_rows * (block_ids - first_block), 0, block_rows)
    return job_index, chosen, valid_rows


def reference(tokens, cotangent, frozen_value_weight, adapter_down, adapter_up, tokens_per_job, packed_block_slots):
    highest_precision = lax.Precision.HIGHEST
    block_total = N_DP * BLK_DEV
    feature_width = MODEL_WIDTH // N_TENSOR
    slot_table = packed_block_slots.reshape(block_total).astype(jnp.int32)
    block_order = jnp.arange(block_total, dtype=jnp.int32)
    block_of = jnp.zeros((block_total,), jnp.int32).at[slot_table].set(block_order)
    packed = jnp.zeros((block_total, BLOCK, MODEL_WIDTH), jnp.bfloat16).at[slot_table].set(tokens.reshape(block_total, BLOCK, MODEL_WIDTH))
    job_index, chosen, valid_rows = block_facts(tokens_per_job.astype(jnp.int32), block_of, BLOCK)
    row_valid_mask = (jnp.arange(BLOCK, dtype=jnp.int32)[None, :] < valid_rows[:, None]).astype(jnp.float32)
    masked_grad = jnp.where(row_valid_mask[:, :, None] > 0, cotangent.reshape(block_total, BLOCK, VALUE_WIDTH), jnp.zeros((), jnp.bfloat16))
    onehot = chosen.astype(jnp.float32)
    weight_full = frozen_value_weight.astype(jnp.float32)
    weight_split = weight_full.reshape(N_TENSOR, feature_width, VALUE_WIDTH)

    def group_step(items):
        block_tokens, block_grad, job_of_block, block_valid_mask, block_hot = items
        selected_down = adapter_down[job_of_block].astype(jnp.float32)
        selected_up = adapter_up[job_of_block].astype(jnp.float32)
        tokens_f = block_tokens.astype(jnp.float32)
        grad_f = block_grad.astype(jnp.float32)
        products = jnp.einsum('bhtf,tfk->bhtk', tokens_f.reshape(BLK_DEV, BLOCK, N_TENSOR, feature_width), weight_split, precision=highest_precision)
        rounded = lax.optimization_barrier(products.astype(jnp.bfloat16))
        frozen_sum = jnp.sum(rounded.astype(jnp.float32), axis=2)
        down_sum = jnp.einsum('bhf,brf->bhr', tokens_f, selected_down, precision=highest_precision)
        downward_rounded = lax.optimization_barrier(down_sum.astype(jnp.bfloat16)).astype(jnp.float32)
        adapter_output = jnp.einsum('poz,pzv->pov', downward_rounded, selected_up, precision=highest_precision)
        layer_output = ((frozen_sum + adapter_scale * adapter_output) * block_valid_mask[:, :, None]).astype(jnp.bfloat16)
        back_sum = jnp.einsum('bhk,brk->bhr', grad_f, selected_up, precision=highest_precision)
        backward_rounded = lax.optimization_barrier(back_sum.astype(jnp.bfloat16)).astype(jnp.float32)
        frozen_gradient = jnp.einsum('bhk,fk->bhf', grad_f, weight_full, precision=highest_precision)
        adapter_gradient = jnp.einsum('jpy,jyu->jpu', backward_rounded, selected_down, precision=highest_precision)
        token_gradient = (frozen_gradient + adapter_scale * adapter_gradient).astype(jnp.bfloat16)
        down_blocks = jnp.einsum('bhr,bhf->brf', backward_rounded, tokens_f, precision=highest_precision)
        up_blocks = jnp.einsum('bhr,bhk->brk', downward_rounded, grad_f, precision=highest_precision)
        table_down = jnp.einsum('bj,brf->jrf', block_hot, down_blocks, precision=highest_precision)
        table_up = jnp.einsum('bj,brk->jrk', block_hot, up_blocks, precision=highest_precision)
        return layer_output, token_gradient, table_down, table_up

    items = (packed.reshape(N_DP, BLK_DEV, BLOCK, MODEL_WIDTH), masked_grad.reshape(N_DP, BLK_DEV, BLOCK, VALUE_WIDTH),
             job_index.reshape(N_DP, BLK_DEV), row_valid_mask.reshape(N_DP, BLK_DEV, BLOCK),
             onehot.reshape(N_DP, BLK_DEV, JOB_TOTAL_SIZE))
    layer_output, token_gradient, table_down, table_up = lax.map(group_step, items)
    scale_factor = adapter_scale / tokens_per_job.astype(jnp.float32)
    grad_down = jnp.sum(table_down, axis=0) * scale_factor[:, None, None]
    grad_up = jnp.sum(table_up, axis=0) * scale_factor[:, None, None]
    return layer_output, token_gradient, grad_down, grad_up
```

```python
import jax
import jax.numpy as jnp
from jax import lax
from jax.sharding import PartitionSpec as P

adapter_scale = 2.0


def block_facts(tokens_per_job, block_ids, block_rows):
    job_total = tokens_per_job.shape[0]
    blocks = (tokens_per_job + (block_rows - 1)) // block_rows
    block_ends = jnp.cumsum(blocks, dtype=jnp.int32)
    starts = block_ends - blocks
    job_index = jnp.sum(
        (block_ends[None, :] <= block_ids[:, None]).astype(jnp.int32), axis=1, dtype=jnp.int32
    )
    chosen = job_index[:, None] == jnp.arange(job_total, dtype=jnp.int32)[None, :]
    job_count = jnp.sum(jnp.where(chosen, tokens_per_job[None, :], 0), axis=1, dtype=jnp.int32)
    first_block = jnp.sum(jnp.where(chosen, starts[None, :], 0), axis=1, dtype=jnp.int32)
    valid_rows = jnp.clip(job_count - block_rows * (block_ids - first_block), 0, block_rows)
    return job_index, valid_rows


def shifted(values, axis, count, step):
    if step % count == 0:
        return values
    return lax.ppermute(values, axis, [(i, (i + step) % count) for i in range(count)])


def gather_shifts(values, axis, count):
    return [shifted(values, axis, count, d) for d in range(count)]


def body(
    tokens,
    cotangent,
    frozen_value_weight,
    adapter_down,
    adapter_up,
    tokens_per_job,
    packed_block_slots,
):
    nd, nt, ns, np_ = (lax.axis_size(a) for a in ("dp", "tensor", "sub", "parts"))
    z, t, s, p = (lax.axis_index(a) for a in ("dp", "tensor", "sub", "parts"))
    blocks, halved, width = tokens.shape[1:]
    heads = cotangent.shape[3]
    jobs_dev, rank, _ = adapter_down.shape
    cap = -(-blocks // nd)
    rows = blocks * halved
    f32, bf16, i32 = jnp.float32, jnp.bfloat16, jnp.int32

    quarter = width // (np_ * ns)
    own_quarter = lax.dynamic_slice_in_dim(
        frozen_value_weight, (p * ns + s) * quarter, quarter, axis=0
    )
    weight_all = lax.all_gather(own_quarter, ("dp", "parts", "sub"), axis=0, tiled=True)
    weight_all = weight_all.reshape(nd, width, -1)

    grad_rel = gather_shifts(cotangent[0], "tensor", nt)
    up_rel = jnp.concatenate(gather_shifts(adapter_up, "tensor", nt), axis=2)
    maps = jnp.concatenate([adapter_down, up_rel], axis=2)
    maps = jnp.concatenate(gather_shifts(maps, "dp", nd), axis=0).reshape(nd * jobs_dev * rank, -1)
    down_cat, up_cat = maps[:, :width], maps[:, width:]

    positions = jnp.arange(blocks, dtype=i32)
    dest = packed_block_slots // blocks
    same = dest[:, :, None] == dest[:, None, :]
    earlier = positions[None, None, :] < positions[None, :, None]
    send_rank = jnp.sum((same & earlier).astype(i32), axis=2, dtype=i32)
    flat_slots = packed_block_slots.reshape(-1)
    flat_ids = jnp.arange(nd * blocks, dtype=i32)
    slot_owner = flat_slots[None, :] == (z * blocks + positions)[:, None]
    block_ids = jnp.sum(jnp.where(slot_owner, flat_ids[None, :], 0), axis=1, dtype=i32)
    in_rank = jnp.sum(jnp.where(slot_owner, send_rank.reshape(-1)[None, :], 0), axis=1, dtype=i32)
    in_slot = (z - block_ids // blocks) % nd * cap + in_rank
    own_dest = lax.dynamic_index_in_dim(dest, z, 0, keepdims=False)
    own_rank = lax.dynamic_index_in_dim(send_rank, z, 0, keepdims=False)
    out_slot = (own_dest - z) % nd * cap + own_rank

    slot_range = jnp.arange(nd * cap, dtype=i32)

    def positions_of(slots):
        match = slots[None, :] == slot_range[:, None]
        return jnp.sum(jnp.where(match, positions[None, :], 0), axis=1, dtype=i32), jnp.any(match, axis=1)

    out_pos, out_filled = positions_of(out_slot)
    in_pos, in_filled = positions_of(in_slot)

    def exchange(values, picks, filled, back, direction):
        ordered = jnp.where(filled[:, None, None], jnp.take(values, picks, axis=0), 0).astype(values.dtype)
        ordered = ordered.reshape(nd, cap, *values.shape[1:])
        got = [shifted(ordered[d], "dp", nd, direction * d) for d in range(nd)]
        return jnp.take(jnp.concatenate(got, axis=0), back, axis=0)

    def facts(ids):
        job, valid = block_facts(tokens_per_job, ids, halved * ns)
        row = s * halved + jnp.arange(halved, dtype=i32)
        mask = row[None, :] < valid[:, None]
        rel = (z - job // jobs_dev) % nd * jobs_dev + job % jobs_dev
        hot = rel[:, None] == jnp.arange(nd * jobs_dev, dtype=i32)[None, :]
        return mask, hot

    out_mask, out_hot = facts(z * blocks + positions)
    in_mask, in_hot = facts(block_ids)

    def pick(wide, hot):
        wide = wide.reshape(blocks, halved, nd * jobs_dev, rank)
        return jnp.sum(jnp.where(hot[:, None, :, None], wide, 0.0), axis=2)

    def spread(narrow, hot):
        wide = jnp.where(hot[:, None, :, None], narrow[:, :, None, :], 0).astype(narrow.dtype)
        return wide.reshape(rows, nd * jobs_dev * rank)

    def dot(a, b, dims):
        return lax.dot_general(a, b, (dims, ((), ())), preferred_element_type=f32)

    grad_rel_cat = jnp.concatenate(grad_rel, axis=2)
    grad_rel_cat = jnp.where(in_mask[:, :, None], grad_rel_cat, 0).astype(bf16).reshape(rows, -1)
    own_grad = grad_rel_cat[:, :heads]
    back_sum = pick(dot(grad_rel_cat, up_cat, ((1,), (1,))), in_hot).astype(bf16)
    back_wide = spread(back_sum, in_hot)

    own_tokens = tokens[0].reshape(rows, width)
    down_part = pick(dot(own_tokens, down_cat, ((1,), (1,))), out_hot).astype(bf16)
    down_parts = gather_shifts(down_part, "tensor", nt)
    down_sum = sum(x.astype(f32) for x in down_parts).astype(bf16)
    down_wide = spread(down_sum, out_hot)

    back_at_tokens = exchange(back_sum, in_pos, in_filled, out_slot, -1)
    down_at_grad = exchange(down_sum, out_pos, out_filled, in_slot, 1)
    table_down = dot(spread(back_at_tokens, out_hot), own_tokens, ((0,), (0,)))
    table_up = dot(spread(down_at_grad, in_hot), own_grad, ((0,), (0,)))
    table = jnp.concatenate([table_down, table_up], axis=1).reshape(nd * jobs_dev, ns, rank // ns, -1)

    def half(index):
        return lax.dynamic_index_in_dim(table, index, 1, keepdims=False)

    summed = half(s)
    for d in range(1, ns):
        summed = summed + shifted(half((s + d) % ns), "sub", ns, d)
    summed = summed.reshape(nd, jobs_dev, rank // ns, -1)
    total = summed[0].astype(bf16).astype(f32)
    for d in range(1, nd):
        total = total + shifted(summed[d].astype(bf16), "dp", nd, -d).astype(f32)
    halves = jnp.stack(gather_shifts(total, "sub", ns), axis=1)
    order = (s - jnp.arange(ns, dtype=i32)) % ns
    owned = jnp.take(halves, order, axis=1).reshape(jobs_dev, rank, -1)
    counts = lax.dynamic_slice_in_dim(tokens_per_job, z * jobs_dev, jobs_dev).astype(f32)
    owned = owned * (adapter_scale / counts)[:, None, None]
    grad_down, grad_up = owned[:, :, :width], owned[:, :, width:]

    base = jnp.concatenate([dot(own_tokens, weight_all[i], ((1,), (0,))).astype(bf16) for i in range(nd)], axis=1)
    base = base.reshape(rows, nt, heads)
    frozen = lax.dynamic_index_in_dim(base, t, 1, keepdims=False).astype(f32)
    for d in range(1, nt):
        frozen = frozen + shifted(
            lax.dynamic_index_in_dim(base, (t + d) % nt, 1, keepdims=False), "tensor", nt, d
        ).astype(f32)
    adapter_out = dot(down_wide, up_cat[:, :heads], ((1,), (0,)))
    layer = (frozen + adapter_scale * adapter_out).reshape(blocks, halved, heads)
    layer = jnp.where(out_mask[:, :, None], layer, 0.0).astype(bf16)
    layer_output = exchange(layer, out_pos, out_filled, in_slot, 1)

    grad_abs = jnp.take(
        grad_rel_cat.reshape(rows, nt, heads), (t - jnp.arange(nt, dtype=i32)) % nt, axis=1
    ).reshape(rows, nd, -1)
    gradient = adapter_scale * dot(back_wide, down_cat, ((1,), (0,)))
    for i in range(nd):
        gradient = gradient + dot(grad_abs[:, i], weight_all[i], ((1,), (1,)))
    token_gradient = gradient.astype(bf16).reshape(blocks, halved, width)
    return layer_output[None], token_gradient[None], grad_down, grad_up


def solution(mesh):
    return jax.shard_map(
        body,
        mesh=mesh,
        in_specs=(
            P(("parts", "dp"), None, "sub", "tensor"),
            P(("parts", "dp"), None, "sub", "tensor"),
            P("tensor", "dp"),
            P(("parts", "dp"), None, "tensor"),
            P(("parts", "dp"), None, "tensor"),
            P("parts"),
            P("parts", None),
        ),
        out_specs=(
            P(("parts", "dp"), None, "sub", "tensor"),
            P(("parts", "dp"), None, "sub", "tensor"),
            P(("parts", "dp"), None, "tensor"),
            P(("parts", "dp"), None, "tensor"),
        ),
        check_vma=False,
    )
```

```python
import functools

import jax
import jax.numpy as jnp
from jax import lax
from jax.experimental import pallas as pl
from jax.experimental.pallas import tpu as pltpu
from jax.sharding import PartitionSpec as P

adapter_scale = 2.0


def block_facts(tokens_per_job, block_ids, block_rows):
    job_total = tokens_per_job.shape[0]
    blocks = (tokens_per_job + (block_rows - 1)) // block_rows
    block_ends = jnp.cumsum(blocks, dtype=jnp.int32)
    starts = block_ends - blocks
    job_index = jnp.sum(
        (block_ends[None, :] <= block_ids[:, None]).astype(jnp.int32), axis=1, dtype=jnp.int32
    )
    chosen = job_index[:, None] == jnp.arange(job_total, dtype=jnp.int32)[None, :]
    job_count = jnp.sum(jnp.where(chosen, tokens_per_job[None, :], 0), axis=1, dtype=jnp.int32)
    first_block = jnp.sum(jnp.where(chosen, starts[None, :], 0), axis=1, dtype=jnp.int32)
    valid_rows = jnp.clip(job_count - block_rows * (block_ids - first_block), 0, block_rows)
    return job_index, valid_rows


def shifted(values, axis, count, step):
    if step % count == 0:
        return values
    return lax.ppermute(values, axis, [(i, (i + step) % count) for i in range(count)])


def gather_shifts(values, axis, count):
    return [shifted(values, axis, count, d) for d in range(count)]


def dot(a, b, dims):
    return lax.dot_general(a, b, (dims, ((), ())), preferred_element_type=jnp.float32)


def piece_specs(piece_list, tile, per, whole_rows):
    specs = []
    for d, shard in enumerate(piece_list):
        for r in range(len(shard)):
            columns = shard[r].shape[1]
            if d == 0 and whole_rows:
                index = lambda i, q, r=r: (q[r] * per + jnp.clip(i - r * per, 0, per - 1), 0)
            else:
                index = lambda i, q, r=r: (jnp.clip(i - r * per, 0, per - 1), 0)
            specs.append(pl.BlockSpec((tile, columns), index))
    return specs


def base_kernel(fq, q, tokens, *refs):
    pieces, out = refs[:-1], refs[-1]
    total = None
    for r, piece in enumerate(pieces):
        start = pl.multiple_of(q[r] * fq, fq)
        part = dot(tokens[:, pl.ds(start, fq)], piece[...], ((1,), (0,)))
        total = part if total is None else total + part
    out[...] = total.astype(out.dtype)


def base_product(tokens, pieces, quarters, own, name):
    rows, width = tokens.shape
    fq = width // len(pieces)
    columns = pieces[0].shape[1]
    steps = 4
    if own:
        specs = [pl.BlockSpec((fq, columns), lambda i, q, r=r: (q[r], 0)) for r in range(len(pieces))]
    else:
        specs = [pl.BlockSpec((fq, columns), lambda i, q: (0, 0)) for _ in pieces]
    return pl.pallas_call(
        functools.partial(base_kernel, fq),
        out_shape=jax.ShapeDtypeStruct((rows, columns), jnp.bfloat16),
        grid_spec=pltpu.PrefetchScalarGridSpec(
            num_scalar_prefetch=1,
            grid=(steps,),
            in_specs=[pl.BlockSpec((rows // steps, width), lambda i, q: (i, 0))] + specs,
            out_specs=pl.BlockSpec((rows // steps, columns), lambda i, q: (i, 0)),
        ),
        compiler_params=pltpu.CompilerParams(vmem_limit_bytes=16 << 20),
        cost_estimate=pl.CostEstimate(
            flops=2 * rows * width * columns,
            bytes_accessed=2 * (rows * width + width * columns + rows * columns),
            transcendentals=0,
        ),
        name=name,
    )(quarters, tokens, *pieces)


def gradient_kernel(nq, per, q, grad, back, down, *refs):
    pieces, out = refs[:-1], refs[-1]
    shards = len(pieces) // nq
    step = pl.program_id(0)
    for r in range(nq):

        @pl.when(step // per == r)
        def _():
            total = adapter_scale * dot(back[...], down[...], ((1,), (0,)))
            for d in range(shards):
                total = total + dot(grad[d], pieces[d * nq + r][...], ((1,), (1,)))
            out[...] = total.astype(out.dtype)


def token_gradient_of(grad, back, down, piece_list, quarters, width):
    shards, rows, columns = grad.shape
    nq = len(piece_list[0])
    fq = width // nq
    tile = min(512, fq)
    per = fq // tile
    place = lambda i, q: (0, q[i // per] * per + i % per)
    flat = [x for shard in piece_list for x in shard]
    return pl.pallas_call(
        functools.partial(gradient_kernel, nq, per),
        out_shape=jax.ShapeDtypeStruct((rows, width), jnp.bfloat16),
        grid_spec=pltpu.PrefetchScalarGridSpec(
            num_scalar_prefetch=1,
            grid=(nq * per,),
            in_specs=[
                pl.BlockSpec(grad.shape, lambda i, q: (0, 0, 0)),
                pl.BlockSpec(back.shape, lambda i, q: (0, 0)),
                pl.BlockSpec((down.shape[0], tile), place),
            ]
            + piece_specs(piece_list, tile, per, True),
            out_specs=pl.BlockSpec((rows, tile), place),
        ),
        compiler_params=pltpu.CompilerParams(vmem_limit_bytes=32 << 20),
        cost_estimate=pl.CostEstimate(
            flops=2 * rows * width * (shards * columns + down.shape[0]),
            bytes_accessed=2 * (rows * width + shards * columns * (width + rows)),
            transcendentals=0,
        ),
        name="token_gradient",
    )(quarters, grad, back, down, *flat)


def table_kernel(tiles, back, down, tokens, grad, mine, theirs):
    half = mine.shape[0]
    step = pl.program_id(0)

    def put(wide, values):
        total = dot(wide[...], values[...], ((1,), (0,)))
        mine[...] = total[:half]
        theirs[...] = total[half:]

    @pl.when(step < tiles)
    def _():
        put(back, tokens)

    @pl.when(step == tiles)
    def _():
        put(down, grad)


def tables_of(back, down, tokens, grad):
    total_rank, rows = back.shape
    width, heads = tokens.shape[1], grad.shape[1]
    tiles = width // heads
    half = total_rank // 2
    shape = jax.ShapeDtypeStruct((half, width + heads), jnp.float32)
    out = pl.BlockSpec((half, heads), lambda i: (0, i))
    return pl.pallas_call(
        functools.partial(table_kernel, tiles),
        out_shape=(shape, shape),
        grid=(tiles + 1,),
        in_specs=[
            pl.BlockSpec(back.shape, lambda i: (0, 0)),
            pl.BlockSpec(down.shape, lambda i: (0, 0)),
            pl.BlockSpec((rows, heads), lambda i: (0, jnp.minimum(i, tiles - 1))),
            pl.BlockSpec((rows, heads), lambda i: (0, 0)),
        ],
        out_specs=(out, out),
        compiler_params=pltpu.CompilerParams(vmem_limit_bytes=16 << 20),
        cost_estimate=pl.CostEstimate(
            flops=2 * total_rank * rows * (width + heads),
            bytes_accessed=2 * rows * (width + heads) + 4 * total_rank * (width + heads),
            transcendentals=0,
        ),
        name="job_tables",
    )(back, down, tokens, grad)


def body(
    tokens,
    cotangent,
    frozen_value_weight,
    adapter_down,
    adapter_up,
    tokens_per_job,
    packed_block_slots,
):
    nd, nt, ns, np_ = (lax.axis_size(a) for a in ("dp", "tensor", "sub", "parts"))
    z, t, s, p = (lax.axis_index(a) for a in ("dp", "tensor", "sub", "parts"))
    blocks, halved, width = tokens.shape[1:]
    heads = cotangent.shape[3]
    jobs_dev, rank, _ = adapter_down.shape
    columns = frozen_value_weight.shape[1]
    cap = -(-blocks // nd)
    rows = blocks * halved
    r2 = rank // ns
    f32, bf16, i32 = jnp.float32, jnp.bfloat16, jnp.int32

    maps = jnp.concatenate([adapter_down, adapter_up], axis=2).reshape(jobs_dev, ns, r2, width + heads)
    maps = lax.dynamic_index_in_dim(maps, s, 1, keepdims=False)
    maps = jnp.concatenate(gather_shifts(maps, "dp", nd), axis=0).reshape(nd * jobs_dev * r2, -1)
    maps = jnp.concatenate(gather_shifts(maps, "sub", ns), axis=0)
    down_cat, up_cat = maps[:, :width], maps[:, width:]

    nq = np_ * ns
    quarter = width // nq
    quarters = jnp.stack([(p - a) % np_ * ns + (s - b) % ns for a in range(np_) for b in range(ns)])
    quarters = quarters.astype(i32)
    moving = lax.dynamic_slice_in_dim(frozen_value_weight, quarters[0] * quarter, quarter, axis=0)
    piece_list = [[frozen_value_weight] * nq]
    for d in range(1, nd):
        moving = shifted(moving, "dp", nd, 1)
        piece_list.append(
            [x for y in gather_shifts(moving, "parts", np_) for x in gather_shifts(y, "sub", ns)]
        )

    grad_rel = gather_shifts(cotangent[0], "tensor", nt)

    positions = jnp.arange(blocks, dtype=i32)
    dest = packed_block_slots // blocks
    same = dest[:, :, None] == dest[:, None, :]
    earlier = positions[None, None, :] < positions[None, :, None]
    send_rank = jnp.sum((same & earlier).astype(i32), axis=2, dtype=i32)
    flat_slots = packed_block_slots.reshape(-1)
    flat_ids = jnp.arange(nd * blocks, dtype=i32)
    slot_owner = flat_slots[None, :] == (z * blocks + positions)[:, None]
    block_ids = jnp.sum(jnp.where(slot_owner, flat_ids[None, :], 0), axis=1, dtype=i32)
    in_rank = jnp.sum(jnp.where(slot_owner, send_rank.reshape(-1)[None, :], 0), axis=1, dtype=i32)
    in_slot = (z - block_ids // blocks) % nd * cap + in_rank
    own_dest = lax.dynamic_index_in_dim(dest, z, 0, keepdims=False)
    own_rank = lax.dynamic_index_in_dim(send_rank, z, 0, keepdims=False)
    out_slot = (own_dest - z) % nd * cap + own_rank
    slot_range = jnp.arange(nd * cap, dtype=i32)

    def positions_of(slots):
        match = slots[None, :] == slot_range[:, None]
        return jnp.sum(jnp.where(match, positions[None, :], 0), axis=1, dtype=i32), jnp.any(match, axis=1)

    out_pos, out_filled = positions_of(out_slot)
    in_pos, in_filled = positions_of(in_slot)

    def ordered(values, picks, filled):
        got = jnp.where(filled[:, None, None], jnp.take(values, picks, axis=0), 0).astype(values.dtype)
        return got.reshape(nd, cap, *values.shape[1:])

    def facts(ids):
        job, valid = block_facts(tokens_per_job, ids, halved * ns)
        row = s * halved + jnp.arange(halved, dtype=i32)
        mask = row[None, :] < valid[:, None]
        rel = (z - job // jobs_dev) % nd * jobs_dev + job % jobs_dev
        hot = rel[:, None] == jnp.arange(nd * jobs_dev, dtype=i32)[None, :]
        return mask, hot

    out_mask, out_hot = facts(z * blocks + positions)
    in_mask, in_hot = facts(block_ids)

    def pick(wide, hot):
        wide = wide.reshape(blocks, halved, ns, nd * jobs_dev, r2)
        return jnp.sum(jnp.where(hot[:, None, None, :, None], wide, 0.0), axis=3).reshape(blocks, halved, rank)

    def spread(narrow, hot):
        narrow = narrow.reshape(blocks, halved, ns, 1, r2)
        wide = jnp.where(hot[:, None, None, :, None], narrow, 0).astype(bf16)
        return wide.reshape(rows, ns * nd * jobs_dev * r2)

    own_tokens = tokens[0].reshape(rows, width)
    own_grad = jnp.where(in_mask[:, :, None], cotangent[0], 0).astype(bf16).reshape(rows, heads)
    down_part = pick(dot(own_tokens, down_cat, ((1,), (1,))), out_hot).astype(bf16)
    back_part = pick(dot(own_grad, up_cat, ((1,), (1,))), in_hot).astype(bf16)
    parts = gather_shifts(jnp.concatenate([down_part, back_part], axis=2), "tensor", nt)
    sums = sum(x.astype(f32) for x in parts).astype(bf16)
    down_sum, back_sum = sums[:, :, :rank], sums[:, :, rank:]
    down_wide, back_wide = spread(down_sum, out_hot), spread(back_sum, in_hot)

    down_out = ordered(down_sum, out_pos, out_filled)
    back_out = ordered(back_sum, in_pos, in_filled)
    down_got, back_got = [None] * nd, [None] * nd
    for d in range(nd):
        pair = shifted(jnp.concatenate([down_out[d], back_out[(nd - d) % nd]], axis=2), "dp", nd, d)
        down_got[d], back_got[(nd - d) % nd] = pair[:, :, :rank], pair[:, :, rank:]
    down_at_grad = jnp.take(jnp.concatenate(down_got, axis=0), in_slot, axis=0)
    back_at_tokens = jnp.take(jnp.concatenate(back_got, axis=0), out_slot, axis=0)
    mine, theirs = tables_of(
        spread(back_at_tokens, out_hot).T, spread(down_at_grad, in_hot).T, own_tokens, own_grad
    )

    summed = (mine + shifted(theirs, "sub", ns, 1)).reshape(nd, jobs_dev * r2, -1)
    total = summed[0].astype(bf16).astype(f32)
    for d in range(1, nd):
        total = total + shifted(summed[d].astype(bf16), "dp", nd, -d).astype(f32)
    counts = lax.dynamic_slice_in_dim(tokens_per_job, z * jobs_dev, jobs_dev).astype(f32)
    total = total.reshape(jobs_dev, r2, -1) * (adapter_scale / counts)[:, None, None]
    halves = jnp.stack(gather_shifts(total, "sub", ns), axis=1)
    order = (s - jnp.arange(ns, dtype=i32)) % ns
    owned = jnp.take(halves, order, axis=1).reshape(jobs_dev, rank, -1)
    grad_down, grad_up = owned[:, :, :width], owned[:, :, width:]

    base = [
        base_product(own_tokens, piece_list[d], quarters, d == 0, "base_%d" % d) for d in range(nd)
    ]
    base = jnp.stack(base)
    per_head = nd // nt

    def of_heads(index):
        shard = index * per_head + jnp.arange(per_head, dtype=i32)
        return jnp.take(base, (z - shard) % nd, axis=0)

    frozen = of_heads(t).astype(f32)
    for d in range(1, nt):
        frozen = frozen + shifted(of_heads((t + d) % nt), "tensor", nt, d).astype(f32)
    adapter_out = dot(down_wide, up_cat, ((1,), (0,)))
    layer = frozen.transpose(1, 0, 2).reshape(rows, heads) + adapter_scale * adapter_out
    layer = jnp.where(out_mask[:, :, None], layer.reshape(blocks, halved, heads), 0.0).astype(bf16)
    layer = ordered(layer, out_pos, out_filled)
    layer = jnp.concatenate([shifted(layer[d], "dp", nd, d) for d in range(nd)], axis=0)
    layer_output = jnp.take(layer, in_slot, axis=0)

    grad_abs = jnp.take(jnp.stack(grad_rel), (t - jnp.arange(nt, dtype=i32)) % nt, axis=0)
    grad_abs = jnp.where(in_mask[None, :, :, None], grad_abs, 0).astype(bf16)
    grad_abs = grad_abs.reshape(nt, rows, per_head, columns).transpose(0, 2, 1, 3)
    grad_shift = jnp.take(
        grad_abs.reshape(nd, rows, columns), (z - jnp.arange(nd, dtype=i32)) % nd, axis=0
    )
    token_gradient = token_gradient_of(grad_shift, back_wide, down_cat, piece_list, quarters, width)
    return (
        layer_output[None],
        token_gradient.reshape(1, blocks, halved, width),
        grad_down,
        grad_up,
    )


def solution(mesh):
    return jax.shard_map(
        body,
        mesh=mesh,
        in_specs=(
            P(("parts", "dp"), None, "sub", "tensor"),
            P(("parts", "dp"), None, "sub", "tensor"),
            P("tensor", "dp"),
            P(("parts", "dp"), None, "tensor"),
            P(("parts", "dp"), None, "tensor"),
            P("parts"),
            P("parts", None),
        ),
        out_specs=(
            P(("parts", "dp"), None, "sub", "tensor"),
            P(("parts", "dp"), None, "sub", "tensor"),
            P(("parts", "dp"), None, "tensor"),
            P(("parts", "dp"), None, "tensor"),
        ),
        check_vma=False,
    )
```

```python
import functools

import jax
import jax.numpy as jnp
from jax import lax
from jax.experimental import pallas as pl
from jax.experimental.pallas import tpu as pltpu
from jax.sharding import PartitionSpec as P

adapter_scale = 2.0
f32, bf16, i32 = jnp.float32, jnp.bfloat16, jnp.int32
MIB = 1 << 20


def block_facts(tokens_per_job, block_ids, block_rows):
    job_total = tokens_per_job.shape[0]
    blocks = (tokens_per_job + (block_rows - 1)) // block_rows
    block_ends = jnp.cumsum(blocks, dtype=jnp.int32)
    starts = block_ends - blocks
    job_index = jnp.sum(
        (block_ends[None, :] <= block_ids[:, None]).astype(jnp.int32), axis=1, dtype=jnp.int32
    )
    chosen = job_index[:, None] == jnp.arange(job_total, dtype=jnp.int32)[None, :]
    job_count = jnp.sum(jnp.where(chosen, tokens_per_job[None, :], 0), axis=1, dtype=jnp.int32)
    first_block = jnp.sum(jnp.where(chosen, starts[None, :], 0), axis=1, dtype=jnp.int32)
    valid_rows = jnp.clip(job_count - block_rows * (block_ids - first_block), 0, block_rows)
    return job_index, valid_rows


def shifted(values, axis, count, step):
    if step % count == 0:
        return values
    return lax.ppermute(values, axis, [(i, (i + step) % count) for i in range(count)])


def gather_shifts(values, axis, count):
    return [shifted(values, axis, count, d) for d in range(count)]


def dot(a, b, dims, precision=None):
    return lax.dot_general(a, b, (dims, ((), ())), precision=precision, preferred_element_type=f32)


def tie(*values):
    return lax.optimization_barrier(values)


class Sizes:
    def __init__(self, nd, nt, ns, np_, blocks, halved, width, heads, jobs_dev, rank, columns):
        self.nd, self.nt, self.ns, self.np_ = nd, nt, ns, np_
        self.blocks, self.halved, self.width, self.heads = blocks, halved, width, heads
        self.jobs, self.jobs_dev, self.rank, self.columns = nd * jobs_dev, jobs_dev, rank, columns
        self.wide = self.jobs * rank
        self.rows = blocks * halved
        self.cap = -(-blocks // nd)
        self.slots = nd * self.cap
        self.nq = np_ * ns
        self.fq = width // self.nq
        self.per_head = nd // nt
        at, self.at = 0, {}
        for name, count in (
            ("out_pos", self.slots), ("in_pos", self.slots), ("out_fill", self.slots), ("in_fill", self.slots),
            ("out_rel", blocks), ("in_rel", blocks), ("out_valid", blocks), ("in_valid", blocks),
            ("quarter", self.nq), ("shard", nd), ("head", self.per_head),
        ):
            self.at[name] = at
            at += count

    def get(self, ref, name, index):
        return ref[self.at[name] + index]


def call(kernel, name, grid, scalars, inputs, in_specs, out_shape, out_specs, flops, moved, limit, scratch=(), alias=None):
    return pl.pallas_call(
        kernel,
        out_shape=out_shape,
        grid_spec=pltpu.PrefetchScalarGridSpec(
            num_scalar_prefetch=1, grid=grid, in_specs=in_specs, out_specs=out_specs, scratch_shapes=list(scratch)
        ),
        input_output_aliases=alias or {},
        compiler_params=pltpu.CompilerParams(vmem_limit_bytes=limit),
        cost_estimate=pl.CostEstimate(flops=flops, bytes_accessed=moved, transcendentals=0),
        name=name,
    )(scalars, *inputs)


def whole(x):
    return pl.BlockSpec(x.shape, lambda *_: (0,) * len(x.shape))


def rows_of(index, z):
    return pl.ds(pl.multiple_of(index * z.halved, z.halved), z.halved)


def row_mask(valid, z, lanes):
    return lax.broadcasted_iota(i32, (z.halved, lanes), 0) < valid


def widen(values, rel, unfold, job_of, z):
    wide = dot(values, unfold, ((1,), (0,)))
    return jnp.where(job_of == rel, wide, 0.0).astype(bf16)


def products_kernel(z, n, sc, tokens, grad, maps, fold, job_of, out):
    step = pl.program_id(0)
    down = dot(tokens[...], maps[:, : z.width], ((1,), (1,)))
    back = dot(grad[...], maps[:, z.width :], ((1,), (1,)))
    for k in range(n):
        block = step * n + k
        own = slice(k * z.halved, (k + 1) * z.halved)
        picked = jnp.where(job_of[...] == z.get(sc, "out_rel", block), down[own], 0.0)
        out[own, : z.rank] = dot(picked, fold[...], ((1,), (0,)), lax.Precision.HIGHEST).astype(bf16)
        picked = jnp.where(job_of[...] == z.get(sc, "in_rel", block), back[own], 0.0)
        picked = jnp.where(row_mask(z.get(sc, "in_valid", block), z, z.wide), picked, 0.0)
        out[own, z.rank :] = dot(picked, fold[...], ((1,), (0,)), lax.Precision.HIGHEST).astype(bf16)


def products(z, sc, tokens, grad, maps, fold, job_of):
    n = 2
    return call(
        functools.partial(products_kernel, z, n), "adapter_products", (z.blocks // n,), sc,
        (tokens, grad, maps, fold, job_of),
        [
            pl.BlockSpec((n * z.halved, z.width), lambda i, _: (i, 0)),
            pl.BlockSpec((n * z.halved, z.heads), lambda i, _: (i, 0)),
            whole(maps), whole(fold), whole(job_of),
        ],
        jax.ShapeDtypeStruct((z.rows, 2 * z.rank), bf16),
        pl.BlockSpec((n * z.halved, 2 * z.rank), lambda i, _: (i, 0)),
        2 * z.rows * (z.width + z.heads) * z.wide, 2 * z.rows * (z.width + z.heads), 16 * MIB,
    )


def sums_kernel(z, sc, *refs):
    parts, outs = refs[: z.nt], refs[z.nt :]
    sums, pays = outs[0], outs[1:]
    total = parts[0][...].astype(f32)
    for part in parts[1:]:
        total = total + part[...].astype(f32)
    sums[...] = total.astype(bf16)
    for d in range(z.nd):
        back = (z.nd - d) % z.nd
        for r in range(z.cap):
            own = slice(r * z.halved, (r + 1) * z.halved)
            picked = sums[rows_of(z.get(sc, "out_pos", d * z.cap + r), z), : z.rank]
            pays[d][own, : z.rank] = jnp.where(z.get(sc, "out_fill", d * z.cap + r) > 0, picked, 0)
            picked = sums[rows_of(z.get(sc, "in_pos", back * z.cap + r), z), z.rank :]
            pays[d][own, z.rank :] = jnp.where(z.get(sc, "in_fill", back * z.cap + r) > 0, picked, 0)


def sums_of(z, sc, parts):
    shapes = [jax.ShapeDtypeStruct((z.rows, 2 * z.rank), bf16)]
    shapes += [jax.ShapeDtypeStruct((z.cap * z.halved, 2 * z.rank), bf16)] * z.nd
    return call(
        functools.partial(sums_kernel, z), "adapter_sums", (1,), sc, parts, [whole(x) for x in parts],
        tuple(shapes), tuple(whole(x) for x in shapes), 1000, 8 * z.rows * z.rank, 8 * MIB,
    )


def table_kernel(z, tiles, sc, tokens, grad, unfold, job_of, *refs):
    got, (mine, theirs, back, down) = refs[: z.nd], refs[z.nd :]
    half = mine.shape[0]
    step = pl.program_id(0)

    @pl.when(step == 0)
    def _():
        for d in range(z.nd):
            for r in range(z.cap):
                slot = d * z.cap + r
                own = slice(r * z.halved, (r + 1) * z.halved)

                @pl.when(z.get(sc, "out_fill", slot) > 0)
                def _():
                    at = z.get(sc, "out_pos", slot)
                    values = got[(z.nd - d) % z.nd][own, z.rank :]
                    back[rows_of(at, z), :] = widen(values, z.get(sc, "out_rel", at), unfold[...], job_of[...], z)

                @pl.when(z.get(sc, "in_fill", slot) > 0)
                def _():
                    at = z.get(sc, "in_pos", slot)
                    values = widen(got[d][own, : z.rank], z.get(sc, "in_rel", at), unfold[...], job_of[...], z)
                    mask = row_mask(z.get(sc, "in_valid", at), z, z.wide)
                    down[rows_of(at, z), :] = jnp.where(mask, values, 0).astype(bf16)

    def put(wide, values):
        total = dot(wide[...], values[...], ((0,), (0,)))
        mine[...] = total[:half]
        theirs[...] = total[half:]

    @pl.when(step < tiles)
    def _():
        put(back, tokens)

    @pl.when(step == tiles)
    def _():
        put(down, grad)


def tables_of(z, sc, tokens, grad, unfold, job_of, got):
    tiles = z.width // z.heads
    half = z.wide // z.ns
    shape = jax.ShapeDtypeStruct((half, z.width + z.heads), f32)
    out = pl.BlockSpec((half, z.heads), lambda i, _: (0, i))
    return call(
        functools.partial(table_kernel, z, tiles), "job_tables", (tiles + 1,), sc,
        (tokens, grad, unfold, job_of, *got),
        [
            pl.BlockSpec((z.rows, z.heads), lambda i, _: (0, jnp.minimum(i, tiles - 1))),
            whole(grad), whole(unfold), whole(job_of),
        ]
        + [whole(x) for x in got],
        (shape, shape), (out, out),
        2 * z.wide * z.rows * (z.width + z.heads), 2 * z.rows * z.width + 4 * z.wide * z.width, 16 * MIB,
        scratch=(pltpu.VMEM((z.rows, z.wide), bf16), pltpu.VMEM((z.rows, z.wide), bf16)),
    )


def base_kernel(z, sc, tokens, *refs):
    pieces, (out, total) = refs[: z.nq], refs[z.nq :]
    step = pl.program_id(0)
    for r in range(z.nq):

        @pl.when(step == r)
        def _():
            part = dot(tokens[...], pieces[r][...], ((1,), (0,)))
            if r == 0:
                total[...] = part
            elif r < z.nq - 1:
                total[...] += part
            else:
                out[...] = (total[...] + part).astype(bf16)


def base_product(z, sc, tokens, pieces, d):
    at = z.at["quarter"]
    if d == 0:
        specs = [pl.BlockSpec((z.fq, z.columns), lambda i, q, r=r: (q[at + r], 0)) for r in range(z.nq)]
    else:
        specs = [whole(x) for x in pieces]
    return call(
        functools.partial(base_kernel, z), "base_%d" % d, (z.nq,), sc, (tokens, *pieces),
        [pl.BlockSpec((z.rows, z.fq), lambda i, q: (0, q[at + i]))] + specs,
        jax.ShapeDtypeStruct((z.rows, z.columns), bf16),
        pl.BlockSpec((z.rows, z.columns), lambda i, q: (0, 0)),
        2 * z.rows * z.width * z.columns, 2 * (z.rows * z.width + z.width * z.columns), 16 * MIB,
        scratch=(pltpu.VMEM((z.rows, z.columns), f32),),
    )


def layer_kernel(z, sc, sums, maps, unfold, job_of, *refs):
    m = z.per_head
    given, (outs, frozen) = refs[: m * z.nt], (refs[m * z.nt : -1], refs[-1])
    for j in range(m):
        total = given[j][...].astype(f32)
        for d in range(1, z.nt):
            total = total + given[d * m + j][...].astype(f32)
        for i in range(m):

            @pl.when(z.get(sc, "head", j) == i)
            def _():
                frozen[:, i * z.columns : (i + 1) * z.columns] = total

    for d in range(z.nd):
        for r in range(z.cap):
            slot = d * z.cap + r
            at = z.get(sc, "out_pos", slot)
            valid = jnp.where(z.get(sc, "out_fill", slot) > 0, z.get(sc, "out_valid", at), 0)
            wide = widen(sums[rows_of(at, z), : z.rank], z.get(sc, "out_rel", at), unfold[...], job_of[...], z)
            adapter = dot(wide, maps[...], ((1,), (0,)))
            layer = frozen[rows_of(at, z), :] + adapter_scale * adapter
            layer = jnp.where(row_mask(valid, z, z.heads), layer, 0.0)
            outs[d][r * z.halved : (r + 1) * z.halved, :] = layer.astype(bf16)


def layer_of(z, sc, sums, maps, unfold, job_of, given):
    shapes = [jax.ShapeDtypeStruct((z.cap * z.halved, z.heads), bf16)] * z.nd
    at = z.width // z.heads
    return call(
        functools.partial(layer_kernel, z), "layer", (1,), sc, (sums, maps, unfold, job_of, *given),
        [whole(sums), pl.BlockSpec((z.wide, z.heads), lambda i, _: (0, at)), whole(unfold), whole(job_of)]
        + [whole(x) for x in given],
        tuple(shapes), tuple(whole(x) for x in shapes),
        2 * z.rows * z.wide * z.heads, 6 * z.rows * z.heads, 16 * MIB,
        scratch=(pltpu.VMEM((z.rows, z.heads), f32),),
    )


def place_kernel(z, sc, *refs):
    got, out = refs[: z.nd], refs[z.nd]
    for d in range(z.nd):
        for r in range(z.cap):
            slot = d * z.cap + r

            @pl.when(z.get(sc, "in_fill", slot) > 0)
            def _():
                out[rows_of(z.get(sc, "in_pos", slot), z), :] = got[d][r * z.halved : (r + 1) * z.halved, :]


def place(z, sc, got):
    shape = jax.ShapeDtypeStruct((z.rows, z.heads), bf16)
    return call(
        functools.partial(place_kernel, z), "place", (1,), sc, got, [whole(x) for x in got],
        shape, whole(shape), 1000, 4 * z.rows * z.heads, 8 * MIB,
    )


def gradient_kernel(z, quarters, per, aliased, sc, maps, sums, unfold, job_of, *refs):
    grads, refs = refs[: z.nt], refs[z.nt :]
    count = len(quarters)
    pieces, refs = refs[: z.nd * count], refs[z.nd * count :]
    out, grad, back = refs[1:] if aliased else refs
    step = pl.program_id(0)
    m = z.per_head

    @pl.when(step == 0)
    def _():
        for v in range(z.nt * m):
            grad[v] = grads[v // m][:, v % m * z.columns : (v % m + 1) * z.columns]
        for b in range(z.blocks):
            own = slice(b * z.halved, (b + 1) * z.halved)
            back[own, :] = widen(sums[own, z.rank :], z.get(sc, "in_rel", b), unfold[...], job_of[...], z)

    for k in range(count):

        @pl.when(step // per == k)
        def _():
            total = adapter_scale * dot(back[...], maps[...], ((1,), (0,)))
            for d in range(z.nd):
                total = total + dot(grad[z.get(sc, "shard", d)], pieces[d * count + k][...], ((1,), (1,)))
            for b in range(z.blocks):
                own = slice(b * z.halved, (b + 1) * z.halved)
                mask = row_mask(z.get(sc, "in_valid", b), z, total.shape[1])
                out[own, :] = jnp.where(mask, total[own], 0.0).astype(bf16)


def token_gradient_of(z, sc, grads, maps, sums, unfold, job_of, piece_list, quarters, before):
    tile = min(512, z.fq)
    per = z.fq // tile
    at = z.at["quarter"]
    first = quarters[0]
    block = lambda i, q: (0, q[at + first + i // per] * per + i % per)
    specs, flat = [], []
    for d in range(z.nd):
        for k, r in enumerate(quarters):
            inner = lambda i, k=k: jnp.clip(i - k * per, 0, per - 1)
            if d == 0:
                index = lambda i, q, r=r, inner=inner: (q[at + r] * per + inner(i), 0)
            else:
                index = lambda i, q, inner=inner: (inner(i), 0)
            specs.append(pl.BlockSpec((tile, z.columns), index))
            flat.append(piece_list[d][r])
    inputs = [maps, sums, unfold, job_of, *grads, *flat]
    in_specs = [pl.BlockSpec((z.wide, tile), block), whole(sums), whole(unfold), whole(job_of)]
    in_specs += [whole(x) for x in grads] + specs
    alias = None
    if before is not None:
        alias = {1 + len(inputs): 0}
        inputs.append(before)
        in_specs.append(pl.BlockSpec(memory_space=pl.ANY))
    share = len(quarters) * z.fq
    return call(
        functools.partial(gradient_kernel, z, quarters, per, before is not None),
        "token_gradient_%d" % first, (len(quarters) * per,), sc, inputs, in_specs,
        jax.ShapeDtypeStruct((z.rows, z.width), bf16), pl.BlockSpec((z.rows, tile), block),
        2 * z.rows * share * (z.nd * z.columns + z.wide), 2 * share * (z.rows + z.nd * z.columns), 32 * MIB,
        scratch=(pltpu.VMEM((z.nd, z.rows, z.columns), bf16), pltpu.VMEM((z.rows, z.wide), bf16)),
        alias=alias,
    )


def body(
    tokens,
    cotangent,
    frozen_value_weight,
    adapter_down,
    adapter_up,
    tokens_per_job,
    packed_block_slots,
):
    nd, nt, ns, np_ = (lax.axis_size(a) for a in ("dp", "tensor", "sub", "parts"))
    z, t, s, p = (lax.axis_index(a) for a in ("dp", "tensor", "sub", "parts"))
    blocks, halved, width = tokens.shape[1:]
    heads = cotangent.shape[3]
    jobs_dev, rank, _ = adapter_down.shape
    columns = frozen_value_weight.shape[1]
    zz = Sizes(nd, nt, ns, np_, blocks, halved, width, heads, jobs_dev, rank, columns)
    rows, r2, m, cap = zz.rows, rank // ns, zz.per_head, zz.cap
    own_tokens = tokens.reshape(rows, width)
    own_grad = cotangent.reshape(rows, heads)

    quarters = jnp.stack([(p - a) % np_ * ns + (s - b) % ns for a in range(np_) for b in range(ns)]).astype(i32)
    moving = lax.dynamic_slice_in_dim(frozen_value_weight, (p * ns + s) * zz.fq, zz.fq, axis=0)
    rounds = [None, shifted(moving, "dp", nd, 1)]

    maps = jnp.concatenate([adapter_down, adapter_up], axis=2).reshape(jobs_dev, ns, r2, width + heads)
    maps = lax.dynamic_index_in_dim(maps, s, 1, keepdims=False)
    maps = jnp.concatenate(gather_shifts(maps, "dp", nd), axis=0).reshape(zz.jobs * r2, -1)
    maps = jnp.concatenate(gather_shifts(maps, "sub", ns), axis=0)
    grads = gather_shifts(own_grad, "tensor", nt)

    positions = jnp.arange(blocks, dtype=i32)
    dest = packed_block_slots // blocks
    same = dest[:, :, None] == dest[:, None, :]
    earlier = positions[None, None, :] < positions[None, :, None]
    send_rank = jnp.sum((same & earlier).astype(i32), axis=2, dtype=i32)
    flat_slots = packed_block_slots.reshape(-1)
    flat_ids = jnp.arange(nd * blocks, dtype=i32)
    slot_owner = flat_slots[None, :] == (z * blocks + positions)[:, None]
    block_ids = jnp.sum(jnp.where(slot_owner, flat_ids[None, :], 0), axis=1, dtype=i32)
    in_rank = jnp.sum(jnp.where(slot_owner, send_rank.reshape(-1)[None, :], 0), axis=1, dtype=i32)
    in_slot = (z - block_ids // blocks) % nd * cap + in_rank
    own_dest = lax.dynamic_index_in_dim(dest, z, 0, keepdims=False)
    own_rank = lax.dynamic_index_in_dim(send_rank, z, 0, keepdims=False)
    out_slot = (own_dest - z) % nd * cap + own_rank
    slot_range = jnp.arange(zz.slots, dtype=i32)

    def positions_of(slots):
        match = slots[None, :] == slot_range[:, None]
        return jnp.sum(jnp.where(match, positions[None, :], 0), axis=1, dtype=i32), jnp.any(match, axis=1)

    out_pos, out_fill = positions_of(out_slot)
    in_pos, in_fill = positions_of(in_slot)

    def facts(ids):
        job, valid = block_facts(tokens_per_job, ids, halved * ns)
        return (z - job // jobs_dev) % nd * jobs_dev + job % jobs_dev, valid - s * halved

    out_rel, out_valid = facts(z * blocks + positions)
    in_rel, in_valid = facts(block_ids)

    def arrival(index):
        found = (z - index * m - jnp.arange(m, dtype=i32)) % nd
        place_of = jnp.sum((found[None, :] < found[:, None]).astype(i32), axis=1)
        match = place_of[None, :] == jnp.arange(m, dtype=i32)[:, None]
        return jnp.sum(jnp.where(match, found[None, :], 0), axis=1, dtype=i32)

    shard_of = (z - jnp.arange(nd, dtype=i32)) % nd
    shard_at = (t - shard_of // m) % nt * m + shard_of % m
    head_at = (z - arrival(t)) % nd - t * m
    sc = jnp.concatenate(
        [
            x.astype(i32)
            for x in (out_pos, in_pos, out_fill, in_fill, out_rel, in_rel, out_valid, in_valid, quarters, shard_at, head_at)
        ]
    )
    column = jnp.arange(zz.wide, dtype=i32)
    job_of = (column // r2 % zz.jobs)[None, :]
    rank_of = column // (zz.jobs * r2) * r2 + column % r2
    unfold = (jnp.arange(rank, dtype=i32)[:, None] == rank_of[None, :]).astype(bf16)
    fold = unfold.astype(f32).T

    def spread_round(d, over_parts):
        pieces = []
        for y in over_parts:
            pieces += gather_shifts(y, "sub", ns)
        return pieces

    maps, rounds[1], sc = tie(maps, rounds[1], sc)
    over = [None] * nd
    over[1] = gather_shifts(rounds[1], "parts", np_)
    if nd > 2:
        rounds.append(shifted(rounds[1], "dp", nd, 1))
    part = products(zz, sc, own_tokens, own_grad, maps, fold, job_of)
    parts = gather_shifts(part, "tensor", nt)
    late_tokens, _ = tie(own_tokens, part)
    base = [base_product(zz, sc, late_tokens, [frozen_value_weight] * zz.nq, 0)]
    tied = tie(base[0], *parts)
    base[0], parts = tied[0], tied[1:]
    sums, *pays = sums_of(zz, sc, parts)
    got = [shifted(pays[d], "dp", nd, d) for d in range(nd)]

    if nd > 2:
        tied = tie(rounds[2], *over[1], *got)
        rounds[2], over[1], got = tied[0], list(tied[1 : 1 + np_]), tied[1 + np_ :]
    piece_list = [[frozen_value_weight] * zz.nq, spread_round(1, over[1])]
    for d in range(2, nd):
        over[d] = gather_shifts(rounds[d], "parts", np_)
        if d + 1 < nd:
            rounds.append(shifted(rounds[d], "dp", nd, 1))
        piece_list.append(spread_round(d, over[d]))
    mine, theirs = tables_of(zz, sc, own_tokens, own_grad, unfold, job_of, got)
    theirs = shifted(theirs, "sub", ns, 1)
    late_tokens, mine = tie(own_tokens, mine)
    base.append(base_product(zz, sc, late_tokens, piece_list[1], 1))
    mine, base[1], theirs = tie(mine, base[1], theirs)

    summed = (mine + theirs).reshape(nd, jobs_dev * r2, -1)
    sending = [summed[d].astype(bf16) for d in range(nd)]
    if nd > 3:
        rounds[3], *sending = tie(rounds[3], *sending)
        over[3] = gather_shifts(rounds[3], "parts", np_)
        piece_list[3] = spread_round(3, over[3])
    total = sending[0].astype(f32)
    for d in range(1, nd):
        total = total + shifted(sending[d], "dp", nd, -d).astype(f32)
    counts = lax.dynamic_slice_in_dim(tokens_per_job, z * jobs_dev, jobs_dev).astype(f32)
    total = total.reshape(jobs_dev, r2, -1) * (adapter_scale / counts)[:, None, None]
    halves = gather_shifts(total, "sub", ns)
    owned = jnp.concatenate(
        [sum(jnp.where((s - h) % ns == k, x, 0.0) for k, x in enumerate(halves)) for h in range(ns)], axis=1
    )
    grad_down, grad_up = owned[:, :, :width], owned[:, :, width:]

    for d in range(2, nd):
        base.append(base_product(zz, sc, own_tokens, piece_list[d], d))

    def arriving(index, j):
        d = arrival(index)[j]
        picked = base[j]
        for k in range(j + 1, nd - m + j + 1):
            picked = jnp.where(d == k, base[k], picked)
        return picked

    given = [arriving(t, j) for j in range(m)]
    for d in range(1, nt):
        given += [shifted(arriving((t + d) % nt, j), "tensor", nt, d) for j in range(m)]
    half = zz.nq // 2
    grads = [grads[0]] + list(tie(base[-1], *grads[1:])[1:])
    gradient = token_gradient_of(zz, sc, grads, maps, sums, unfold, job_of, piece_list, list(range(half)), None)
    gradient, *given = tie(gradient, *given)
    layer = layer_of(zz, sc, sums, maps, unfold, job_of, given)
    layer, gradient = tie(layer, gradient)
    landed = [shifted(layer[d], "dp", nd, d) for d in range(nd)]
    gradient = token_gradient_of(
        zz, sc, grads, maps, sums, unfold, job_of, piece_list, list(range(half, zz.nq)), gradient
    )
    gradient, *landed = tie(gradient, *landed)
    layer_output = place(zz, sc, landed)
    return (
        layer_output.reshape(1, blocks, halved, heads),
        gradient.reshape(1, blocks, halved, width),
        grad_down,
        grad_up,
    )


def solution(mesh):
    return jax.shard_map(
        body,
        mesh=mesh,
        in_specs=(
            P(("parts", "dp"), None, "sub", "tensor"),
            P(("parts", "dp"), None, "sub", "tensor"),
            P("tensor", "dp"),
            P(("parts", "dp"), None, "tensor"),
            P(("parts", "dp"), None, "tensor"),
            P("parts"),
            P("parts", None),
        ),
        out_specs=(
            P(("parts", "dp"), None, "sub", "tensor"),
            P(("parts", "dp"), None, "sub", "tensor"),
            P(("parts", "dp"), None, "tensor"),
            P(("parts", "dp"), None, "tensor"),
        ),
        check_vma=False,
    )
```

```python
import functools

import jax
import jax.numpy as jnp
from jax import lax
from jax.experimental import pallas as pl
from jax.experimental.pallas import tpu as pltpu
from jax.sharding import PartitionSpec as P

adapter_scale = 2.0
f32, bf16, i32 = jnp.float32, jnp.bfloat16, jnp.int32
MIB = 1 << 20
TOKEN_LIMIT = 50 * MIB


def block_facts(tokens_per_job, block_ids, block_rows):
    job_total = tokens_per_job.shape[0]
    blocks = (tokens_per_job + (block_rows - 1)) // block_rows
    block_ends = jnp.cumsum(blocks, dtype=jnp.int32)
    starts = block_ends - blocks
    job_index = jnp.sum(
        (block_ends[None, :] <= block_ids[:, None]).astype(jnp.int32), axis=1, dtype=jnp.int32
    )
    chosen = job_index[:, None] == jnp.arange(job_total, dtype=jnp.int32)[None, :]
    job_count = jnp.sum(jnp.where(chosen, tokens_per_job[None, :], 0), axis=1, dtype=jnp.int32)
    first_block = jnp.sum(jnp.where(chosen, starts[None, :], 0), axis=1, dtype=jnp.int32)
    valid_rows = jnp.clip(job_count - block_rows * (block_ids - first_block), 0, block_rows)
    return job_index, valid_rows


def shifted(values, axis, count, step):
    if step % count == 0:
        return values
    return lax.ppermute(values, axis, [(i, (i + step) % count) for i in range(count)])


def gather_shifts(values, axis, count):
    return [shifted(values, axis, count, d) for d in range(count)]


def dot(a, b, dims, precision=None):
    return lax.dot_general(a, b, (dims, ((), ())), precision=precision, preferred_element_type=f32)


def tie(*values):
    return lax.optimization_barrier(values)


class Sizes:
    def __init__(self, nd, nt, ns, np_, blocks, halved, width, heads, jobs_dev, rank, columns):
        self.nd, self.nt, self.ns, self.np_ = nd, nt, ns, np_
        self.blocks, self.halved, self.width, self.heads = blocks, halved, width, heads
        self.jobs, self.jobs_dev, self.rank, self.columns = nd * jobs_dev, jobs_dev, rank, columns
        self.wide = self.jobs * rank
        self.rows = blocks * halved
        self.cap = -(-blocks // nd)
        self.slots = nd * self.cap
        self.nq = np_ * ns
        self.fq = width // self.nq
        self.per_head = nd // nt
        at, self.at = 0, {}
        for name, count in (
            ("out_pos", self.slots), ("in_pos", self.slots), ("out_fill", self.slots), ("in_fill", self.slots),
            ("out_rel", blocks), ("in_rel", blocks), ("out_valid", blocks), ("in_valid", blocks),
            ("quarter", self.nq), ("shard", nd), ("head", self.per_head),
        ):
            self.at[name] = at
            at += count

    def get(self, ref, name, index):
        return ref[self.at[name] + index]


def call(kernel, name, grid, scalars, inputs, in_specs, out_shape, out_specs, flops, moved, limit, scratch=(), alias=None):
    return pl.pallas_call(
        kernel,
        out_shape=out_shape,
        grid_spec=pltpu.PrefetchScalarGridSpec(
            num_scalar_prefetch=1, grid=grid, in_specs=in_specs, out_specs=out_specs, scratch_shapes=list(scratch)
        ),
        input_output_aliases=alias or {},
        compiler_params=pltpu.CompilerParams(vmem_limit_bytes=limit),
        cost_estimate=pl.CostEstimate(flops=1000, bytes_accessed=1000, transcendentals=0),
        name=name,
    )(scalars, *inputs)


def whole(x):
    return pl.BlockSpec(x.shape, lambda *_: (0,) * len(x.shape))


def rows_of(index, z):
    return pl.ds(pl.multiple_of(index * z.halved, z.halved), z.halved)


def row_mask(valid, z, lanes):
    return lax.broadcasted_iota(i32, (z.halved, lanes), 0) < valid


def widen(values, rel, unfold, job_of, z):
    wide = dot(values, unfold, ((1,), (0,)))
    return jnp.where(job_of == rel, wide, 0.0).astype(bf16)


def products_kernel(z, n, sc, tokens, grad, maps, fold, job_of, out):
    step = pl.program_id(0)
    down = dot(tokens[...], maps[:, : z.width], ((1,), (1,)))
    back = dot(grad[...], maps[:, z.width :], ((1,), (1,)))
    for k in range(n):
        block = step * n + k
        own = slice(k * z.halved, (k + 1) * z.halved)
        picked = jnp.where(job_of[...] == z.get(sc, "out_rel", block), down[own], 0.0)
        out[own, : z.rank] = dot(picked, fold[...], ((1,), (0,)), lax.Precision.HIGHEST).astype(bf16)
        picked = jnp.where(job_of[...] == z.get(sc, "in_rel", block), back[own], 0.0)
        picked = jnp.where(row_mask(z.get(sc, "in_valid", block), z, z.wide), picked, 0.0)
        out[own, z.rank :] = dot(picked, fold[...], ((1,), (0,)), lax.Precision.HIGHEST).astype(bf16)


def products(z, sc, tokens, grad, maps, fold, job_of):
    n = 2
    return call(
        functools.partial(products_kernel, z, n), "adapter_products", (z.blocks // n,), sc,
        (tokens, grad, maps, fold, job_of),
        [
            pl.BlockSpec((n * z.halved, z.width), lambda i, _: (i, 0)),
            pl.BlockSpec((n * z.halved, z.heads), lambda i, _: (i, 0)),
            whole(maps), whole(fold), whole(job_of),
        ],
        jax.ShapeDtypeStruct((z.rows, 2 * z.rank), bf16),
        pl.BlockSpec((n * z.halved, 2 * z.rank), lambda i, _: (i, 0)),
        2 * z.rows * (z.width + z.heads) * z.wide, 2 * z.rows * (z.width + z.heads), TOKEN_LIMIT,
    )


def sums_kernel(z, sc, *refs):
    parts, outs = refs[: z.nt], refs[z.nt :]
    sums, pays = outs[0], outs[1:]
    total = parts[0][...].astype(f32)
    for part in parts[1:]:
        total = total + part[...].astype(f32)
    sums[...] = total.astype(bf16)
    for d in range(z.nd):
        back = (z.nd - d) % z.nd
        for r in range(z.cap):
            own = slice(r * z.halved, (r + 1) * z.halved)
            picked = sums[rows_of(z.get(sc, "out_pos", d * z.cap + r), z), : z.rank]
            pays[d][own, : z.rank] = jnp.where(z.get(sc, "out_fill", d * z.cap + r) > 0, picked, 0)
            picked = sums[rows_of(z.get(sc, "in_pos", back * z.cap + r), z), z.rank :]
            pays[d][own, z.rank :] = jnp.where(z.get(sc, "in_fill", back * z.cap + r) > 0, picked, 0)


def sums_of(z, sc, parts):
    shapes = [jax.ShapeDtypeStruct((z.rows, 2 * z.rank), bf16)]
    shapes += [jax.ShapeDtypeStruct((z.cap * z.halved, 2 * z.rank), bf16)] * z.nd
    return call(
        functools.partial(sums_kernel, z), "adapter_sums", (1,), sc, parts, [whole(x) for x in parts],
        tuple(shapes), tuple(whole(x) for x in shapes), 1000, 8 * z.rows * z.rank, 8 * MIB,
    )


def table_kernel(z, tiles, sc, tokens, grad, unfold, job_of, *refs):
    got, (mine, theirs, back, down) = refs[: z.nd], refs[z.nd :]
    half = mine.shape[0]
    step = pl.program_id(0)

    @pl.when(step == 0)
    def _():
        for d in range(z.nd):
            for r in range(z.cap):
                slot = d * z.cap + r
                own = slice(r * z.halved, (r + 1) * z.halved)

                @pl.when(z.get(sc, "out_fill", slot) > 0)
                def _():
                    at = z.get(sc, "out_pos", slot)
                    values = got[(z.nd - d) % z.nd][own, z.rank :]
                    back[rows_of(at, z), :] = widen(values, z.get(sc, "out_rel", at), unfold[...], job_of[...], z)

                @pl.when(z.get(sc, "in_fill", slot) > 0)
                def _():
                    at = z.get(sc, "in_pos", slot)
                    values = widen(got[d][own, : z.rank], z.get(sc, "in_rel", at), unfold[...], job_of[...], z)
                    mask = row_mask(z.get(sc, "in_valid", at), z, z.wide)
                    down[rows_of(at, z), :] = jnp.where(mask, values, 0).astype(bf16)

    def put(wide, values):
        total = dot(wide[...], values[...], ((0,), (0,)))
        mine[...] = total[:half]
        theirs[...] = total[half:]

    @pl.when(step < tiles)
    def _():
        put(back, tokens)

    @pl.when(step == tiles)
    def _():
        put(down, grad)


def tables_of(z, sc, tokens, grad, unfold, job_of, got):
    tiles = z.width // z.heads
    half = z.wide // z.ns
    shape = jax.ShapeDtypeStruct((half, z.width + z.heads), f32)
    out = pl.BlockSpec((half, z.heads), lambda i, _: (0, i))
    return call(
        functools.partial(table_kernel, z, tiles), "job_tables", (tiles + 1,), sc,
        (tokens, grad, unfold, job_of, *got),
        [
            pl.BlockSpec((z.rows, z.heads), lambda i, _: (0, jnp.minimum(i, tiles - 1))),
            whole(grad), whole(unfold), whole(job_of),
        ]
        + [whole(x) for x in got],
        (shape, shape), (out, out),
        2 * z.wide * z.rows * (z.width + z.heads), 2 * z.rows * z.width + 4 * z.wide * z.width, TOKEN_LIMIT,
        scratch=(pltpu.VMEM((z.rows, z.wide), bf16), pltpu.VMEM((z.rows, z.wide), bf16)),
    )


def base_kernel(z, sc, tokens, *refs):
    pieces, (out, total) = refs[: z.nq], refs[z.nq :]
    step = pl.program_id(0)
    for r in range(z.nq):

        @pl.when(step == r)
        def _():
            part = dot(tokens[...], pieces[r][...], ((1,), (0,)))
            if r == 0:
                total[...] = part
            elif r < z.nq - 1:
                total[...] += part
            else:
                out[...] = (total[...] + part).astype(bf16)


def base_product(z, sc, tokens, pieces, d):
    at = z.at["quarter"]
    if d == 0:
        specs = [pl.BlockSpec((z.fq, z.columns), lambda i, q, r=r: (q[at + r], 0)) for r in range(z.nq)]
    else:
        specs = [whole(x) for x in pieces]
    return call(
        functools.partial(base_kernel, z), "base_%d" % d, (z.nq,), sc, (tokens, *pieces),
        [pl.BlockSpec((z.rows, z.fq), lambda i, q: (0, q[at + i]))] + specs,
        jax.ShapeDtypeStruct((z.rows, z.columns), bf16),
        pl.BlockSpec((z.rows, z.columns), lambda i, q: (0, 0)),
        2 * z.rows * z.width * z.columns, 2 * (z.rows * z.width + z.width * z.columns), TOKEN_LIMIT,
        scratch=(pltpu.VMEM((z.rows, z.columns), f32),),
    )


def layer_kernel(z, sc, sums, maps, unfold, job_of, *refs):
    m = z.per_head
    given, (outs, frozen) = refs[: m * z.nt], (refs[m * z.nt : -1], refs[-1])
    for j in range(m):
        total = given[j][...].astype(f32)
        for d in range(1, z.nt):
            total = total + given[d * m + j][...].astype(f32)
        for i in range(m):

            @pl.when(z.get(sc, "head", j) == i)
            def _():
                frozen[:, i * z.columns : (i + 1) * z.columns] = total

    for d in range(z.nd):
        for r in range(z.cap):
            slot = d * z.cap + r
            at = z.get(sc, "out_pos", slot)
            valid = jnp.where(z.get(sc, "out_fill", slot) > 0, z.get(sc, "out_valid", at), 0)
            wide = widen(sums[rows_of(at, z), : z.rank], z.get(sc, "out_rel", at), unfold[...], job_of[...], z)
            adapter = dot(wide, maps[...], ((1,), (0,)))
            layer = frozen[rows_of(at, z), :] + adapter_scale * adapter
            layer = jnp.where(row_mask(valid, z, z.heads), layer, 0.0)
            outs[d][r * z.halved : (r + 1) * z.halved, :] = layer.astype(bf16)


def layer_of(z, sc, sums, maps, unfold, job_of, given):
    shapes = [jax.ShapeDtypeStruct((z.cap * z.halved, z.heads), bf16)] * z.nd
    at = z.width // z.heads
    return call(
        functools.partial(layer_kernel, z), "layer", (1,), sc, (sums, maps, unfold, job_of, *given),
        [whole(sums), pl.BlockSpec((z.wide, z.heads), lambda i, _: (0, at)), whole(unfold), whole(job_of)]
        + [whole(x) for x in given],
        tuple(shapes), tuple(whole(x) for x in shapes),
        2 * z.rows * z.wide * z.heads, 6 * z.rows * z.heads, 16 * MIB,
        scratch=(pltpu.VMEM((z.rows, z.heads), f32),),
    )


def place_kernel(z, sc, *refs):
    got, out = refs[: z.nd], refs[z.nd]
    for d in range(z.nd):
        for r in range(z.cap):
            slot = d * z.cap + r

            @pl.when(z.get(sc, "in_fill", slot) > 0)
            def _():
                out[rows_of(z.get(sc, "in_pos", slot), z), :] = got[d][r * z.halved : (r + 1) * z.halved, :]


def place(z, sc, got):
    shape = jax.ShapeDtypeStruct((z.rows, z.heads), bf16)
    return call(
        functools.partial(place_kernel, z), "place", (1,), sc, got, [whole(x) for x in got],
        shape, whole(shape), 1000, 4 * z.rows * z.heads, 8 * MIB,
    )


def gradient_kernel(z, quarters, per, aliased, sc, maps, sums, unfold, job_of, *refs):
    grads, refs = refs[: z.nt], refs[z.nt :]
    count = len(quarters)
    pieces, refs = refs[: z.nd * count], refs[z.nd * count :]
    out, grad, back = refs[1:] if aliased else refs
    step = pl.program_id(0)
    m = z.per_head

    @pl.when(step == 0)
    def _():
        for v in range(z.nt * m):
            grad[v] = grads[v // m][:, v % m * z.columns : (v % m + 1) * z.columns]
        for b in range(z.blocks):
            own = slice(b * z.halved, (b + 1) * z.halved)
            back[own, :] = widen(sums[own, z.rank :], z.get(sc, "in_rel", b), unfold[...], job_of[...], z)

    for k in range(count):

        @pl.when(step // per == k)
        def _():
            total = adapter_scale * dot(back[...], maps[...], ((1,), (0,)))
            for d in range(z.nd):
                total = total + dot(grad[z.get(sc, "shard", d)], pieces[d * count + k][...], ((1,), (1,)))
            for b in range(z.blocks):
                own = slice(b * z.halved, (b + 1) * z.halved)
                mask = row_mask(z.get(sc, "in_valid", b), z, total.shape[1])
                out[own, :] = jnp.where(mask, total[own], 0.0).astype(bf16)


def token_gradient_of(z, sc, grads, maps, sums, unfold, job_of, piece_list, quarters, before):
    tile = min(512, z.fq)
    per = z.fq // tile
    at = z.at["quarter"]
    first = quarters[0]
    block = lambda i, q: (0, q[at + first + i // per] * per + i % per)
    specs, flat = [], []
    for d in range(z.nd):
        for k, r in enumerate(quarters):
            inner = lambda i, k=k: jnp.clip(i - k * per, 0, per - 1)
            if d == 0:
                index = lambda i, q, r=r, inner=inner: (q[at + r] * per + inner(i), 0)
            else:
                index = lambda i, q, inner=inner: (inner(i), 0)
            specs.append(pl.BlockSpec((tile, z.columns), index))
            flat.append(piece_list[d][r])
    inputs = [maps, sums, unfold, job_of, *grads, *flat]
    in_specs = [pl.BlockSpec((z.wide, tile), block), whole(sums), whole(unfold), whole(job_of)]
    in_specs += [whole(x) for x in grads] + specs
    alias = None
    if before is not None:
        alias = {1 + len(inputs): 0}
        inputs.append(before)
        in_specs.append(pl.BlockSpec(memory_space=pl.ANY))
    share = len(quarters) * z.fq
    return call(
        functools.partial(gradient_kernel, z, quarters, per, before is not None),
        "token_gradient_%d" % first, (len(quarters) * per,), sc, inputs, in_specs,
        jax.ShapeDtypeStruct((z.rows, z.width), bf16), pl.BlockSpec((z.rows, tile), block),
        2 * z.rows * share * (z.nd * z.columns + z.wide), 2 * share * (z.rows + z.nd * z.columns), 32 * MIB,
        scratch=(pltpu.VMEM((z.nd, z.rows, z.columns), bf16), pltpu.VMEM((z.rows, z.wide), bf16)),
        alias=alias,
    )


def body(
    tokens,
    cotangent,
    frozen_value_weight,
    adapter_down,
    adapter_up,
    tokens_per_job,
    packed_block_slots,
):
    nd, nt, ns, np_ = (lax.axis_size(a) for a in ("dp", "tensor", "sub", "parts"))
    z, t, s, p = (lax.axis_index(a) for a in ("dp", "tensor", "sub", "parts"))
    blocks, halved, width = tokens.shape[1:]
    heads = cotangent.shape[3]
    jobs_dev, rank, _ = adapter_down.shape
    columns = frozen_value_weight.shape[1]
    zz = Sizes(nd, nt, ns, np_, blocks, halved, width, heads, jobs_dev, rank, columns)
    rows, r2, m, cap = zz.rows, rank // ns, zz.per_head, zz.cap
    own_tokens = tokens.reshape(rows, width)
    own_grad = cotangent.reshape(rows, heads)

    quarters = jnp.stack([(p - a) % np_ * ns + (s - b) % ns for a in range(np_) for b in range(ns)]).astype(i32)
    moving = lax.dynamic_slice_in_dim(frozen_value_weight, (p * ns + s) * zz.fq, zz.fq, axis=0)
    rounds = [None, shifted(moving, "dp", nd, 1)]

    maps = jnp.concatenate([adapter_down, adapter_up], axis=2).reshape(jobs_dev, ns, r2, width + heads)
    maps = lax.dynamic_index_in_dim(maps, s, 1, keepdims=False)
    maps = jnp.concatenate(gather_shifts(maps, "dp", nd), axis=0).reshape(zz.jobs * r2, -1)
    maps = jnp.concatenate(gather_shifts(maps, "sub", ns), axis=0)
    grads = gather_shifts(own_grad, "tensor", nt)

    positions = jnp.arange(blocks, dtype=i32)
    dest = packed_block_slots // blocks
    same = dest[:, :, None] == dest[:, None, :]
    earlier = positions[None, None, :] < positions[None, :, None]
    send_rank = jnp.sum((same & earlier).astype(i32), axis=2, dtype=i32)
    flat_slots = packed_block_slots.reshape(-1)
    flat_ids = jnp.arange(nd * blocks, dtype=i32)
    slot_owner = flat_slots[None, :] == (z * blocks + positions)[:, None]
    block_ids = jnp.sum(jnp.where(slot_owner, flat_ids[None, :], 0), axis=1, dtype=i32)
    in_rank = jnp.sum(jnp.where(slot_owner, send_rank.reshape(-1)[None, :], 0), axis=1, dtype=i32)
    in_slot = (z - block_ids // blocks) % nd * cap + in_rank
    own_dest = lax.dynamic_index_in_dim(dest, z, 0, keepdims=False)
    own_rank = lax.dynamic_index_in_dim(send_rank, z, 0, keepdims=False)
    out_slot = (own_dest - z) % nd * cap + own_rank
    slot_range = jnp.arange(zz.slots, dtype=i32)

    def positions_of(slots):
        match = slots[None, :] == slot_range[:, None]
        return jnp.sum(jnp.where(match, positions[None, :], 0), axis=1, dtype=i32), jnp.any(match, axis=1)

    out_pos, out_fill = positions_of(out_slot)
    in_pos, in_fill = positions_of(in_slot)

    def facts(ids):
        job, valid = block_facts(tokens_per_job, ids, halved * ns)
        return (z - job // jobs_dev) % nd * jobs_dev + job % jobs_dev, valid - s * halved

    out_rel, out_valid = facts(z * blocks + positions)
    in_rel, in_valid = facts(block_ids)

    def arrival(index):
        found = (z - index * m - jnp.arange(m, dtype=i32)) % nd
        place_of = jnp.sum((found[None, :] < found[:, None]).astype(i32), axis=1)
        match = place_of[None, :] == jnp.arange(m, dtype=i32)[:, None]
        return jnp.sum(jnp.where(match, found[None, :], 0), axis=1, dtype=i32)

    shard_of = (z - jnp.arange(nd, dtype=i32)) % nd
    shard_at = (t - shard_of // m) % nt * m + shard_of % m
    head_at = (z - arrival(t)) % nd - t * m
    sc = jnp.concatenate(
        [
            x.astype(i32)
            for x in (out_pos, in_pos, out_fill, in_fill, out_rel, in_rel, out_valid, in_valid, quarters, shard_at, head_at)
        ]
    )
    column = jnp.arange(zz.wide, dtype=i32)
    job_of = (column // r2 % zz.jobs)[None, :]
    rank_of = column // (zz.jobs * r2) * r2 + column % r2
    unfold = (jnp.arange(rank, dtype=i32)[:, None] == rank_of[None, :]).astype(bf16)
    fold = unfold.astype(f32).T

    def spread_round(d, over_parts):
        pieces = []
        for y in over_parts:
            pieces += gather_shifts(y, "sub", ns)
        return pieces

    over = [None] * nd
    part = products(zz, sc, own_tokens, own_grad, maps, fold, job_of)
    part, rounds[1] = tie(part, rounds[1])
    over[1] = gather_shifts(rounds[1], "parts", np_)
    if nd > 2:
        rounds.append(shifted(rounds[1], "dp", nd, 1))
    parts = gather_shifts(part, "tensor", nt)
    late_tokens, _ = tie(own_tokens, part)
    base = [base_product(zz, sc, late_tokens, [frozen_value_weight] * zz.nq, 0)]
    tied = tie(base[0], *parts)
    base[0], parts = tied[0], tied[1:]
    sums, *pays = sums_of(zz, sc, parts)
    got = [shifted(pays[d], "dp", nd, d) for d in range(nd)]

    if nd > 2:
        rounds[2], over[1], got, grads = tie(rounds[2], over[1], got, grads)
        for d in range(3, nd):
            rounds.append(shifted(rounds[d - 1], "dp", nd, 1))
    mine, theirs = tables_of(zz, sc, own_tokens, own_grad, unfold, job_of, got)
    if nd > 2:
        theirs, over[1], late = tie(theirs, over[1], rounds[2])
        over[2] = gather_shifts(late, "parts", np_)
    theirs = shifted(theirs, "sub", ns, 1)
    piece_list = [[frozen_value_weight] * zz.nq, spread_round(1, over[1])]
    late_tokens, mine = tie(own_tokens, mine)
    base.append(base_product(zz, sc, late_tokens, piece_list[1], 1))
    mine, base[1], theirs = tie(mine, base[1], theirs)

    summed = (mine + theirs).reshape(nd, jobs_dev * r2, -1)
    sending = [summed[d].astype(bf16) for d in range(nd)]
    if nd > 3:
        rounds[3], sending, over[2] = tie(rounds[3], sending, over[2])
        over[3] = gather_shifts(rounds[3], "parts", np_)
    for d in range(4, nd):
        over[d] = gather_shifts(rounds[d], "parts", np_)
    for d in range(2, nd - 1):
        piece_list.append(spread_round(d, over[d]))
    tables = [sending[0]] + [shifted(sending[d], "dp", nd, -d) for d in range(1, nd)]

    for d in range(2, nd - 1):
        base.append(base_product(zz, sc, own_tokens, piece_list[d], d))

    def arriving(index, j):
        d = arrival(index)[j]
        picked = base[j]
        for k in range(j + 1, nd - m + j + 1):
            picked = jnp.where(d == k, base[k], picked)
        return picked

    def heads_of(j):
        own = arriving(t, j)
        return [own] + [shifted(arriving((t + d) % nt, j), "tensor", nt, d) for d in range(1, nt)]

    early = [heads_of(j) for j in range(m - 1)]
    tables, over[nd - 1], early = tie(tables, over[nd - 1], early)
    piece_list.append(spread_round(nd - 1, over[nd - 1]))
    total = sum(x.astype(f32) for x in tables)
    counts = lax.dynamic_slice_in_dim(tokens_per_job, z * jobs_dev, jobs_dev).astype(f32)
    total = total.reshape(jobs_dev, r2, -1) * (adapter_scale / counts)[:, None, None]
    halves = gather_shifts(total, "sub", ns)
    base.append(base_product(zz, sc, own_tokens, piece_list[nd - 1], nd - 1))
    base[-1], halves = tie(base[-1], halves)
    owned = jnp.concatenate(
        [sum(jnp.where((s - h) % ns == k, x, 0.0) for k, x in enumerate(halves)) for h in range(ns)], axis=1
    )
    grad_down, grad_up = owned[:, :, :width], owned[:, :, width:]

    slots = early + [heads_of(m - 1)]
    half = zz.nq // 2
    _, grads = tie(base[-1], grads)
    gradient = token_gradient_of(zz, sc, grads, maps, sums, unfold, job_of, piece_list, list(range(half)), None)
    given = [slots[j][d] for d in range(nt) for j in range(m)]
    gradient, grad_down, grad_up, *given = tie(gradient, grad_down, grad_up, *given)
    layer = layer_of(zz, sc, sums, maps, unfold, job_of, given)
    *layer, gradient = tie(*layer, gradient)
    landed = [shifted(layer[d], "dp", nd, d) for d in range(nd)]
    gradient = token_gradient_of(
        zz, sc, grads, maps, sums, unfold, job_of, piece_list, list(range(half, zz.nq)), gradient
    )
    gradient, *landed = tie(gradient, *landed)
    layer_output = place(zz, sc, landed)
    return (
        layer_output.reshape(1, blocks, halved, heads),
        gradient.reshape(1, blocks, halved, width),
        grad_down,
        grad_up,
    )


def solution(mesh):
    return jax.shard_map(
        body,
        mesh=mesh,
        in_specs=(
            P(("parts", "dp"), None, "sub", "tensor"),
            P(("parts", "dp"), None, "sub", "tensor"),
            P("tensor", "dp"),
            P(("parts", "dp"), None, "tensor"),
            P(("parts", "dp"), None, "tensor"),
            P("parts"),
            P("parts", None),
        ),
        out_specs=(
            P(("parts", "dp"), None, "sub", "tensor"),
            P(("parts", "dp"), None, "sub", "tensor"),
            P(("parts", "dp"), None, "tensor"),
            P(("parts", "dp"), None, "tensor"),
        ),
        check_vma=False,
    )
```

```python
import functools

import jax
import jax.numpy as jnp
from jax import lax
from jax.experimental import pallas as pl
from jax.experimental.pallas import tpu as pltpu
from jax.sharding import PartitionSpec as P

adapter_scale = 2.0
f32, bf16, i32 = jnp.float32, jnp.bfloat16, jnp.int32
MIB = 1 << 20
TOKEN_LIMIT = 50 * MIB


def block_facts(tokens_per_job, block_ids, block_rows):
    job_total = tokens_per_job.shape[0]
    blocks = (tokens_per_job + (block_rows - 1)) // block_rows
    block_ends = jnp.cumsum(blocks, dtype=jnp.int32)
    starts = block_ends - blocks
    job_index = jnp.sum(
        (block_ends[None, :] <= block_ids[:, None]).astype(jnp.int32), axis=1, dtype=jnp.int32
    )
    chosen = job_index[:, None] == jnp.arange(job_total, dtype=jnp.int32)[None, :]
    job_count = jnp.sum(jnp.where(chosen, tokens_per_job[None, :], 0), axis=1, dtype=jnp.int32)
    first_block = jnp.sum(jnp.where(chosen, starts[None, :], 0), axis=1, dtype=jnp.int32)
    valid_rows = jnp.clip(job_count - block_rows * (block_ids - first_block), 0, block_rows)
    return job_index, valid_rows


def shifted(values, axis, count, step):
    if step % count == 0:
        return values
    return lax.ppermute(values, axis, [(i, (i + step) % count) for i in range(count)])


def gather_shifts(values, axis, count):
    return [shifted(values, axis, count, d) for d in range(count)]


def dot(a, b, dims, precision=None):
    return lax.dot_general(a, b, (dims, ((), ())), precision=precision, preferred_element_type=f32)


def tie(*values):
    return lax.optimization_barrier(values)


class Sizes:
    def __init__(self, nd, nt, ns, np_, blocks, halved, width, heads, jobs_dev, rank, columns):
        self.nd, self.nt, self.ns, self.np_ = nd, nt, ns, np_
        self.blocks, self.halved, self.width, self.heads = blocks, halved, width, heads
        self.jobs, self.jobs_dev, self.rank, self.columns = nd * jobs_dev, jobs_dev, rank, columns
        self.wide = self.jobs * rank
        self.rows = blocks * halved
        self.cap = -(-blocks // nd)
        self.slots = nd * self.cap
        self.nq = np_ * ns
        self.fq = width // self.nq
        self.per_head = nd // nt
        self.chunks = 2
        self.fe = self.fq // self.chunks
        at, self.at = 0, {}
        for name, count in (
            ("out_pos", self.slots), ("in_pos", self.slots), ("out_fill", self.slots), ("in_fill", self.slots),
            ("out_rel", blocks), ("in_rel", blocks), ("out_valid", blocks), ("in_valid", blocks),
            ("quarter", self.nq), ("shard", nd), ("head", self.per_head),
            ("step", self.nq * self.chunks), ("pick", self.per_head * nt),
        ):
            self.at[name] = at
            at += count

    def get(self, ref, name, index):
        return ref[self.at[name] + index]


def call(kernel, name, grid, scalars, inputs, in_specs, out_shape, out_specs, flops, moved, limit, scratch=(), alias=None):
    return pl.pallas_call(
        kernel,
        out_shape=out_shape,
        grid_spec=pltpu.PrefetchScalarGridSpec(
            num_scalar_prefetch=1, grid=grid, in_specs=in_specs, out_specs=out_specs, scratch_shapes=list(scratch)
        ),
        input_output_aliases=alias or {},
        compiler_params=pltpu.CompilerParams(vmem_limit_bytes=limit),
        cost_estimate=pl.CostEstimate(flops=1000, bytes_accessed=1000, transcendentals=0),
        name=name,
    )(scalars, *inputs)


def whole(x):
    return pl.BlockSpec(x.shape, lambda *_: (0,) * len(x.shape))


def rows_of(index, z):
    return pl.ds(pl.multiple_of(index * z.halved, z.halved), z.halved)


def row_mask(valid, z, lanes):
    return lax.broadcasted_iota(i32, (z.halved, lanes), 0) < valid


def widen(values, rel, unfold, job_of, z):
    wide = dot(values, unfold, ((1,), (0,)))
    return jnp.where(job_of == rel, wide, 0.0).astype(bf16)


def products_kernel(z, n, sc, tokens, grad, maps, fold, job_of, out):
    step = pl.program_id(0)
    down = dot(tokens[...], maps[:, : z.width], ((1,), (1,)))
    back = dot(grad[...], maps[:, z.width :], ((1,), (1,)))
    for k in range(n):
        block = step * n + k
        own = slice(k * z.halved, (k + 1) * z.halved)
        picked = jnp.where(job_of[...] == z.get(sc, "out_rel", block), down[own], 0.0)
        out[own, : z.rank] = dot(picked, fold[...], ((1,), (0,)), lax.Precision.HIGHEST).astype(bf16)
        picked = jnp.where(job_of[...] == z.get(sc, "in_rel", block), back[own], 0.0)
        picked = jnp.where(row_mask(z.get(sc, "in_valid", block), z, z.wide), picked, 0.0)
        out[own, z.rank :] = dot(picked, fold[...], ((1,), (0,)), lax.Precision.HIGHEST).astype(bf16)


def products(z, sc, tokens, grad, maps, fold, job_of):
    n = 2
    return call(
        functools.partial(products_kernel, z, n), "adapter_products", (z.blocks // n,), sc,
        (tokens, grad, maps, fold, job_of),
        [
            pl.BlockSpec((n * z.halved, z.width), lambda i, _: (i, 0)),
            pl.BlockSpec((n * z.halved, z.heads), lambda i, _: (i, 0)),
            whole(maps), whole(fold), whole(job_of),
        ],
        jax.ShapeDtypeStruct((z.rows, 2 * z.rank), bf16),
        pl.BlockSpec((n * z.halved, 2 * z.rank), lambda i, _: (i, 0)),
        2 * z.rows * (z.width + z.heads) * z.wide, 2 * z.rows * (z.width + z.heads), TOKEN_LIMIT,
    )


def sums_kernel(z, sc, *refs):
    parts, outs = refs[: z.nt], refs[z.nt :]
    sums, pays = outs[0], outs[1:]
    total = parts[0][...].astype(f32)
    for part in parts[1:]:
        total = total + part[...].astype(f32)
    sums[...] = total.astype(bf16)
    for d in range(z.nd):
        back = (z.nd - d) % z.nd
        for r in range(z.cap):
            own = slice(r * z.halved, (r + 1) * z.halved)
            picked = sums[rows_of(z.get(sc, "out_pos", d * z.cap + r), z), : z.rank]
            pays[d][own, : z.rank] = jnp.where(z.get(sc, "out_fill", d * z.cap + r) > 0, picked, 0)
            picked = sums[rows_of(z.get(sc, "in_pos", back * z.cap + r), z), z.rank :]
            pays[d][own, z.rank :] = jnp.where(z.get(sc, "in_fill", back * z.cap + r) > 0, picked, 0)


def sums_of(z, sc, parts):
    shapes = [jax.ShapeDtypeStruct((z.rows, 2 * z.rank), bf16)]
    shapes += [jax.ShapeDtypeStruct((z.cap * z.halved, 2 * z.rank), bf16)] * z.nd
    return call(
        functools.partial(sums_kernel, z), "adapter_sums", (1,), sc, parts, [whole(x) for x in parts],
        tuple(shapes), tuple(whole(x) for x in shapes), 1000, 8 * z.rows * z.rank, 8 * MIB,
    )


def table_kernel(z, tiles, sc, tokens, grad, unfold, job_of, *refs):
    got, (mine, theirs, back, down, back_t, down_t) = refs[: z.nd], refs[z.nd :]
    half = mine.shape[0]
    step = pl.program_id(0)

    @pl.when(step == 0)
    def _():
        for d in range(z.nd):
            for r in range(z.cap):
                slot = d * z.cap + r
                own = slice(r * z.halved, (r + 1) * z.halved)

                @pl.when(z.get(sc, "out_fill", slot) > 0)
                def _():
                    at = z.get(sc, "out_pos", slot)
                    values = got[(z.nd - d) % z.nd][own, z.rank :]
                    back[rows_of(at, z), :] = widen(values, z.get(sc, "out_rel", at), unfold[...], job_of[...], z)

                @pl.when(z.get(sc, "in_fill", slot) > 0)
                def _():
                    at = z.get(sc, "in_pos", slot)
                    values = widen(got[d][own, : z.rank], z.get(sc, "in_rel", at), unfold[...], job_of[...], z)
                    mask = row_mask(z.get(sc, "in_valid", at), z, z.wide)
                    down[rows_of(at, z), :] = jnp.where(mask, values, 0).astype(bf16)

        same = lax.broadcasted_iota(i32, (z.rows, z.rows), 0) == lax.broadcasted_iota(i32, (z.rows, z.rows), 1)
        unit = jnp.where(same, 1.0, 0.0).astype(bf16)
        back_t[...] = dot(back[...], unit, ((0,), (0,))).astype(bf16)
        down_t[...] = dot(down[...], unit, ((0,), (0,))).astype(bf16)

    def put(wide, values):
        total = dot(wide[...], values[...], ((1,), (0,)))
        mine[...] = total[:half]
        theirs[...] = total[half:]

    @pl.when(step < tiles)
    def _():
        put(back_t, tokens)

    @pl.when(step == tiles)
    def _():
        put(down_t, grad)


def tables_of(z, sc, tokens, grad, unfold, job_of, got):
    tiles = z.width // z.heads
    half = z.wide // z.ns
    shape = jax.ShapeDtypeStruct((half, z.width + z.heads), f32)
    out = pl.BlockSpec((half, z.heads), lambda i, _: (0, i))
    return call(
        functools.partial(table_kernel, z, tiles), "job_tables", (tiles + 1,), sc,
        (tokens, grad, unfold, job_of, *got),
        [
            pl.BlockSpec((z.rows, z.heads), lambda i, _: (0, jnp.minimum(i, tiles - 1))),
            whole(grad), whole(unfold), whole(job_of),
        ]
        + [whole(x) for x in got],
        (shape, shape), (out, out),
        2 * z.wide * z.rows * (z.width + z.heads), 2 * z.rows * z.width + 4 * z.wide * z.width, TOKEN_LIMIT,
        scratch=(pltpu.VMEM((z.rows, z.wide), bf16),) * 2 + (pltpu.VMEM((z.wide, z.rows), bf16),) * 2,
    )


def base_kernel(z, d, count, started, partial, slot, others, sc, tokens, *refs):
    pieces, refs = refs[:count], refs[count:]
    if started:
        begun, refs = refs[0], refs[1:]
    earlier, refs = refs[: len(others)], refs[len(others) :]
    outs, total = refs[:-1], refs[-1]
    step = pl.program_id(0)
    for k in range(count):

        @pl.when(step == k)
        def _():
            part = dot(tokens[...], pieces[k][...], ((1,), (0,)))
            if k > 0:
                part = part + total[...]
            elif started:
                part = part + begun[...]
            if k < count - 1:
                total[...] = part
            elif partial:
                outs[0][...] = part
            else:
                done = part.astype(bf16)
                outs[0][...] = done
                for g in range(len(outs) - 1):
                    outs[1 + g][...] = done
                    for at, values in zip(others, earlier):

                        @pl.when(z.get(sc, "pick", g * z.per_head + slot) == at)
                        def _():
                            outs[1 + g][...] = values[...]


def base_product(z, sc, tokens, pieces, d, base, first=0, begun=None, partial=False):
    count, features = len(pieces), pieces[0].shape[0] if d else z.fq
    at = z.at["quarter"] if features == z.fq else z.at["step"]
    if d == 0:
        specs = [pl.BlockSpec((z.fq, z.columns), lambda i, q, r=r: (q[at + r], 0)) for r in range(z.nq)]
    else:
        specs = [whole(x) for x in pieces]
    inputs = [tokens, *pieces]
    if begun is not None:
        inputs.append(begun)
        specs.append(whole(begun))
    slot = d - (z.nd - z.per_head)
    others = []
    shapes = [jax.ShapeDtypeStruct((z.rows, z.columns), f32 if partial else bf16)]
    if slot >= 0 and not partial:
        others = list(range(slot, d))
        inputs += [base[k] for k in others]
        specs += [whole(base[k]) for k in others]
        shapes += [jax.ShapeDtypeStruct((z.rows, z.columns), bf16)] * z.nt
    return call(
        functools.partial(base_kernel, z, d, count, begun is not None, partial, slot, others),
        "base_%d_%d" % (d, first), (count,), sc, inputs,
        [pl.BlockSpec((z.rows, features), lambda i, q: (0, q[at + first + i]))] + specs,
        tuple(shapes), tuple(whole(x) for x in shapes),
        1000, 1000, TOKEN_LIMIT,
        scratch=(pltpu.VMEM((z.rows, z.columns), f32),),
    )


def layer_kernel(z, sc, sums, maps, unfold, job_of, *refs):
    m = z.per_head
    given, (outs, frozen) = refs[: m * z.nt], (refs[m * z.nt : -1], refs[-1])
    for j in range(m):
        total = given[j][...].astype(f32)
        for d in range(1, z.nt):
            total = total + given[d * m + j][...].astype(f32)
        for i in range(m):

            @pl.when(z.get(sc, "head", j) == i)
            def _():
                frozen[:, i * z.columns : (i + 1) * z.columns] = total

    for d in range(z.nd):
        for r in range(z.cap):
            slot = d * z.cap + r
            at = z.get(sc, "out_pos", slot)
            valid = jnp.where(z.get(sc, "out_fill", slot) > 0, z.get(sc, "out_valid", at), 0)
            wide = widen(sums[rows_of(at, z), : z.rank], z.get(sc, "out_rel", at), unfold[...], job_of[...], z)
            adapter = dot(wide, maps[...], ((1,), (0,)))
            layer = frozen[rows_of(at, z), :] + adapter_scale * adapter
            layer = jnp.where(row_mask(valid, z, z.heads), layer, 0.0)
            outs[d][r * z.halved : (r + 1) * z.halved, :] = layer.astype(bf16)


def layer_of(z, sc, sums, maps, unfold, job_of, given):
    shapes = [jax.ShapeDtypeStruct((z.cap * z.halved, z.heads), bf16)] * z.nd
    at = z.width // z.heads
    return call(
        functools.partial(layer_kernel, z), "layer", (1,), sc, (sums, maps, unfold, job_of, *given),
        [whole(sums), pl.BlockSpec((z.wide, z.heads), lambda i, _: (0, at)), whole(unfold), whole(job_of)]
        + [whole(x) for x in given],
        tuple(shapes), tuple(whole(x) for x in shapes),
        2 * z.rows * z.wide * z.heads, 6 * z.rows * z.heads, 16 * MIB,
        scratch=(pltpu.VMEM((z.rows, z.heads), f32),),
    )


def place_kernel(z, sc, *refs):
    got, out = refs[: z.nd], refs[z.nd]
    for d in range(z.nd):
        for r in range(z.cap):
            slot = d * z.cap + r

            @pl.when(z.get(sc, "in_fill", slot) > 0)
            def _():
                out[rows_of(z.get(sc, "in_pos", slot), z), :] = got[d][r * z.halved : (r + 1) * z.halved, :]


def place(z, sc, got):
    shape = jax.ShapeDtypeStruct((z.rows, z.heads), bf16)
    return call(
        functools.partial(place_kernel, z), "place", (1,), sc, got, [whole(x) for x in got],
        shape, whole(shape), 1000, 4 * z.rows * z.heads, 8 * MIB,
    )


def gradient_kernel(z, count, per, aliased, sc, maps, sums, unfold, job_of, *refs):
    grads, refs = refs[: z.nt], refs[z.nt :]
    whole_pieces, refs = refs[: (z.nd - 1) * count], refs[(z.nd - 1) * count :]
    last_pieces, refs = refs[: count * per], refs[count * per :]
    out, grad, back = refs[1:] if aliased else refs
    step = pl.program_id(0)
    m = z.per_head

    @pl.when(step == 0)
    def _():
        for v in range(z.nt * m):
            grad[v] = grads[v // m][:, v % m * z.columns : (v % m + 1) * z.columns]
        for b in range(z.blocks):
            own = slice(b * z.halved, (b + 1) * z.halved)
            back[own, :] = widen(sums[own, z.rank :], z.get(sc, "in_rel", b), unfold[...], job_of[...], z)

    for i in range(count * per):

        @pl.when(step == i)
        def _():
            total = adapter_scale * dot(back[...], maps[...], ((1,), (0,)))
            for d in range(z.nd):
                piece = last_pieces[i] if d == z.nd - 1 else whole_pieces[d * count + i // per]
                total = total + dot(grad[z.get(sc, "shard", d)], piece[...], ((1,), (1,)))
            for b in range(z.blocks):
                own = slice(b * z.halved, (b + 1) * z.halved)
                mask = row_mask(z.get(sc, "in_valid", b), z, total.shape[1])
                out[own, :] = jnp.where(mask, total[own], 0.0).astype(bf16)


def token_gradient_of(z, sc, grads, maps, sums, unfold, job_of, piece_list, quarters, before):
    tile, per = z.fe, z.chunks
    at = z.at["quarter"]
    first, count = quarters[0], len(quarters)
    block = lambda i, q: (0, q[at + first + i // per] * per + i % per)
    specs, flat = [], []
    for d in range(z.nd - 1):
        for k, r in enumerate(quarters):
            inner = lambda i, k=k: jnp.clip(i - k * per, 0, per - 1)
            if d == 0:
                index = lambda i, q, r=r, inner=inner: (q[at + r] * per + inner(i), 0)
            else:
                index = lambda i, q, inner=inner: (inner(i), 0)
            specs.append(pl.BlockSpec((tile, z.columns), index))
            flat.append(piece_list[d][r])
    for r in quarters:
        for c in range(per):
            flat.append(piece_list[z.nd - 1][c * z.nq + r])
            specs.append(whole(flat[-1]))
    inputs = [maps, sums, unfold, job_of, *grads, *flat]
    in_specs = [pl.BlockSpec((z.wide, tile), block), whole(sums), whole(unfold), whole(job_of)]
    in_specs += [whole(x) for x in grads] + specs
    alias = None
    if before is not None:
        alias = {1 + len(inputs): 0}
        inputs.append(before)
        in_specs.append(pl.BlockSpec(memory_space=pl.ANY))
    return call(
        functools.partial(gradient_kernel, z, count, per, before is not None),
        "token_gradient_%d" % first, (count * per,), sc, inputs, in_specs,
        jax.ShapeDtypeStruct((z.rows, z.width), bf16), pl.BlockSpec((z.rows, tile), block),
        1000, 1000, 32 * MIB,
        scratch=(pltpu.VMEM((z.nd, z.rows, z.columns), bf16), pltpu.VMEM((z.rows, z.wide), bf16)),
        alias=alias,
    )


def body(
    tokens,
    cotangent,
    frozen_value_weight,
    adapter_down,
    adapter_up,
    tokens_per_job,
    packed_block_slots,
):
    nd, nt, ns, np_ = (lax.axis_size(a) for a in ("dp", "tensor", "sub", "parts"))
    z, t, s, p = (lax.axis_index(a) for a in ("dp", "tensor", "sub", "parts"))
    blocks, halved, width = tokens.shape[1:]
    heads = cotangent.shape[3]
    jobs_dev, rank, _ = adapter_down.shape
    columns = frozen_value_weight.shape[1]
    zz = Sizes(nd, nt, ns, np_, blocks, halved, width, heads, jobs_dev, rank, columns)
    rows, r2, m, cap = zz.rows, rank // ns, zz.per_head, zz.cap
    own_tokens = tokens.reshape(rows, width)
    own_grad = cotangent.reshape(rows, heads)

    quarters = jnp.stack([(p - a) % np_ * ns + (s - b) % ns for a in range(np_) for b in range(ns)]).astype(i32)
    moving = lax.dynamic_slice_in_dim(frozen_value_weight, (p * ns + s) * zz.fq, zz.fq, axis=0)
    rounds = [None, shifted(moving, "dp", nd, 1)]

    maps = jnp.concatenate([adapter_down, adapter_up], axis=2).reshape(jobs_dev, ns, r2, width + heads)
    maps = lax.dynamic_index_in_dim(maps, s, 1, keepdims=False)
    maps, rounds[1] = tie(gather_shifts(maps, "dp", nd), rounds[1])
    maps = jnp.concatenate(maps, axis=0).reshape(zz.jobs * r2, -1)
    maps = jnp.concatenate(gather_shifts(maps, "sub", ns), axis=0)
    grads = gather_shifts(own_grad, "tensor", nt)

    positions = jnp.arange(blocks, dtype=i32)
    dest = packed_block_slots // blocks
    same = dest[:, :, None] == dest[:, None, :]
    earlier = positions[None, None, :] < positions[None, :, None]
    send_rank = jnp.sum((same & earlier).astype(i32), axis=2, dtype=i32)
    flat_slots = packed_block_slots.reshape(-1)
    flat_ids = jnp.arange(nd * blocks, dtype=i32)
    slot_owner = flat_slots[None, :] == (z * blocks + positions)[:, None]
    block_ids = jnp.sum(jnp.where(slot_owner, flat_ids[None, :], 0), axis=1, dtype=i32)
    in_rank = jnp.sum(jnp.where(slot_owner, send_rank.reshape(-1)[None, :], 0), axis=1, dtype=i32)
    in_slot = (z - block_ids // blocks) % nd * cap + in_rank
    own_dest = lax.dynamic_index_in_dim(dest, z, 0, keepdims=False)
    own_rank = lax.dynamic_index_in_dim(send_rank, z, 0, keepdims=False)
    out_slot = (own_dest - z) % nd * cap + own_rank
    slot_range = jnp.arange(zz.slots, dtype=i32)

    def positions_of(slots):
        match = slots[None, :] == slot_range[:, None]
        return jnp.sum(jnp.where(match, positions[None, :], 0), axis=1, dtype=i32), jnp.any(match, axis=1)

    out_pos, out_fill = positions_of(out_slot)
    in_pos, in_fill = positions_of(in_slot)

    def facts(ids):
        job, valid = block_facts(tokens_per_job, ids, halved * ns)
        return (z - job // jobs_dev) % nd * jobs_dev + job % jobs_dev, valid - s * halved

    out_rel, out_valid = facts(z * blocks + positions)
    in_rel, in_valid = facts(block_ids)

    def arrival(index):
        found = (z - index * m - jnp.arange(m, dtype=i32)) % nd
        place_of = jnp.sum((found[None, :] < found[:, None]).astype(i32), axis=1)
        match = place_of[None, :] == jnp.arange(m, dtype=i32)[:, None]
        return jnp.sum(jnp.where(match, found[None, :], 0), axis=1, dtype=i32)

    shard_of = (z - jnp.arange(nd, dtype=i32)) % nd
    shard_at = (t - shard_of // m) % nt * m + shard_of % m
    arrivals = [arrival((t + g) % nt) for g in range(nt)]
    head_at = (z - arrivals[0]) % nd - t * m
    steps = (quarters[None, :] * zz.chunks + jnp.arange(zz.chunks, dtype=i32)[:, None]).reshape(-1)
    sc = jnp.concatenate(
        [
            x.astype(i32)
            for x in (out_pos, in_pos, out_fill, in_fill, out_rel, in_rel, out_valid, in_valid, quarters, shard_at, head_at, steps, *arrivals)
        ]
    )
    column = jnp.arange(zz.wide, dtype=i32)
    job_of = (column // r2 % zz.jobs)[None, :]
    rank_of = column // (zz.jobs * r2) * r2 + column % r2
    unfold = (jnp.arange(rank, dtype=i32)[:, None] == rank_of[None, :]).astype(bf16)
    fold = unfold.astype(f32).T

    def spread_round(over_parts):
        return [x for y in over_parts for x in gather_shifts(y, "sub", ns)]

    last = nd - 1
    over = [None] * nd
    over[1] = gather_shifts(rounds[1], "parts", np_)
    for d in range(2, last):
        rounds.append(shifted(rounds[-1], "dp", nd, 1))
    part = products(zz, sc, own_tokens, own_grad, maps, fold, job_of)
    parts = gather_shifts(part, "tensor", nt)
    late_tokens, _ = tie(own_tokens, part)
    base = [base_product(zz, sc, late_tokens, [frozen_value_weight] * zz.nq, 0, None)[0]]
    base[0], parts = tie(base[0], parts)
    sums, *pays = sums_of(zz, sc, parts)

    rounds[last - 1], over[1], pays, grads = tie(rounds[last - 1], over[1], pays, grads)
    ends = [
        shifted(rounds[last - 1][c * zz.fe : (c + 1) * zz.fe], "dp", nd, 1) for c in range(zz.chunks)
    ]
    got = [shifted(pays[d], "dp", nd, d) for d in range(nd)]
    mine, theirs = tables_of(zz, sc, own_tokens, own_grad, unfold, job_of, got)
    for d in range(2, last):
        over[d] = gather_shifts(rounds[d], "parts", np_)
    mine, theirs, ends[0] = tie(mine, theirs, ends[0])
    end_over = [gather_shifts(ends[0], "parts", np_)]
    theirs = shifted(theirs, "sub", ns, 1)
    piece_list = [[frozen_value_weight] * zz.nq, spread_round(over[1])]
    late_tokens, mine = tie(own_tokens, mine)
    base.append(base_product(zz, sc, late_tokens, piece_list[1], 1, base)[0])
    base[1], ends[1:], over[2:last] = tie(base[1], ends[1:], over[2:last])
    end_over += [gather_shifts(x, "parts", np_) for x in ends[1:]]
    piece_list += [spread_round(over[d]) for d in range(2, last)]
    end_over[0], *piece_list[2:] = tie(end_over[0], *piece_list[2:])

    slots = []

    def finish(d, made):
        base.append(made[0])
        if len(made) > 1:
            slots.append([made[1]] + [shifted(made[1 + g], "tensor", nt, g) for g in range(1, nt)])

    for d in range(2, last):
        finish(d, base_product(zz, sc, own_tokens, piece_list[d], d, base))
    base[-1], mine, theirs = tie(base[-1], mine, theirs)

    summed = (mine + theirs).reshape(nd, jobs_dev * r2, -1)
    sending = [summed[d].astype(bf16) for d in range(nd)]
    tables = [sending[0]] + [shifted(sending[d], "dp", nd, -d) for d in range(1, nd)]
    ahead, behind = [x for y in end_over[:-1] for x in spread_round(y)], end_over[-1]
    ahead += gather_shifts(behind[0], "sub", ns)
    begun = base_product(zz, sc, own_tokens, ahead, last, base, 0, None, True)[0]
    begun, tables, behind, slots = tie(begun, tables, behind, slots)
    tail = spread_round(behind[1:])
    piece_list.append(ahead + tail)
    total = sum(x.astype(f32) for x in tables)
    counts = lax.dynamic_slice_in_dim(tokens_per_job, z * jobs_dev, jobs_dev).astype(f32)
    total = total.reshape(jobs_dev, r2, -1) * (adapter_scale / counts)[:, None, None]
    halves = gather_shifts(total, "sub", ns)
    finish(last, base_product(zz, sc, own_tokens, tail, last, base, len(ahead), begun))
    base[-1], halves, grads = tie(base[-1], halves, grads)
    owned = jnp.concatenate(
        [sum(jnp.where((s - h) % ns == k, x, 0.0) for k, x in enumerate(halves)) for h in range(ns)], axis=1
    )
    grad_down, grad_up = owned[:, :, :width], owned[:, :, width:]

    half = zz.nq // 2
    gradient = token_gradient_of(zz, sc, grads, maps, sums, unfold, job_of, piece_list, list(range(half)), None)
    given = [slots[j][d] for d in range(nt) for j in range(m)]
    gradient, grad_down, grad_up, *given = tie(gradient, grad_down, grad_up, *given)
    layer = layer_of(zz, sc, sums, maps, unfold, job_of, given)
    *layer, gradient = tie(*layer, gradient)
    landed = [shifted(layer[d], "dp", nd, d) for d in range(nd)]
    gradient = token_gradient_of(
        zz, sc, grads, maps, sums, unfold, job_of, piece_list, list(range(half, zz.nq)), gradient
    )
    gradient, *landed = tie(gradient, *landed)
    layer_output = place(zz, sc, landed)
    return (
        layer_output.reshape(1, blocks, halved, heads),
        gradient.reshape(1, blocks, halved, width),
        grad_down,
        grad_up,
    )


def solution(mesh):
    return jax.shard_map(
        body,
        mesh=mesh,
        in_specs=(
            P(("parts", "dp"), None, "sub", "tensor"),
            P(("parts", "dp"), None, "sub", "tensor"),
            P("tensor", "dp"),
            P(("parts", "dp"), None, "tensor"),
            P(("parts", "dp"), None, "tensor"),
            P("parts"),
            P("parts", None),
        ),
        out_specs=(
            P(("parts", "dp"), None, "sub", "tensor"),
            P(("parts", "dp"), None, "sub", "tensor"),
            P(("parts", "dp"), None, "tensor"),
            P(("parts", "dp"), None, "tensor"),
        ),
        check_vma=False,
    )
```

```python
import functools

import jax
import jax.numpy as jnp
from jax import lax
from jax.experimental import pallas as pl
from jax.experimental.pallas import tpu as pltpu
from jax.sharding import PartitionSpec as P

adapter_scale = 2.0
f32, bf16, i32 = jnp.float32, jnp.bfloat16, jnp.int32
MIB = 1 << 20
TOKEN_LIMIT = 50 * MIB


def block_facts(tokens_per_job, block_ids, block_rows):
    job_total = tokens_per_job.shape[0]
    blocks = (tokens_per_job + (block_rows - 1)) // block_rows
    block_ends = jnp.cumsum(blocks, dtype=jnp.int32)
    starts = block_ends - blocks
    job_index = jnp.sum(
        (block_ends[None, :] <= block_ids[:, None]).astype(jnp.int32), axis=1, dtype=jnp.int32
    )
    chosen = job_index[:, None] == jnp.arange(job_total, dtype=jnp.int32)[None, :]
    job_count = jnp.sum(jnp.where(chosen, tokens_per_job[None, :], 0), axis=1, dtype=jnp.int32)
    first_block = jnp.sum(jnp.where(chosen, starts[None, :], 0), axis=1, dtype=jnp.int32)
    valid_rows = jnp.clip(job_count - block_rows * (block_ids - first_block), 0, block_rows)
    return job_index, valid_rows


def shifted(values, axis, count, step):
    if step % count == 0:
        return values
    return lax.ppermute(values, axis, [(i, (i + step) % count) for i in range(count)])


def gather_shifts(values, axis, count):
    return [shifted(values, axis, count, d) for d in range(count)]


def dot(a, b, dims, precision=None):
    return lax.dot_general(a, b, (dims, ((), ())), precision=precision, preferred_element_type=f32)


def tie(*values):
    return lax.optimization_barrier(values)


class Sizes:
    def __init__(self, nd, nt, ns, np_, blocks, halved, width, heads, jobs_dev, rank, columns):
        self.nd, self.nt, self.ns, self.np_ = nd, nt, ns, np_
        self.blocks, self.halved, self.width, self.heads = blocks, halved, width, heads
        self.jobs, self.jobs_dev, self.rank, self.columns = nd * jobs_dev, jobs_dev, rank, columns
        self.wide = self.jobs * rank
        self.rows = blocks * halved
        self.cap = -(-blocks // nd)
        self.slots = nd * self.cap
        self.nq = np_ * ns
        self.fq = width // self.nq
        self.per_head = nd // nt
        self.chunks = 2
        self.fe = self.fq // self.chunks
        at, self.at = 0, {}
        for name, count in (
            ("out_pos", self.slots), ("in_pos", self.slots), ("out_fill", self.slots), ("in_fill", self.slots),
            ("out_rel", blocks), ("in_rel", blocks), ("out_valid", blocks), ("in_valid", blocks),
            ("quarter", self.nq), ("shard", nd), ("head", self.per_head),
            ("step", self.nq * self.chunks), ("pick", self.per_head * nt),
        ):
            self.at[name] = at
            at += count

    def get(self, ref, name, index):
        return ref[self.at[name] + index]


def call(kernel, name, grid, scalars, inputs, in_specs, out_shape, out_specs, flops, moved, limit, scratch=(), alias=None):
    return pl.pallas_call(
        kernel,
        out_shape=out_shape,
        grid_spec=pltpu.PrefetchScalarGridSpec(
            num_scalar_prefetch=1, grid=grid, in_specs=in_specs, out_specs=out_specs, scratch_shapes=list(scratch)
        ),
        input_output_aliases=alias or {},
        compiler_params=pltpu.CompilerParams(vmem_limit_bytes=limit),
        cost_estimate=pl.CostEstimate(flops=1000, bytes_accessed=1000, transcendentals=0),
        name=name,
    )(scalars, *inputs)


ANY = pl.BlockSpec(memory_space=pl.ANY)


def whole(x):
    return pl.BlockSpec(x.shape, lambda *_: (0,) * len(x.shape))


def rows_of(index, z):
    return pl.ds(pl.multiple_of(index * z.halved, z.halved), z.halved)


def row_mask(valid, z, lanes):
    return lax.broadcasted_iota(i32, (z.halved, lanes), 0) < valid


def widen(values, rel, unfold, job_of, z):
    wide = dot(values, unfold, ((1,), (0,)))
    return jnp.where(job_of == rel, wide, 0.0).astype(bf16)


def products_kernel(z, n, sc, tokens, grad, maps, fold, job_of, out, held, sems):
    many = z.blocks // n
    copies = [
        pltpu.make_async_copy(tokens.at[pl.ds(k * n * z.halved, n * z.halved), :], held.at[k], sems.at[k])
        for k in range(many)
    ]
    for copy in copies:
        copy.start()
    back = dot(grad[...], maps[:, z.width :], ((1,), (1,)))
    for block in range(z.blocks):
        own = slice(block * z.halved, (block + 1) * z.halved)
        picked = jnp.where(job_of[...] == z.get(sc, "in_rel", block), back[own], 0.0)
        picked = jnp.where(row_mask(z.get(sc, "in_valid", block), z, z.wide), picked, 0.0)
        out[own, z.rank :] = dot(picked, fold[...], ((1,), (0,)), lax.Precision.HIGHEST).astype(bf16)
    for k in range(many):
        copies[k].wait()
        down = dot(held[k], maps[:, : z.width], ((1,), (1,)))
        for r in range(n):
            block = k * n + r
            own = slice(block * z.halved, (block + 1) * z.halved)
            mine = slice(r * z.halved, (r + 1) * z.halved)
            picked = jnp.where(job_of[...] == z.get(sc, "out_rel", block), down[mine], 0.0)
            out[own, : z.rank] = dot(picked, fold[...], ((1,), (0,)), lax.Precision.HIGHEST).astype(bf16)


def products(z, sc, tokens, grad, maps, fold, job_of):
    n = 2
    shape = jax.ShapeDtypeStruct((z.rows, 2 * z.rank), bf16)
    return call(
        functools.partial(products_kernel, z, n), "adapter_products", (1,), sc,
        (tokens, grad, maps, fold, job_of),
        [ANY, whole(grad), whole(maps), whole(fold), whole(job_of)],
        shape, whole(shape), 1000, 1000, TOKEN_LIMIT,
        scratch=(
            pltpu.VMEM((z.blocks // n, n * z.halved, z.width), bf16),
            pltpu.SemaphoreType.DMA((z.blocks // n,)),
        ),
    )


def sums_kernel(z, sc, *refs):
    parts, outs = refs[: z.nt], refs[z.nt :]
    sums, pays = outs[0], outs[1:]
    total = parts[0][...].astype(f32)
    for part in parts[1:]:
        total = total + part[...].astype(f32)
    sums[...] = total.astype(bf16)
    for d in range(z.nd):
        back = (z.nd - d) % z.nd
        for r in range(z.cap):
            own = slice(r * z.halved, (r + 1) * z.halved)
            picked = sums[rows_of(z.get(sc, "out_pos", d * z.cap + r), z), : z.rank]
            pays[d][own, : z.rank] = jnp.where(z.get(sc, "out_fill", d * z.cap + r) > 0, picked, 0)
            picked = sums[rows_of(z.get(sc, "in_pos", back * z.cap + r), z), z.rank :]
            pays[d][own, z.rank :] = jnp.where(z.get(sc, "in_fill", back * z.cap + r) > 0, picked, 0)


def sums_of(z, sc, parts):
    shapes = [jax.ShapeDtypeStruct((z.rows, 2 * z.rank), bf16)]
    shapes += [jax.ShapeDtypeStruct((z.cap * z.halved, 2 * z.rank), bf16)] * z.nd
    return call(
        functools.partial(sums_kernel, z), "adapter_sums", (1,), sc, parts, [whole(x) for x in parts],
        tuple(shapes), tuple(whole(x) for x in shapes), 1000, 8 * z.rows * z.rank, 8 * MIB,
    )


def table_kernel(z, tiles, sc, tokens, grad, unfold, job_of, *refs):
    got, (mine, theirs, back, down, back_t, down_t, held, sems) = refs[: z.nd], refs[z.nd :]
    half = mine.shape[0]
    part = z.width // tiles
    copies = [
        pltpu.make_async_copy(tokens.at[:, pl.ds(k * part, part)], held.at[k], sems.at[k]) for k in range(tiles)
    ]
    for copy in copies:
        copy.start()
    for d in range(z.nd):
        for r in range(z.cap):
            slot = d * z.cap + r
            own = slice(r * z.halved, (r + 1) * z.halved)

            @pl.when(z.get(sc, "out_fill", slot) > 0)
            def _():
                at = z.get(sc, "out_pos", slot)
                values = got[(z.nd - d) % z.nd][own, z.rank :]
                back[rows_of(at, z), :] = widen(values, z.get(sc, "out_rel", at), unfold[...], job_of[...], z)

            @pl.when(z.get(sc, "in_fill", slot) > 0)
            def _():
                at = z.get(sc, "in_pos", slot)
                values = widen(got[d][own, : z.rank], z.get(sc, "in_rel", at), unfold[...], job_of[...], z)
                mask = row_mask(z.get(sc, "in_valid", at), z, z.wide)
                down[rows_of(at, z), :] = jnp.where(mask, values, 0).astype(bf16)

    same = lax.broadcasted_iota(i32, (z.rows, z.rows), 0) == lax.broadcasted_iota(i32, (z.rows, z.rows), 1)
    unit = jnp.where(same, 1.0, 0.0).astype(bf16)
    back_t[...] = dot(back[...], unit, ((0,), (0,))).astype(bf16)
    down_t[...] = dot(down[...], unit, ((0,), (0,))).astype(bf16)
    total = dot(down_t[...], grad[...], ((1,), (0,)))
    mine[:, z.width :] = total[:half]
    theirs[:, z.width :] = total[half:]
    for k in range(tiles):
        copies[k].wait()
        total = dot(back_t[...], held[k], ((1,), (0,)))
        mine[:, k * part : (k + 1) * part] = total[:half]
        theirs[:, k * part : (k + 1) * part] = total[half:]


def tables_of(z, sc, tokens, grad, unfold, job_of, got):
    tiles = 4
    shape = jax.ShapeDtypeStruct((z.wide // z.ns, z.width + z.heads), f32)
    return call(
        functools.partial(table_kernel, z, tiles), "job_tables", (1,), sc,
        (tokens, grad, unfold, job_of, *got),
        [ANY, whole(grad), whole(unfold), whole(job_of)] + [whole(x) for x in got],
        (shape, shape), (whole(shape), whole(shape)), 1000, 1000, TOKEN_LIMIT,
        scratch=(pltpu.VMEM((z.rows, z.wide), bf16),) * 2
        + (pltpu.VMEM((z.wide, z.rows), bf16),) * 2
        + (pltpu.VMEM((tiles, z.rows, z.width // tiles), bf16), pltpu.SemaphoreType.DMA((tiles,))),
    )


def base_kernel(z, d, count, started, partial, slot, others, at, features, sc, tokens, *refs):
    pieces, refs = refs[:count], refs[count:]
    if started:
        begun, refs = refs[0], refs[1:]
    earlier, refs = refs[: len(others)], refs[len(others) :]
    outs, (held, parts, sems) = refs[:-3], refs[-3:]
    copies = []
    for k in range(count):
        start = pl.multiple_of(sc[at + k] * features, features)
        copies.append(pltpu.make_async_copy(tokens.at[:, pl.ds(start, features)], held.at[k], sems.at[0, k]))
        source = pieces[k].at[pl.ds(start, features), :] if d == 0 else pieces[k]
        copies.append(pltpu.make_async_copy(source, parts.at[k], sems.at[1, k]))
    for copy in copies:
        copy.start()
    total = begun[...] if started else None
    for k in range(count):
        copies[2 * k].wait()
        copies[2 * k + 1].wait()
        part = dot(held[k], parts[k], ((1,), (0,)))
        total = part if total is None else total + part
    if partial:
        outs[0][...] = total
        return
    done = total.astype(bf16)
    outs[0][...] = done
    for g in range(len(outs) - 1):
        outs[1 + g][...] = done
        for where, values in zip(others, earlier):

            @pl.when(z.get(sc, "pick", g * z.per_head + slot) == where)
            def _():
                outs[1 + g][...] = values[...]


def base_product(z, sc, tokens, pieces, d, base, first=0, begun=None, partial=False):
    count, features = len(pieces), pieces[0].shape[0] if d else z.fq
    at = z.at["quarter"] if features == z.fq else z.at["step"] + first
    inputs, specs = [tokens, *pieces], [ANY] * (1 + count)
    if begun is not None:
        inputs.append(begun)
        specs.append(whole(begun))
    slot = d - (z.nd - z.per_head)
    others = []
    shapes = [jax.ShapeDtypeStruct((z.rows, z.columns), f32 if partial else bf16)]
    if slot >= 0 and not partial:
        others = list(range(slot, d))
        inputs += [base[k] for k in others]
        specs += [whole(base[k]) for k in others]
        shapes += [jax.ShapeDtypeStruct((z.rows, z.columns), bf16)] * z.nt
    return call(
        functools.partial(base_kernel, z, d, count, begun is not None, partial, slot, others, at, features),
        "base_%d_%d" % (d, first), (1,), sc, inputs, specs,
        tuple(shapes), tuple(whole(x) for x in shapes),
        1000, 1000, TOKEN_LIMIT,
        scratch=(
            pltpu.VMEM((count, z.rows, features), bf16),
            pltpu.VMEM((count, features, z.columns), bf16),
            pltpu.SemaphoreType.DMA((2, count)),
        ),
    )


def layer_kernel(z, sc, sums, maps, unfold, job_of, *refs):
    m = z.per_head
    given, (outs, frozen) = refs[: m * z.nt], (refs[m * z.nt : -1], refs[-1])
    for j in range(m):
        total = given[j][...].astype(f32)
        for d in range(1, z.nt):
            total = total + given[d * m + j][...].astype(f32)
        for i in range(m):

            @pl.when(z.get(sc, "head", j) == i)
            def _():
                frozen[:, i * z.columns : (i + 1) * z.columns] = total

    for d in range(z.nd):
        for r in range(z.cap):
            slot = d * z.cap + r
            at = z.get(sc, "out_pos", slot)
            valid = jnp.where(z.get(sc, "out_fill", slot) > 0, z.get(sc, "out_valid", at), 0)
            wide = widen(sums[rows_of(at, z), : z.rank], z.get(sc, "out_rel", at), unfold[...], job_of[...], z)
            adapter = dot(wide, maps[...], ((1,), (0,)))
            layer = frozen[rows_of(at, z), :] + adapter_scale * adapter
            layer = jnp.where(row_mask(valid, z, z.heads), layer, 0.0)
            outs[d][r * z.halved : (r + 1) * z.halved, :] = layer.astype(bf16)


def layer_of(z, sc, sums, maps, unfold, job_of, given):
    shapes = [jax.ShapeDtypeStruct((z.cap * z.halved, z.heads), bf16)] * z.nd
    at = z.width // z.heads
    return call(
        functools.partial(layer_kernel, z), "layer", (1,), sc, (sums, maps, unfold, job_of, *given),
        [whole(sums), pl.BlockSpec((z.wide, z.heads), lambda i, _: (0, at)), whole(unfold), whole(job_of)]
        + [whole(x) for x in given],
        tuple(shapes), tuple(whole(x) for x in shapes),
        2 * z.rows * z.wide * z.heads, 6 * z.rows * z.heads, 16 * MIB,
        scratch=(pltpu.VMEM((z.rows, z.heads), f32),),
    )


def place_kernel(z, sc, *refs):
    got, out = refs[: z.nd], refs[z.nd]
    for d in range(z.nd):
        for r in range(z.cap):
            slot = d * z.cap + r

            @pl.when(z.get(sc, "in_fill", slot) > 0)
            def _():
                out[rows_of(z.get(sc, "in_pos", slot), z), :] = got[d][r * z.halved : (r + 1) * z.halved, :]


def place(z, sc, got):
    shape = jax.ShapeDtypeStruct((z.rows, z.heads), bf16)
    return call(
        functools.partial(place_kernel, z), "place", (1,), sc, got, [whole(x) for x in got],
        shape, whole(shape), 1000, 4 * z.rows * z.heads, 8 * MIB,
    )


def gradient_kernel(z, count, per, aliased, sc, maps, sums, unfold, job_of, *refs):
    grads, refs = refs[: z.nt], refs[z.nt :]
    whole_pieces, refs = refs[: (z.nd - 1) * count], refs[(z.nd - 1) * count :]
    last_pieces, refs = refs[: count * per], refs[count * per :]
    out, grad, back = refs[1:] if aliased else refs
    step = pl.program_id(0)
    m = z.per_head

    @pl.when(step == 0)
    def _():
        for v in range(z.nt * m):
            grad[v] = grads[v // m][:, v % m * z.columns : (v % m + 1) * z.columns]
        for b in range(z.blocks):
            own = slice(b * z.halved, (b + 1) * z.halved)
            back[own, :] = widen(sums[own, z.rank :], z.get(sc, "in_rel", b), unfold[...], job_of[...], z)

    for i in range(count * per):

        @pl.when(step == i)
        def _():
            total = adapter_scale * dot(back[...], maps[...], ((1,), (0,)))
            for d in range(z.nd):
                piece = last_pieces[i] if d == z.nd - 1 else whole_pieces[d * count + i // per]
                total = total + dot(grad[z.get(sc, "shard", d)], piece[...], ((1,), (1,)))
            for b in range(z.blocks):
                own = slice(b * z.halved, (b + 1) * z.halved)
                mask = row_mask(z.get(sc, "in_valid", b), z, total.shape[1])
                out[own, :] = jnp.where(mask, total[own], 0.0).astype(bf16)


def token_gradient_of(z, sc, grads, maps, sums, unfold, job_of, piece_list, quarters, before):
    tile, per = z.fe, z.chunks
    at = z.at["quarter"]
    first, count = quarters[0], len(quarters)
    block = lambda i, q: (0, q[at + first + i // per] * per + i % per)
    specs, flat = [], []
    for d in range(z.nd - 1):
        for k, r in enumerate(quarters):
            inner = lambda i, k=k: jnp.clip(i - k * per, 0, per - 1)
            if d == 0:
                index = lambda i, q, r=r, inner=inner: (q[at + r] * per + inner(i), 0)
            else:
                index = lambda i, q, inner=inner: (inner(i), 0)
            specs.append(pl.BlockSpec((tile, z.columns), index))
            flat.append(piece_list[d][r])
    for r in quarters:
        for c in range(per):
            flat.append(piece_list[z.nd - 1][c * z.nq + r])
            specs.append(whole(flat[-1]))
    inputs = [maps, sums, unfold, job_of, *grads, *flat]
    in_specs = [pl.BlockSpec((z.wide, tile), block), whole(sums), whole(unfold), whole(job_of)]
    in_specs += [whole(x) for x in grads] + specs
    alias = None
    if before is not None:
        alias = {1 + len(inputs): 0}
        inputs.append(before)
        in_specs.append(pl.BlockSpec(memory_space=pl.ANY))
    return call(
        functools.partial(gradient_kernel, z, count, per, before is not None),
        "token_gradient_%d" % first, (count * per,), sc, inputs, in_specs,
        jax.ShapeDtypeStruct((z.rows, z.width), bf16), pl.BlockSpec((z.rows, tile), block),
        1000, 1000, 32 * MIB,
        scratch=(pltpu.VMEM((z.nd, z.rows, z.columns), bf16), pltpu.VMEM((z.rows, z.wide), bf16)),
        alias=alias,
    )


def body(
    tokens,
    cotangent,
    frozen_value_weight,
    adapter_down,
    adapter_up,
    tokens_per_job,
    packed_block_slots,
):
    nd, nt, ns, np_ = (lax.axis_size(a) for a in ("dp", "tensor", "sub", "parts"))
    z, t, s, p = (lax.axis_index(a) for a in ("dp", "tensor", "sub", "parts"))
    blocks, halved, width = tokens.shape[1:]
    heads = cotangent.shape[3]
    jobs_dev, rank, _ = adapter_down.shape
    columns = frozen_value_weight.shape[1]
    zz = Sizes(nd, nt, ns, np_, blocks, halved, width, heads, jobs_dev, rank, columns)
    rows, r2, m, cap = zz.rows, rank // ns, zz.per_head, zz.cap
    own_tokens = tokens.reshape(rows, width)
    own_grad = cotangent.reshape(rows, heads)

    quarters = jnp.stack([(p - a) % np_ * ns + (s - b) % ns for a in range(np_) for b in range(ns)]).astype(i32)
    moving = lax.dynamic_slice_in_dim(frozen_value_weight, (p * ns + s) * zz.fq, zz.fq, axis=0)
    rounds = [None, shifted(moving, "dp", nd, 1)]

    maps = jnp.concatenate([adapter_down, adapter_up], axis=2).reshape(jobs_dev, ns, r2, width + heads)
    maps = lax.dynamic_index_in_dim(maps, s, 1, keepdims=False)
    maps, rounds[1] = tie(gather_shifts(maps, "dp", nd), rounds[1])
    maps = jnp.concatenate(maps, axis=0).reshape(zz.jobs * r2, -1)
    maps = jnp.concatenate(gather_shifts(maps, "sub", ns), axis=0)
    grads = gather_shifts(own_grad, "tensor", nt)

    positions = jnp.arange(blocks, dtype=i32)
    dest = packed_block_slots // blocks
    same = dest[:, :, None] == dest[:, None, :]
    earlier = positions[None, None, :] < positions[None, :, None]
    send_rank = jnp.sum((same & earlier).astype(i32), axis=2, dtype=i32)
    flat_slots = packed_block_slots.reshape(-1)
    flat_ids = jnp.arange(nd * blocks, dtype=i32)
    slot_owner = flat_slots[None, :] == (z * blocks + positions)[:, None]
    block_ids = jnp.sum(jnp.where(slot_owner, flat_ids[None, :], 0), axis=1, dtype=i32)
    in_rank = jnp.sum(jnp.where(slot_owner, send_rank.reshape(-1)[None, :], 0), axis=1, dtype=i32)
    in_slot = (z - block_ids // blocks) % nd * cap + in_rank
    own_dest = lax.dynamic_index_in_dim(dest, z, 0, keepdims=False)
    own_rank = lax.dynamic_index_in_dim(send_rank, z, 0, keepdims=False)
    out_slot = (own_dest - z) % nd * cap + own_rank
    slot_range = jnp.arange(zz.slots, dtype=i32)

    def positions_of(slots):
        match = slots[None, :] == slot_range[:, None]
        return jnp.sum(jnp.where(match, positions[None, :], 0), axis=1, dtype=i32), jnp.any(match, axis=1)

    out_pos, out_fill = positions_of(out_slot)
    in_pos, in_fill = positions_of(in_slot)

    def facts(ids):
        job, valid = block_facts(tokens_per_job, ids, halved * ns)
        return (z - job // jobs_dev) % nd * jobs_dev + job % jobs_dev, valid - s * halved

    out_rel, out_valid = facts(z * blocks + positions)
    in_rel, in_valid = facts(block_ids)

    def arrival(index):
        found = (z - index * m - jnp.arange(m, dtype=i32)) % nd
        place_of = jnp.sum((found[None, :] < found[:, None]).astype(i32), axis=1)
        match = place_of[None, :] == jnp.arange(m, dtype=i32)[:, None]
        return jnp.sum(jnp.where(match, found[None, :], 0), axis=1, dtype=i32)

    shard_of = (z - jnp.arange(nd, dtype=i32)) % nd
    shard_at = (t - shard_of // m) % nt * m + shard_of % m
    arrivals = [arrival((t + g) % nt) for g in range(nt)]
    head_at = (z - arrivals[0]) % nd - t * m
    steps = (quarters[None, :] * zz.chunks + jnp.arange(zz.chunks, dtype=i32)[:, None]).reshape(-1)
    sc = jnp.concatenate(
        [
            x.astype(i32)
            for x in (out_pos, in_pos, out_fill, in_fill, out_rel, in_rel, out_valid, in_valid, quarters, shard_at, head_at, steps, *arrivals)
        ]
    )
    column = jnp.arange(zz.wide, dtype=i32)
    job_of = (column // r2 % zz.jobs)[None, :]
    rank_of = column // (zz.jobs * r2) * r2 + column % r2
    unfold = (jnp.arange(rank, dtype=i32)[:, None] == rank_of[None, :]).astype(bf16)
    fold = unfold.astype(f32).T

    def spread_round(over_parts):
        return [x for y in over_parts for x in gather_shifts(y, "sub", ns)]

    last = nd - 1
    over = [None] * nd
    over[1] = gather_shifts(rounds[1], "parts", np_)
    for d in range(2, last):
        rounds.append(shifted(rounds[-1], "dp", nd, 1))
    part = products(zz, sc, own_tokens, own_grad, maps, fold, job_of)
    parts = gather_shifts(part, "tensor", nt)
    late_tokens, _ = tie(own_tokens, part)
    base = [base_product(zz, sc, late_tokens, [frozen_value_weight] * zz.nq, 0, None)[0]]
    base[0], parts = tie(base[0], parts)
    sums, *pays = sums_of(zz, sc, parts)

    got = [shifted(pays[d], "dp", nd, d) for d in range(nd)]
    rounds[last - 1], over[1], got, grads = tie(rounds[last - 1], over[1], got, grads)
    ends = [
        shifted(rounds[last - 1][c * zz.fe : (c + 1) * zz.fe], "dp", nd, 1) for c in range(zz.chunks)
    ]
    mine, theirs = tables_of(zz, sc, own_tokens, own_grad, unfold, job_of, got)
    for d in range(2, last):
        over[d] = gather_shifts(rounds[d], "parts", np_)
    mine, theirs, ends[0] = tie(mine, theirs, ends[0])
    end_over = [gather_shifts(ends[0], "parts", np_)]
    theirs = shifted(theirs, "sub", ns, 1)
    piece_list = [[frozen_value_weight] * zz.nq, spread_round(over[1])]
    late_tokens, mine = tie(own_tokens, mine)
    base.append(base_product(zz, sc, late_tokens, piece_list[1], 1, base)[0])
    base[1], ends[1:], over[2:last] = tie(base[1], ends[1:], over[2:last])
    end_over += [gather_shifts(x, "parts", np_) for x in ends[1:]]
    piece_list += [spread_round(over[d]) for d in range(2, last)]
    end_over[0], *piece_list[2:] = tie(end_over[0], *piece_list[2:])

    slots = []

    def finish(d, made):
        base.append(made[0])
        if len(made) > 1:
            slots.append([made[1]] + [shifted(made[1 + g], "tensor", nt, g) for g in range(1, nt)])

    for d in range(2, last):
        finish(d, base_product(zz, sc, own_tokens, piece_list[d], d, base))
    base[-1], mine, theirs = tie(base[-1], mine, theirs)

    summed = (mine + theirs).reshape(nd, jobs_dev * r2, -1)
    sending = [summed[d].astype(bf16) for d in range(nd)]
    tables = [sending[0]] + [shifted(sending[d], "dp", nd, -d) for d in range(1, nd)]
    ahead, behind = [x for y in end_over[:-1] for x in spread_round(y)], end_over[-1]
    ahead += gather_shifts(behind[0], "sub", ns)
    begun = base_product(zz, sc, own_tokens, ahead, last, base, 0, None, True)[0]
    begun, behind, slots = tie(begun, behind, slots)
    tail = spread_round(behind[1:])
    piece_list.append(ahead + tail)
    finish(last, base_product(zz, sc, own_tokens, tail, last, base, len(ahead), begun))
    base[-1], tables, grads = tie(base[-1], tables, grads)
    total = sum(x.astype(f32) for x in tables)
    counts = lax.dynamic_slice_in_dim(tokens_per_job, z * jobs_dev, jobs_dev).astype(f32)
    total = total.reshape(jobs_dev, r2, -1) * (adapter_scale / counts)[:, None, None]
    halves = gather_shifts(total, "sub", ns)
    half = zz.nq // 2
    gradient = token_gradient_of(zz, sc, grads, maps, sums, unfold, job_of, piece_list, list(range(half)), None)
    given = [slots[j][d] for d in range(nt) for j in range(m)]
    gradient, halves, *given = tie(gradient, halves, *given)
    layer = layer_of(zz, sc, sums, maps, unfold, job_of, given)
    *layer, gradient = tie(*layer, gradient)
    owned = jnp.concatenate(
        [sum(jnp.where((s - h) % ns == k, x, 0.0) for k, x in enumerate(halves)) for h in range(ns)], axis=1
    )
    grad_down, grad_up = owned[:, :, :width], owned[:, :, width:]
    landed = [shifted(layer[d], "dp", nd, d) for d in range(nd)]
    gradient = token_gradient_of(
        zz, sc, grads, maps, sums, unfold, job_of, piece_list, list(range(half, zz.nq)), gradient
    )
    gradient, grad_down, grad_up, *landed = tie(gradient, grad_down, grad_up, *landed)
    layer_output = place(zz, sc, landed)
    return (
        layer_output.reshape(1, blocks, halved, heads),
        gradient.reshape(1, blocks, halved, width),
        grad_down,
        grad_up,
    )


def solution(mesh):
    return jax.shard_map(
        body,
        mesh=mesh,
        in_specs=(
            P(("parts", "dp"), None, "sub", "tensor"),
            P(("parts", "dp"), None, "sub", "tensor"),
            P("tensor", "dp"),
            P(("parts", "dp"), None, "tensor"),
            P(("parts", "dp"), None, "tensor"),
            P("parts"),
            P("parts", None),
        ),
        out_specs=(
            P(("parts", "dp"), None, "sub", "tensor"),
            P(("parts", "dp"), None, "sub", "tensor"),
            P(("parts", "dp"), None, "tensor"),
            P(("parts", "dp"), None, "tensor"),
        ),
        check_vma=False,
    )
```

```python
import functools

import jax
import jax.numpy as jnp
from jax import lax
from jax.experimental import pallas as pl
from jax.experimental.pallas import tpu as pltpu
from jax.sharding import PartitionSpec as P

adapter_scale = 2.0
f32, bf16, i32 = jnp.float32, jnp.bfloat16, jnp.int32
MIB = 1 << 20
TOKEN_LIMIT = 16 * MIB


def block_facts(tokens_per_job, block_ids, block_rows):
    job_total = tokens_per_job.shape[0]
    blocks = (tokens_per_job + (block_rows - 1)) // block_rows
    block_ends = jnp.cumsum(blocks, dtype=jnp.int32)
    starts = block_ends - blocks
    job_index = jnp.sum(
        (block_ends[None, :] <= block_ids[:, None]).astype(jnp.int32), axis=1, dtype=jnp.int32
    )
    chosen = job_index[:, None] == jnp.arange(job_total, dtype=jnp.int32)[None, :]
    job_count = jnp.sum(jnp.where(chosen, tokens_per_job[None, :], 0), axis=1, dtype=jnp.int32)
    first_block = jnp.sum(jnp.where(chosen, starts[None, :], 0), axis=1, dtype=jnp.int32)
    valid_rows = jnp.clip(job_count - block_rows * (block_ids - first_block), 0, block_rows)
    return job_index, valid_rows


def shifted(values, axis, count, step):
    if step % count == 0:
        return values
    return lax.ppermute(values, axis, [(i, (i + step) % count) for i in range(count)])


def gather_shifts(values, axis, count):
    return [shifted(values, axis, count, d) for d in range(count)]


def dot(a, b, dims, precision=None):
    return lax.dot_general(a, b, (dims, ((), ())), precision=precision, preferred_element_type=f32)


def tie(*values):
    return lax.optimization_barrier(values)


class Sizes:
    def __init__(self, nd, nt, ns, np_, blocks, halved, width, heads, jobs_dev, rank, columns):
        self.nd, self.nt, self.ns, self.np_ = nd, nt, ns, np_
        self.blocks, self.halved, self.width, self.heads = blocks, halved, width, heads
        self.jobs, self.jobs_dev, self.rank, self.columns = nd * jobs_dev, jobs_dev, rank, columns
        self.wide = self.jobs * rank
        self.rows = blocks * halved
        self.cap = -(-blocks // nd)
        self.slots = nd * self.cap
        self.nq = np_ * ns
        self.fq = width // self.nq
        self.per_head = nd // nt
        at, self.at = 0, {}
        for name, count in (
            ("out_pos", self.slots), ("in_pos", self.slots), ("out_fill", self.slots), ("in_fill", self.slots),
            ("out_rel", blocks), ("in_rel", blocks), ("out_valid", blocks), ("in_valid", blocks),
            ("quarter", self.nq), ("shard", nd), ("head", self.per_head),
            ("pick", self.per_head * nt),
        ):
            self.at[name] = at
            at += count

    def get(self, ref, name, index):
        return ref[self.at[name] + index]


def call(kernel, name, grid, scalars, inputs, in_specs, out_shape, out_specs, flops, moved, limit, scratch=(), alias=None):
    return pl.pallas_call(
        kernel,
        out_shape=out_shape,
        grid_spec=pltpu.PrefetchScalarGridSpec(
            num_scalar_prefetch=1, grid=grid, in_specs=in_specs, out_specs=out_specs, scratch_shapes=list(scratch)
        ),
        input_output_aliases=alias or {},
        compiler_params=pltpu.CompilerParams(vmem_limit_bytes=limit),
        cost_estimate=pl.CostEstimate(flops=1000, bytes_accessed=1000, transcendentals=0),
        name=name,
    )(scalars, *inputs)


ANY = pl.BlockSpec(memory_space=pl.ANY)


def whole(x):
    return pl.BlockSpec(x.shape, lambda *_: (0,) * len(x.shape))


def rows_of(index, z):
    return pl.ds(pl.multiple_of(index * z.halved, z.halved), z.halved)


def row_mask(valid, z, lanes):
    return lax.broadcasted_iota(i32, (z.halved, lanes), 0) < valid


def widen(values, rel, unfold, job_of, z):
    wide = dot(values, unfold, ((1,), (0,)))
    return jnp.where(job_of == rel, wide, 0.0).astype(bf16)


def keep_kernel(parts, sc, tokens, out, sems):
    size = tokens.shape[0] // parts
    copies = [
        pltpu.make_async_copy(tokens.at[pl.ds(k * size, size), :], out.at[pl.ds(k * size, size), :], sems.at[k])
        for k in range(parts)
    ]
    for copy in copies:
        copy.start()
    for copy in copies:
        copy.wait()


def keep(z, sc, tokens):
    parts = 4
    return call(
        functools.partial(keep_kernel, parts), "keep_tokens", (1,), sc, (tokens,), [ANY],
        jax.ShapeDtypeStruct(tokens.shape, tokens.dtype), ANY, 1000, 1000, 8 * MIB,
        scratch=(pltpu.SemaphoreType.DMA((parts,)),),
    )


def products_kernel(z, n, sc, tokens, grad, maps, fold, job_of, out, held, sems):
    many = z.blocks // n
    copies = [
        pltpu.make_async_copy(tokens.at[pl.ds(k * n * z.halved, n * z.halved), :], held.at[k], sems.at[k])
        for k in range(many)
    ]
    for copy in copies:
        copy.start()
    back = dot(grad[...], maps[:, z.width :], ((1,), (1,)))
    for block in range(z.blocks):
        own = slice(block * z.halved, (block + 1) * z.halved)
        picked = jnp.where(job_of[...] == z.get(sc, "in_rel", block), back[own], 0.0)
        picked = jnp.where(row_mask(z.get(sc, "in_valid", block), z, z.wide), picked, 0.0)
        out[own, z.rank :] = dot(picked, fold[...], ((1,), (0,)), lax.Precision.HIGHEST).astype(bf16)
    for k in range(many):
        copies[k].wait()
        down = dot(held[k], maps[:, : z.width], ((1,), (1,)))
        for r in range(n):
            block = k * n + r
            own = slice(block * z.halved, (block + 1) * z.halved)
            mine = slice(r * z.halved, (r + 1) * z.halved)
            picked = jnp.where(job_of[...] == z.get(sc, "out_rel", block), down[mine], 0.0)
            out[own, : z.rank] = dot(picked, fold[...], ((1,), (0,)), lax.Precision.HIGHEST).astype(bf16)


def products(z, sc, tokens, grad, maps, fold, job_of):
    n = 2
    shape = jax.ShapeDtypeStruct((z.rows, 2 * z.rank), bf16)
    return call(
        functools.partial(products_kernel, z, n), "adapter_products", (1,), sc,
        (tokens, grad, maps, fold, job_of),
        [ANY, whole(grad), whole(maps), whole(fold), whole(job_of)],
        shape, whole(shape), 1000, 1000, TOKEN_LIMIT,
        scratch=(
            pltpu.VMEM((z.blocks // n, n * z.halved, z.width), bf16),
            pltpu.SemaphoreType.DMA((z.blocks // n,)),
        ),
    )


def sums_kernel(z, sc, *refs):
    parts, outs = refs[: z.nt], refs[z.nt :]
    sums, pays = outs[0], outs[1:]
    total = parts[0][...].astype(f32)
    for part in parts[1:]:
        total = total + part[...].astype(f32)
    sums[...] = total.astype(bf16)
    for d in range(z.nd):
        back = (z.nd - d) % z.nd
        for r in range(z.cap):
            own = slice(r * z.halved, (r + 1) * z.halved)
            picked = sums[rows_of(z.get(sc, "out_pos", d * z.cap + r), z), : z.rank]
            pays[d][own, : z.rank] = jnp.where(z.get(sc, "out_fill", d * z.cap + r) > 0, picked, 0)
            picked = sums[rows_of(z.get(sc, "in_pos", back * z.cap + r), z), z.rank :]
            pays[d][own, z.rank :] = jnp.where(z.get(sc, "in_fill", back * z.cap + r) > 0, picked, 0)


def sums_of(z, sc, parts):
    shapes = [jax.ShapeDtypeStruct((z.rows, 2 * z.rank), bf16)]
    shapes += [jax.ShapeDtypeStruct((z.cap * z.halved, 2 * z.rank), bf16)] * z.nd
    return call(
        functools.partial(sums_kernel, z), "adapter_sums", (1,), sc, parts, [whole(x) for x in parts],
        tuple(shapes), tuple(whole(x) for x in shapes), 1000, 8 * z.rows * z.rank, 8 * MIB,
    )


def table_kernel(z, tiles, sc, tokens, grad, unfold, job_of, *refs):
    got, (mine, theirs, back, down, back_t, down_t, held, sems) = refs[: z.nd], refs[z.nd :]
    half = mine.shape[0]
    part = z.width // tiles
    copies = [
        pltpu.make_async_copy(tokens.at[:, pl.ds(k * part, part)], held.at[k], sems.at[k]) for k in range(tiles)
    ]
    for copy in copies:
        copy.start()
    for d in range(z.nd):
        for r in range(z.cap):
            slot = d * z.cap + r
            own = slice(r * z.halved, (r + 1) * z.halved)

            @pl.when(z.get(sc, "out_fill", slot) > 0)
            def _():
                at = z.get(sc, "out_pos", slot)
                values = got[(z.nd - d) % z.nd][own, z.rank :]
                back[rows_of(at, z), :] = widen(values, z.get(sc, "out_rel", at), unfold[...], job_of[...], z)

            @pl.when(z.get(sc, "in_fill", slot) > 0)
            def _():
                at = z.get(sc, "in_pos", slot)
                values = widen(got[d][own, : z.rank], z.get(sc, "in_rel", at), unfold[...], job_of[...], z)
                mask = row_mask(z.get(sc, "in_valid", at), z, z.wide)
                down[rows_of(at, z), :] = jnp.where(mask, values, 0).astype(bf16)

    same = lax.broadcasted_iota(i32, (z.rows, z.rows), 0) == lax.broadcasted_iota(i32, (z.rows, z.rows), 1)
    unit = jnp.where(same, 1.0, 0.0).astype(bf16)
    back_t[...] = dot(back[...], unit, ((0,), (0,))).astype(bf16)
    down_t[...] = dot(down[...], unit, ((0,), (0,))).astype(bf16)
    total = dot(down_t[...], grad[...], ((1,), (0,)))
    mine[:, z.width :] = total[:half]
    theirs[:, z.width :] = total[half:].astype(bf16)
    for k in range(tiles):
        copies[k].wait()
        total = dot(back_t[...], held[k], ((1,), (0,)))
        mine[:, k * part : (k + 1) * part] = total[:half]
        theirs[:, k * part : (k + 1) * part] = total[half:].astype(bf16)


def tables_of(z, sc, tokens, grad, unfold, job_of, got):
    tiles = 4
    shape = jax.ShapeDtypeStruct((z.wide // z.ns, z.width + z.heads), f32)
    sent = jax.ShapeDtypeStruct(shape.shape, bf16)
    return call(
        functools.partial(table_kernel, z, tiles), "job_tables", (1,), sc,
        (tokens, grad, unfold, job_of, *got),
        [ANY, whole(grad), whole(unfold), whole(job_of)] + [whole(x) for x in got],
        (shape, sent), (whole(shape), whole(sent)), 1000, 1000, TOKEN_LIMIT,
        scratch=(pltpu.VMEM((z.rows, z.wide), bf16),) * 2
        + (pltpu.VMEM((z.wide, z.rows), bf16),) * 2
        + (pltpu.VMEM((tiles, z.rows, z.width // tiles), bf16), pltpu.SemaphoreType.DMA((tiles,))),
    )


def base_kernel(z, d, count, started, partial, slot, others, at, features, sc, tokens, *refs):
    pieces, refs = refs[:count], refs[count:]
    if started:
        begun, refs = refs[0], refs[1:]
    earlier, refs = refs[: len(others)], refs[len(others) :]
    outs, (held, parts, sems) = refs[:-3], refs[-3:]
    copies = []
    for k in range(count):
        start = pl.multiple_of(sc[at + k] * features, features)
        copies.append(pltpu.make_async_copy(tokens.at[:, pl.ds(start, features)], held.at[k], sems.at[0, k]))
        source = pieces[k].at[pl.ds(start, features), :] if d == 0 else pieces[k]
        copies.append(pltpu.make_async_copy(source, parts.at[k], sems.at[1, k]))
    for copy in copies:
        copy.start()
    total = begun[...] if started else None
    for k in range(count):
        copies[2 * k].wait()
        copies[2 * k + 1].wait()
        part = dot(held[k], parts[k], ((1,), (0,)))
        total = part if total is None else total + part
    if partial:
        outs[0][...] = total
        return
    done = total.astype(bf16)
    outs[0][...] = done
    for g in range(len(outs) - 1):
        outs[1 + g][...] = done
        for where, values in zip(others, earlier):

            @pl.when(z.get(sc, "pick", g * z.per_head + slot) == where)
            def _():
                outs[1 + g][...] = values[...]


def base_product(z, sc, tokens, pieces, d, base, first=0, begun=None, partial=False):
    count, features = len(pieces), z.fq
    at = z.at["quarter"] + first
    inputs, specs = [tokens, *pieces], [ANY] * (1 + count)
    if begun is not None:
        inputs.append(begun)
        specs.append(whole(begun))
    slot = d - (z.nd - z.per_head)
    others = []
    shapes = [jax.ShapeDtypeStruct((z.rows, z.columns), f32 if partial else bf16)]
    if slot >= 0 and not partial:
        others = list(range(slot, d))
        inputs += [base[k] for k in others]
        specs += [whole(base[k]) for k in others]
        shapes += [jax.ShapeDtypeStruct((z.rows, z.columns), bf16)] * z.nt
    return call(
        functools.partial(base_kernel, z, d, count, begun is not None, partial, slot, others, at, features),
        "base_%d_%d" % (d, first), (1,), sc, inputs, specs,
        tuple(shapes), tuple(whole(x) for x in shapes),
        1000, 1000, TOKEN_LIMIT,
        scratch=(
            pltpu.VMEM((count, z.rows, features), bf16),
            pltpu.VMEM((count, features, z.columns), bf16),
            pltpu.SemaphoreType.DMA((2, count)),
        ),
    )


def layer_kernel(z, sc, sums, maps, unfold, job_of, *refs):
    m = z.per_head
    given, (outs, frozen) = refs[: m * z.nt], (refs[m * z.nt : -1], refs[-1])
    for j in range(m):
        total = given[j][...].astype(f32)
        for d in range(1, z.nt):
            total = total + given[d * m + j][...].astype(f32)
        for i in range(m):

            @pl.when(z.get(sc, "head", j) == i)
            def _():
                frozen[:, i * z.columns : (i + 1) * z.columns] = total

    for d in range(z.nd):
        for r in range(z.cap):
            slot = d * z.cap + r
            at = z.get(sc, "out_pos", slot)
            valid = jnp.where(z.get(sc, "out_fill", slot) > 0, z.get(sc, "out_valid", at), 0)
            wide = widen(sums[rows_of(at, z), : z.rank], z.get(sc, "out_rel", at), unfold[...], job_of[...], z)
            adapter = dot(wide, maps[...], ((1,), (0,)))
            layer = frozen[rows_of(at, z), :] + adapter_scale * adapter
            layer = jnp.where(row_mask(valid, z, z.heads), layer, 0.0)
            outs[d][r * z.halved : (r + 1) * z.halved, :] = layer.astype(bf16)


def layer_of(z, sc, sums, maps, unfold, job_of, given):
    shapes = [jax.ShapeDtypeStruct((z.cap * z.halved, z.heads), bf16)] * z.nd
    at = z.width // z.heads
    return call(
        functools.partial(layer_kernel, z), "layer", (1,), sc, (sums, maps, unfold, job_of, *given),
        [whole(sums), pl.BlockSpec((z.wide, z.heads), lambda i, _: (0, at)), whole(unfold), whole(job_of)]
        + [whole(x) for x in given],
        tuple(shapes), tuple(whole(x) for x in shapes),
        2 * z.rows * z.wide * z.heads, 6 * z.rows * z.heads, 16 * MIB,
        scratch=(pltpu.VMEM((z.rows, z.heads), f32),),
    )


def place_kernel(z, sc, *refs):
    got, out = refs[: z.nd], refs[z.nd]
    for d in range(z.nd):
        for r in range(z.cap):
            slot = d * z.cap + r

            @pl.when(z.get(sc, "in_fill", slot) > 0)
            def _():
                out[rows_of(z.get(sc, "in_pos", slot), z), :] = got[d][r * z.halved : (r + 1) * z.halved, :]


def place(z, sc, got):
    shape = jax.ShapeDtypeStruct((z.rows, z.heads), bf16)
    return call(
        functools.partial(place_kernel, z), "place", (1,), sc, got, [whole(x) for x in got],
        shape, whole(shape), 1000, 4 * z.rows * z.heads, 8 * MIB,
    )


def gradient_kernel(z, count, per, aliased, sc, maps, sums, unfold, job_of, *refs):
    grads, refs = refs[: z.nt], refs[z.nt :]
    pieces, refs = refs[: z.nd * count], refs[z.nd * count :]
    out, grad, back = refs[1:] if aliased else refs
    step = pl.program_id(0)
    m = z.per_head

    @pl.when(step == 0)
    def _():
        for v in range(z.nt * m):
            grad[v] = grads[v // m][:, v % m * z.columns : (v % m + 1) * z.columns]
        for b in range(z.blocks):
            own = slice(b * z.halved, (b + 1) * z.halved)
            back[own, :] = widen(sums[own, z.rank :], z.get(sc, "in_rel", b), unfold[...], job_of[...], z)

    for k in range(count):

        @pl.when(step // per == k)
        def _():
            total = adapter_scale * dot(back[...], maps[...], ((1,), (0,)))
            for d in range(z.nd):
                total = total + dot(grad[z.get(sc, "shard", d)], pieces[d * count + k][...], ((1,), (1,)))
            for b in range(z.blocks):
                own = slice(b * z.halved, (b + 1) * z.halved)
                mask = row_mask(z.get(sc, "in_valid", b), z, total.shape[1])
                out[own, :] = jnp.where(mask, total[own], 0.0).astype(bf16)


def token_gradient_of(z, sc, grads, maps, sums, unfold, job_of, piece_list, quarters, before):
    tile = min(512, z.fq)
    per = z.fq // tile
    at = z.at["quarter"]
    first, count = quarters[0], len(quarters)
    block = lambda i, q: (0, q[at + first + i // per] * per + i % per)
    specs, flat = [], []
    for d in range(z.nd):
        for k, r in enumerate(quarters):
            inner = lambda i, k=k: jnp.clip(i - k * per, 0, per - 1)
            if d == 0:
                index = lambda i, q, r=r, inner=inner: (q[at + r] * per + inner(i), 0)
            else:
                index = lambda i, q, inner=inner: (inner(i), 0)
            specs.append(pl.BlockSpec((tile, z.columns), index))
            flat.append(piece_list[d][r])
    inputs = [maps, sums, unfold, job_of, *grads, *flat]
    in_specs = [pl.BlockSpec((z.wide, tile), block), whole(sums), whole(unfold), whole(job_of)]
    in_specs += [whole(x) for x in grads] + specs
    alias = None
    if before is not None:
        alias = {1 + len(inputs): 0}
        inputs.append(before)
        in_specs.append(pl.BlockSpec(memory_space=pl.ANY))
    return call(
        functools.partial(gradient_kernel, z, count, per, before is not None),
        "token_gradient_%d" % first, (count * per,), sc, inputs, in_specs,
        jax.ShapeDtypeStruct((z.rows, z.width), bf16), pl.BlockSpec((z.rows, tile), block),
        1000, 1000, 32 * MIB,
        scratch=(pltpu.VMEM((z.nd, z.rows, z.columns), bf16), pltpu.VMEM((z.rows, z.wide), bf16)),
        alias=alias,
    )


def body(
    tokens,
    cotangent,
    frozen_value_weight,
    adapter_down,
    adapter_up,
    tokens_per_job,
    packed_block_slots,
):
    nd, nt, ns, np_ = (lax.axis_size(a) for a in ("dp", "tensor", "sub", "parts"))
    z, t, s, p = (lax.axis_index(a) for a in ("dp", "tensor", "sub", "parts"))
    blocks, halved, width = tokens.shape[1:]
    heads = cotangent.shape[3]
    jobs_dev, rank, _ = adapter_down.shape
    columns = frozen_value_weight.shape[1]
    zz = Sizes(nd, nt, ns, np_, blocks, halved, width, heads, jobs_dev, rank, columns)
    rows, r2, m, cap = zz.rows, rank // ns, zz.per_head, zz.cap
    own_tokens = tokens.reshape(rows, width)
    own_grad = cotangent.reshape(rows, heads)

    own_tokens = keep(zz, jnp.zeros((1,), i32), own_tokens)
    quarters = jnp.stack([(p - a) % np_ * ns + (s - b) % ns for a in range(np_) for b in range(ns)]).astype(i32)
    moving = lax.dynamic_slice_in_dim(frozen_value_weight, (p * ns + s) * zz.fq, zz.fq, axis=0)

    maps = jnp.concatenate([adapter_down, adapter_up], axis=2).reshape(jobs_dev, ns, r2, width + heads)
    maps = lax.dynamic_index_in_dim(maps, s, 1, keepdims=False)
    maps, moving = tie(maps, moving)
    rounds = [None, shifted(moving, "dp", nd, 1)]
    maps, rounds[1] = tie(gather_shifts(maps, "dp", nd), rounds[1])
    maps = jnp.concatenate(maps, axis=0).reshape(zz.jobs * r2, -1)
    maps = jnp.concatenate(gather_shifts(maps, "sub", ns), axis=0)
    grads = gather_shifts(own_grad, "tensor", nt)

    positions = jnp.arange(blocks, dtype=i32)
    dest = packed_block_slots // blocks
    same = dest[:, :, None] == dest[:, None, :]
    earlier = positions[None, None, :] < positions[None, :, None]
    send_rank = jnp.sum((same & earlier).astype(i32), axis=2, dtype=i32)
    flat_slots = packed_block_slots.reshape(-1)
    flat_ids = jnp.arange(nd * blocks, dtype=i32)
    slot_owner = flat_slots[None, :] == (z * blocks + positions)[:, None]
    block_ids = jnp.sum(jnp.where(slot_owner, flat_ids[None, :], 0), axis=1, dtype=i32)
    in_rank = jnp.sum(jnp.where(slot_owner, send_rank.reshape(-1)[None, :], 0), axis=1, dtype=i32)
    in_slot = (z - block_ids // blocks) % nd * cap + in_rank
    own_dest = lax.dynamic_index_in_dim(dest, z, 0, keepdims=False)
    own_rank = lax.dynamic_index_in_dim(send_rank, z, 0, keepdims=False)
    out_slot = (own_dest - z) % nd * cap + own_rank
    slot_range = jnp.arange(zz.slots, dtype=i32)

    def positions_of(slots):
        match = slots[None, :] == slot_range[:, None]
        return jnp.sum(jnp.where(match, positions[None, :], 0), axis=1, dtype=i32), jnp.any(match, axis=1)

    out_pos, out_fill = positions_of(out_slot)
    in_pos, in_fill = positions_of(in_slot)

    def facts(ids):
        job, valid = block_facts(tokens_per_job, ids, halved * ns)
        return (z - job // jobs_dev) % nd * jobs_dev + job % jobs_dev, valid - s * halved

    out_rel, out_valid = facts(z * blocks + positions)
    in_rel, in_valid = facts(block_ids)

    def arrival(index):
        found = (z - index * m - jnp.arange(m, dtype=i32)) % nd
        place_of = jnp.sum((found[None, :] < found[:, None]).astype(i32), axis=1)
        match = place_of[None, :] == jnp.arange(m, dtype=i32)[:, None]
        return jnp.sum(jnp.where(match, found[None, :], 0), axis=1, dtype=i32)

    shard_of = (z - jnp.arange(nd, dtype=i32)) % nd
    shard_at = (t - shard_of // m) % nt * m + shard_of % m
    arrivals = [arrival((t + g) % nt) for g in range(nt)]
    head_at = (z - arrivals[0]) % nd - t * m
    sc = jnp.concatenate(
        [
            x.astype(i32)
            for x in (out_pos, in_pos, out_fill, in_fill, out_rel, in_rel, out_valid, in_valid, quarters, shard_at, head_at, *arrivals)
        ]
    )
    column = jnp.arange(zz.wide, dtype=i32)
    job_of = (column // r2 % zz.jobs)[None, :]
    rank_of = column // (zz.jobs * r2) * r2 + column % r2
    unfold = (jnp.arange(rank, dtype=i32)[:, None] == rank_of[None, :]).astype(bf16)
    fold = unfold.astype(f32).T

    def spread_round(over_parts):
        return [x for y in over_parts for x in gather_shifts(y, "sub", ns)]

    last = nd - 1
    over = [None] * nd
    over[1] = gather_shifts(rounds[1], "parts", np_)
    for d in range(2, last):
        rounds.append(shifted(rounds[-1], "dp", nd, 1))
    swapped = gather_shifts(over[1][0], "sub", ns)
    maps, swapped = tie(maps, swapped)
    part = products(zz, sc, own_tokens, own_grad, maps, fold, job_of)
    parts = gather_shifts(part, "tensor", nt)
    late_tokens, _ = tie(own_tokens, part)
    base = [base_product(zz, sc, late_tokens, [frozen_value_weight] * zz.nq, 0, None)[0]]
    base[0], parts, grads = tie(base[0], parts, grads)
    sums, *pays = sums_of(zz, sc, parts)
    rounds[last - 1], over[1], sums = tie(rounds[last - 1], over[1], sums)

    end = shifted(rounds[last - 1], "dp", nd, 1)
    for d in range(2, last):
        over[d] = gather_shifts(rounds[d], "parts", np_)
    piece_list = [[frozen_value_weight] * zz.nq, swapped + spread_round(over[1][1:])]
    crossed = [gather_shifts(over[d][0], "sub", ns) for d in range(2, last)]
    piece_list[1], crossed = tie(piece_list[1], crossed)
    base.append(base_product(zz, sc, own_tokens, piece_list[1], 1, base)[0])
    base[1], end, over[2:last], pays = tie(base[1], end, over[2:last], pays)

    behind = gather_shifts(end, "parts", np_)
    got = [shifted(pays[d], "dp", nd, d) for d in range(nd)]
    piece_list += [crossed[d - 2] + spread_round(over[d][1:]) for d in range(2, last)]

    slots = []

    def finish(d, made):
        base.append(made[0])
        if len(made) > 1:
            slots.append([made[1]] + [shifted(made[1 + g], "tensor", nt, g) for g in range(1, nt)])

    for d in range(2, last):
        finish(d, base_product(zz, sc, own_tokens, piece_list[d], d, base))
    base[-1], got = tie(base[-1], got)
    mine, theirs = tables_of(zz, sc, own_tokens, own_grad, unfold, job_of, got)
    theirs = shifted(theirs, "sub", ns, 1)
    ahead = gather_shifts(end, "sub", ns)
    ahead, mine = tie(ahead, mine)
    begun = base_product(zz, sc, own_tokens, ahead, last, base, 0, None, True)[0]
    begun, behind, slots = tie(begun, behind, slots)
    tail = spread_round(behind[1:])
    piece_list.append(ahead + tail)
    finish(last, base_product(zz, sc, own_tokens, tail, last, base, len(ahead), begun))
    base[-1], mine, theirs, grads = tie(base[-1], mine, theirs, grads)

    summed = (mine + theirs).reshape(nd, jobs_dev * r2, -1)
    sending = [summed[d].astype(bf16) for d in range(nd)]
    tables = [sending[0]] + [shifted(sending[d], "dp", nd, -d) for d in range(1, nd)]

    half = zz.nq // 2
    gradient = token_gradient_of(zz, sc, grads, maps, sums, unfold, job_of, piece_list, list(range(half)), None)
    given = [slots[j][d] for d in range(nt) for j in range(m)]
    gradient, given = tie(gradient, given)
    layer = layer_of(zz, sc, sums, maps, unfold, job_of, given)
    layer, gradient, tables = tie(layer, gradient, tables)
    landed = [shifted(layer[d], "dp", nd, d) for d in range(nd)]
    total = sum(x.astype(f32) for x in tables)
    counts = lax.dynamic_slice_in_dim(tokens_per_job, z * jobs_dev, jobs_dev).astype(f32)
    total = total.reshape(jobs_dev, r2, -1) * (adapter_scale / counts)[:, None, None]
    halves = gather_shifts(total, "sub", ns)
    gradient, halves = tie(gradient, halves)
    owned = jnp.concatenate(
        [sum(jnp.where((s - h) % ns == k, x, 0.0) for k, x in enumerate(halves)) for h in range(ns)], axis=1
    )
    grad_down, grad_up = owned[:, :, :width], owned[:, :, width:]
    gradient = token_gradient_of(
        zz, sc, grads, maps, sums, unfold, job_of, piece_list, list(range(half, zz.nq)), gradient
    )
    gradient, grad_down, grad_up, landed = tie(gradient, grad_down, grad_up, landed)
    layer_output = place(zz, sc, landed)
    return (
        layer_output.reshape(1, blocks, halved, heads),
        gradient.reshape(1, blocks, halved, width),
        grad_down,
        grad_up,
    )


def solution(mesh):
    return jax.shard_map(
        body,
        mesh=mesh,
        in_specs=(
            P(("parts", "dp"), None, "sub", "tensor"),
            P(("parts", "dp"), None, "sub", "tensor"),
            P("tensor", "dp"),
            P(("parts", "dp"), None, "tensor"),
            P(("parts", "dp"), None, "tensor"),
            P("parts"),
            P("parts", None),
        ),
        out_specs=(
            P(("parts", "dp"), None, "sub", "tensor"),
            P(("parts", "dp"), None, "sub", "tensor"),
            P(("parts", "dp"), None, "tensor"),
            P(("parts", "dp"), None, "tensor"),
        ),
        check_vma=False,
    )
```

```python
import functools

import jax
import jax.numpy as jnp
from jax import lax
from jax.experimental import pallas as pl
from jax.experimental.pallas import tpu as pltpu
from jax.sharding import PartitionSpec as P

adapter_scale = 2.0
f32, bf16, i32 = jnp.float32, jnp.bfloat16, jnp.int32
MIB = 1 << 20
TOKEN_LIMIT = 16 * MIB


def block_facts(tokens_per_job, block_ids, block_rows):
    job_total = tokens_per_job.shape[0]
    blocks = (tokens_per_job + (block_rows - 1)) // block_rows
    block_ends = jnp.cumsum(blocks, dtype=jnp.int32)
    starts = block_ends - blocks
    job_index = jnp.sum(
        (block_ends[None, :] <= block_ids[:, None]).astype(jnp.int32), axis=1, dtype=jnp.int32
    )
    chosen = job_index[:, None] == jnp.arange(job_total, dtype=jnp.int32)[None, :]
    job_count = jnp.sum(jnp.where(chosen, tokens_per_job[None, :], 0), axis=1, dtype=jnp.int32)
    first_block = jnp.sum(jnp.where(chosen, starts[None, :], 0), axis=1, dtype=jnp.int32)
    valid_rows = jnp.clip(job_count - block_rows * (block_ids - first_block), 0, block_rows)
    return job_index, valid_rows


def shifted(values, axis, count, step):
    if step % count == 0:
        return values
    return lax.ppermute(values, axis, [(i, (i + step) % count) for i in range(count)])


def gather_shifts(values, axis, count):
    return [shifted(values, axis, count, d) for d in range(count)]


def dot(a, b, dims, precision=None):
    return lax.dot_general(a, b, (dims, ((), ())), precision=precision, preferred_element_type=f32)


def tie(*values):
    return lax.optimization_barrier(values)


class Sizes:
    def __init__(self, nd, nt, ns, np_, blocks, halved, width, heads, jobs_dev, rank, columns):
        self.nd, self.nt, self.ns, self.np_ = nd, nt, ns, np_
        self.blocks, self.halved, self.width, self.heads = blocks, halved, width, heads
        self.jobs, self.jobs_dev, self.rank, self.columns = nd * jobs_dev, jobs_dev, rank, columns
        self.wide = self.jobs * rank
        self.rows = blocks * halved
        self.cap = -(-blocks // nd)
        self.slots = nd * self.cap
        self.nq = np_ * ns
        self.fq = width // self.nq
        self.per_head = nd // nt
        at, self.at = 0, {}
        for name, count in (
            ("out_pos", self.slots), ("in_pos", self.slots), ("out_fill", self.slots), ("in_fill", self.slots),
            ("out_rel", blocks), ("in_rel", blocks), ("out_valid", blocks), ("in_valid", blocks),
            ("quarter", self.nq), ("shard", nd), ("head", self.per_head),
            ("pick", self.per_head * nt),
        ):
            self.at[name] = at
            at += count

    def get(self, ref, name, index):
        return ref[self.at[name] + index]


def call(kernel, name, grid, scalars, inputs, in_specs, out_shape, out_specs, flops, moved, limit, scratch=(), alias=None):
    return pl.pallas_call(
        kernel,
        out_shape=out_shape,
        grid_spec=pltpu.PrefetchScalarGridSpec(
            num_scalar_prefetch=1, grid=grid, in_specs=in_specs, out_specs=out_specs, scratch_shapes=list(scratch)
        ),
        input_output_aliases=alias or {},
        compiler_params=pltpu.CompilerParams(vmem_limit_bytes=limit),
        cost_estimate=pl.CostEstimate(flops=1000, bytes_accessed=1000, transcendentals=0),
        name=name,
    )(scalars, *inputs)


ANY = pl.BlockSpec(memory_space=pl.ANY)


def whole(x):
    return pl.BlockSpec(x.shape, lambda *_: (0,) * len(x.shape))


def rows_of(index, z):
    return pl.ds(pl.multiple_of(index * z.halved, z.halved), z.halved)


def row_mask(valid, z, lanes):
    return lax.broadcasted_iota(i32, (z.halved, lanes), 0) < valid


def widen(values, rel, unfold, job_of, z):
    wide = dot(values, unfold, ((1,), (0,)))
    return jnp.where(job_of == rel, wide, 0.0).astype(bf16)


def products_kernel(z, n, sc, tokens, grad, maps, fold, job_of, out, held, sems):
    many = z.blocks // n
    copies = [
        pltpu.make_async_copy(tokens.at[pl.ds(k * n * z.halved, n * z.halved), :], held.at[k], sems.at[k])
        for k in range(many)
    ]
    for copy in copies:
        copy.start()
    back = dot(grad[...], maps[:, z.width :], ((1,), (1,)))
    for block in range(z.blocks):
        own = slice(block * z.halved, (block + 1) * z.halved)
        picked = jnp.where(job_of[...] == z.get(sc, "in_rel", block), back[own], 0.0)
        picked = jnp.where(row_mask(z.get(sc, "in_valid", block), z, z.wide), picked, 0.0)
        out[own, z.rank :] = dot(picked, fold[...], ((1,), (0,)), lax.Precision.HIGHEST).astype(bf16)
    for k in range(many):
        copies[k].wait()
        down = dot(held[k], maps[:, : z.width], ((1,), (1,)))
        for r in range(n):
            block = k * n + r
            own = slice(block * z.halved, (block + 1) * z.halved)
            mine = slice(r * z.halved, (r + 1) * z.halved)
            picked = jnp.where(job_of[...] == z.get(sc, "out_rel", block), down[mine], 0.0)
            out[own, : z.rank] = dot(picked, fold[...], ((1,), (0,)), lax.Precision.HIGHEST).astype(bf16)


def products(z, sc, tokens, grad, maps, fold, job_of):
    n = 2
    shape = jax.ShapeDtypeStruct((z.rows, 2 * z.rank), bf16)
    return call(
        functools.partial(products_kernel, z, n), "adapter_products", (1,), sc,
        (tokens, grad, maps, fold, job_of),
        [ANY, whole(grad), whole(maps), whole(fold), whole(job_of)],
        shape, whole(shape), 1000, 1000, TOKEN_LIMIT,
        scratch=(
            pltpu.VMEM((z.blocks // n, n * z.halved, z.width), bf16),
            pltpu.SemaphoreType.DMA((z.blocks // n,)),
        ),
    )


def sums_kernel(z, sc, *refs):
    parts, outs = refs[: z.nt], refs[z.nt :]
    sums, pays = outs[0], outs[1:]
    total = parts[0][...].astype(f32)
    for part in parts[1:]:
        total = total + part[...].astype(f32)
    sums[...] = total.astype(bf16)
    for d in range(z.nd):
        back = (z.nd - d) % z.nd
        for r in range(z.cap):
            own = slice(r * z.halved, (r + 1) * z.halved)
            picked = sums[rows_of(z.get(sc, "out_pos", d * z.cap + r), z), : z.rank]
            pays[d][own, : z.rank] = jnp.where(z.get(sc, "out_fill", d * z.cap + r) > 0, picked, 0)
            picked = sums[rows_of(z.get(sc, "in_pos", back * z.cap + r), z), z.rank :]
            pays[d][own, z.rank :] = jnp.where(z.get(sc, "in_fill", back * z.cap + r) > 0, picked, 0)


def sums_of(z, sc, parts):
    shapes = [jax.ShapeDtypeStruct((z.rows, 2 * z.rank), bf16)]
    shapes += [jax.ShapeDtypeStruct((z.cap * z.halved, 2 * z.rank), bf16)] * z.nd
    return call(
        functools.partial(sums_kernel, z), "adapter_sums", (1,), sc, parts, [whole(x) for x in parts],
        tuple(shapes), tuple(whole(x) for x in shapes), 1000, 8 * z.rows * z.rank, 8 * MIB,
    )


def table_kernel(z, tiles, sc, tokens, grad, unfold, job_of, *refs):
    got, (mine, theirs, back, down, back_t, down_t, held, sems) = refs[: z.nd], refs[z.nd :]
    half = mine.shape[0]
    part = z.width // tiles
    copies = [
        pltpu.make_async_copy(tokens.at[:, pl.ds(k * part, part)], held.at[k], sems.at[k]) for k in range(tiles)
    ]
    for copy in copies:
        copy.start()
    for d in range(z.nd):
        for r in range(z.cap):
            slot = d * z.cap + r
            own = slice(r * z.halved, (r + 1) * z.halved)

            @pl.when(z.get(sc, "out_fill", slot) > 0)
            def _():
                at = z.get(sc, "out_pos", slot)
                values = got[(z.nd - d) % z.nd][own, z.rank :]
                back[rows_of(at, z), :] = widen(values, z.get(sc, "out_rel", at), unfold[...], job_of[...], z)

            @pl.when(z.get(sc, "in_fill", slot) > 0)
            def _():
                at = z.get(sc, "in_pos", slot)
                values = widen(got[d][own, : z.rank], z.get(sc, "in_rel", at), unfold[...], job_of[...], z)
                mask = row_mask(z.get(sc, "in_valid", at), z, z.wide)
                down[rows_of(at, z), :] = jnp.where(mask, values, 0).astype(bf16)

    same = lax.broadcasted_iota(i32, (z.rows, z.rows), 0) == lax.broadcasted_iota(i32, (z.rows, z.rows), 1)
    unit = jnp.where(same, 1.0, 0.0).astype(bf16)
    back_t[...] = dot(back[...], unit, ((0,), (0,))).astype(bf16)
    down_t[...] = dot(down[...], unit, ((0,), (0,))).astype(bf16)
    total = dot(down_t[...], grad[...], ((1,), (0,)))
    mine[:, z.width :] = total[:half]
    theirs[:, z.width :] = total[half:].astype(bf16)
    for k in range(tiles):
        copies[k].wait()
        total = dot(back_t[...], held[k], ((1,), (0,)))
        mine[:, k * part : (k + 1) * part] = total[:half]
        theirs[:, k * part : (k + 1) * part] = total[half:].astype(bf16)


def tables_of(z, sc, tokens, grad, unfold, job_of, got):
    tiles = 4
    shape = jax.ShapeDtypeStruct((z.wide // z.ns, z.width + z.heads), f32)
    sent = jax.ShapeDtypeStruct(shape.shape, bf16)
    return call(
        functools.partial(table_kernel, z, tiles), "job_tables", (1,), sc,
        (tokens, grad, unfold, job_of, *got),
        [ANY, whole(grad), whole(unfold), whole(job_of)] + [whole(x) for x in got],
        (shape, sent), (whole(shape), whole(sent)), 1000, 1000, TOKEN_LIMIT,
        scratch=(pltpu.VMEM((z.rows, z.wide), bf16),) * 2
        + (pltpu.VMEM((z.wide, z.rows), bf16),) * 2
        + (pltpu.VMEM((tiles, z.rows, z.width // tiles), bf16), pltpu.SemaphoreType.DMA((tiles,))),
    )


def layer_kernel(z, sc, sums, maps, unfold, job_of, *refs):
    m = z.per_head
    given, (outs, frozen) = refs[: m * z.nt], (refs[m * z.nt : -1], refs[-1])
    for j in range(m):
        total = given[j][...].astype(f32)
        for d in range(1, z.nt):
            total = total + given[d * m + j][...].astype(f32)
        for i in range(m):

            @pl.when(z.get(sc, "head", j) == i)
            def _():
                frozen[:, i * z.columns : (i + 1) * z.columns] = total

    for d in range(z.nd):
        for r in range(z.cap):
            slot = d * z.cap + r
            at = z.get(sc, "out_pos", slot)
            valid = jnp.where(z.get(sc, "out_fill", slot) > 0, z.get(sc, "out_valid", at), 0)
            wide = widen(sums[rows_of(at, z), : z.rank], z.get(sc, "out_rel", at), unfold[...], job_of[...], z)
            adapter = dot(wide, maps[...], ((1,), (0,)))
            layer = frozen[rows_of(at, z), :] + adapter_scale * adapter
            layer = jnp.where(row_mask(valid, z, z.heads), layer, 0.0)
            outs[d][r * z.halved : (r + 1) * z.halved, :] = layer.astype(bf16)


def layer_of(z, sc, sums, maps, unfold, job_of, given):
    shapes = [jax.ShapeDtypeStruct((z.cap * z.halved, z.heads), bf16)] * z.nd
    at = z.width // z.heads
    return call(
        functools.partial(layer_kernel, z), "layer", (1,), sc, (sums, maps, unfold, job_of, *given),
        [whole(sums), pl.BlockSpec((z.wide, z.heads), lambda i, _: (0, at)), whole(unfold), whole(job_of)]
        + [whole(x) for x in given],
        tuple(shapes), tuple(whole(x) for x in shapes),
        2 * z.rows * z.wide * z.heads, 6 * z.rows * z.heads, 16 * MIB,
        scratch=(pltpu.VMEM((z.rows, z.heads), f32),),
    )


def place_kernel(z, sc, *refs):
    got, out = refs[: z.nd], refs[z.nd]
    for d in range(z.nd):
        for r in range(z.cap):
            slot = d * z.cap + r

            @pl.when(z.get(sc, "in_fill", slot) > 0)
            def _():
                out[rows_of(z.get(sc, "in_pos", slot), z), :] = got[d][r * z.halved : (r + 1) * z.halved, :]


def place(z, sc, got):
    shape = jax.ShapeDtypeStruct((z.rows, z.heads), bf16)
    return call(
        functools.partial(place_kernel, z), "place", (1,), sc, got, [whole(x) for x in got],
        shape, whole(shape), 1000, 4 * z.rows * z.heads, 8 * MIB,
    )


def gradient_kernel(z, count, per, aliased, sc, maps, sums, unfold, job_of, *refs):
    grads, refs = refs[: z.nt], refs[z.nt :]
    pieces, refs = refs[: z.nd * count], refs[z.nd * count :]
    out, grad, back = refs[1:] if aliased else refs
    step = pl.program_id(0)
    m = z.per_head

    @pl.when(step == 0)
    def _():
        for v in range(z.nt * m):
            grad[v] = grads[v // m][:, v % m * z.columns : (v % m + 1) * z.columns]
        for b in range(z.blocks):
            own = slice(b * z.halved, (b + 1) * z.halved)
            back[own, :] = widen(sums[own, z.rank :], z.get(sc, "in_rel", b), unfold[...], job_of[...], z)

    for k in range(count):

        @pl.when(step // per == k)
        def _():
            total = adapter_scale * dot(back[...], maps[...], ((1,), (0,)))
            for d in range(z.nd):
                total = total + dot(grad[z.get(sc, "shard", d)], pieces[d * count + k][...], ((1,), (1,)))
            for b in range(z.blocks):
                own = slice(b * z.halved, (b + 1) * z.halved)
                mask = row_mask(z.get(sc, "in_valid", b), z, total.shape[1])
                out[own, :] = jnp.where(mask, total[own], 0.0).astype(bf16)


def token_gradient_of(z, sc, grads, maps, sums, unfold, job_of, piece_list, quarters, before):
    tile = min(512, z.fq)
    per = z.fq // tile
    at = z.at["quarter"]
    first, count = quarters[0], len(quarters)
    block = lambda i, q: (0, q[at + first + i // per] * per + i % per)
    specs, flat = [], []
    for d in range(z.nd):
        for k, r in enumerate(quarters):
            inner = lambda i, k=k: jnp.clip(i - k * per, 0, per - 1)
            if d == 0:
                index = lambda i, q, r=r, inner=inner: (q[at + r] * per + inner(i), 0)
            else:
                index = lambda i, q, inner=inner: (inner(i), 0)
            specs.append(pl.BlockSpec((tile, z.columns), index))
            flat.append(piece_list[d][r])
    inputs = [maps, sums, unfold, job_of, *grads, *flat]
    in_specs = [pl.BlockSpec((z.wide, tile), block), whole(sums), whole(unfold), whole(job_of)]
    in_specs += [whole(x) for x in grads] + specs
    alias = None
    if before is not None:
        alias = {1 + len(inputs): 0}
        inputs.append(before)
        in_specs.append(pl.BlockSpec(memory_space=pl.ANY))
    return call(
        functools.partial(gradient_kernel, z, count, per, before is not None),
        "token_gradient_%d" % first, (count * per,), sc, inputs, in_specs,
        jax.ShapeDtypeStruct((z.rows, z.width), bf16), pl.BlockSpec((z.rows, tile), block),
        1000, 1000, 14 * MIB,
        scratch=(pltpu.VMEM((z.nd, z.rows, z.columns), bf16), pltpu.VMEM((z.rows, z.wide), bf16)),
        alias=alias,
    )


def body(
    tokens,
    cotangent,
    frozen_value_weight,
    adapter_down,
    adapter_up,
    tokens_per_job,
    packed_block_slots,
):
    nd, nt, ns, np_ = (lax.axis_size(a) for a in ("dp", "tensor", "sub", "parts"))
    z, t, s, p = (lax.axis_index(a) for a in ("dp", "tensor", "sub", "parts"))
    blocks, halved, width = tokens.shape[1:]
    heads = cotangent.shape[3]
    jobs_dev, rank, _ = adapter_down.shape
    columns = frozen_value_weight.shape[1]
    zz = Sizes(nd, nt, ns, np_, blocks, halved, width, heads, jobs_dev, rank, columns)
    rows, r2, m, cap = zz.rows, rank // ns, zz.per_head, zz.cap
    own_tokens = tokens.reshape(rows, width)
    own_grad = cotangent.reshape(rows, heads)

    quarters = jnp.stack([(p - a) % np_ * ns + (s - b) % ns for a in range(np_) for b in range(ns)]).astype(i32)
    moving = lax.dynamic_slice_in_dim(frozen_value_weight, (p * ns + s) * zz.fq, zz.fq, axis=0)

    maps = jnp.concatenate([adapter_down, adapter_up], axis=2).reshape(jobs_dev, ns, r2, width + heads)
    maps = lax.dynamic_index_in_dim(maps, s, 1, keepdims=False)
    maps, moving = tie(maps, moving)
    rounds = [None, shifted(moving, "dp", nd, 1)]
    token_quarters = [lax.dynamic_slice_in_dim(own_tokens, quarters[r] * zz.fq, zz.fq, 1) for r in range(zz.nq)]
    maps, rounds[1], token_quarters = tie(gather_shifts(maps, "dp", nd), rounds[1], token_quarters)
    maps = jnp.concatenate(maps, axis=0).reshape(zz.jobs * r2, -1)
    maps = jnp.concatenate(gather_shifts(maps, "sub", ns), axis=0)
    grads = gather_shifts(own_grad, "tensor", nt)

    positions = jnp.arange(blocks, dtype=i32)
    dest = packed_block_slots // blocks
    same = dest[:, :, None] == dest[:, None, :]
    earlier = positions[None, None, :] < positions[None, :, None]
    send_rank = jnp.sum((same & earlier).astype(i32), axis=2, dtype=i32)
    flat_slots = packed_block_slots.reshape(-1)
    flat_ids = jnp.arange(nd * blocks, dtype=i32)
    slot_owner = flat_slots[None, :] == (z * blocks + positions)[:, None]
    block_ids = jnp.sum(jnp.where(slot_owner, flat_ids[None, :], 0), axis=1, dtype=i32)
    in_rank = jnp.sum(jnp.where(slot_owner, send_rank.reshape(-1)[None, :], 0), axis=1, dtype=i32)
    in_slot = (z - block_ids // blocks) % nd * cap + in_rank
    own_dest = lax.dynamic_index_in_dim(dest, z, 0, keepdims=False)
    own_rank = lax.dynamic_index_in_dim(send_rank, z, 0, keepdims=False)
    out_slot = (own_dest - z) % nd * cap + own_rank
    slot_range = jnp.arange(zz.slots, dtype=i32)

    def positions_of(slots):
        match = slots[None, :] == slot_range[:, None]
        return jnp.sum(jnp.where(match, positions[None, :], 0), axis=1, dtype=i32), jnp.any(match, axis=1)

    out_pos, out_fill = positions_of(out_slot)
    in_pos, in_fill = positions_of(in_slot)

    def facts(ids):
        job, valid = block_facts(tokens_per_job, ids, halved * ns)
        return (z - job // jobs_dev) % nd * jobs_dev + job % jobs_dev, valid - s * halved

    out_rel, out_valid = facts(z * blocks + positions)
    in_rel, in_valid = facts(block_ids)

    def arrival(index):
        found = (z - index * m - jnp.arange(m, dtype=i32)) % nd
        place_of = jnp.sum((found[None, :] < found[:, None]).astype(i32), axis=1)
        match = place_of[None, :] == jnp.arange(m, dtype=i32)[:, None]
        return jnp.sum(jnp.where(match, found[None, :], 0), axis=1, dtype=i32)

    shard_of = (z - jnp.arange(nd, dtype=i32)) % nd
    shard_at = (t - shard_of // m) % nt * m + shard_of % m
    arrivals = [arrival((t + g) % nt) for g in range(nt)]
    head_at = (z - arrivals[0]) % nd - t * m
    sc = jnp.concatenate(
        [
            x.astype(i32)
            for x in (out_pos, in_pos, out_fill, in_fill, out_rel, in_rel, out_valid, in_valid, quarters, shard_at, head_at, *arrivals)
        ]
    )
    column = jnp.arange(zz.wide, dtype=i32)
    job_of = (column // r2 % zz.jobs)[None, :]
    rank_of = column // (zz.jobs * r2) * r2 + column % r2
    unfold = (jnp.arange(rank, dtype=i32)[:, None] == rank_of[None, :]).astype(bf16)
    fold = unfold.astype(f32).T

    def product(pieces, first=0):
        return sum(dot(token_quarters[first + r], x, ((1,), (0,))) for r, x in enumerate(pieces))

    def spread_round(over_parts):
        return [x for y in over_parts for x in gather_shifts(y, "sub", ns)]

    last = nd - 1
    over = [None] * nd
    over[1] = gather_shifts(rounds[1], "parts", np_)
    for d in range(2, last):
        rounds.append(shifted(rounds[-1], "dp", nd, 1))
    swapped = gather_shifts(over[1][0], "sub", ns)
    maps, swapped = tie(maps, swapped)
    part = products(zz, sc, own_tokens, own_grad, maps, fold, job_of)
    parts = gather_shifts(part, "tensor", nt)
    late_weight, _ = tie(frozen_value_weight, part)
    base = [dot(own_tokens, late_weight, ((1,), (0,))).astype(bf16)]
    base[0], parts, grads = tie(base[0], parts, grads)
    sums, *pays = sums_of(zz, sc, parts)
    rounds[last - 1], over[1], sums = tie(rounds[last - 1], over[1], sums)

    end = shifted(rounds[last - 1], "dp", nd, 1)
    for d in range(2, last):
        over[d] = gather_shifts(rounds[d], "parts", np_)
    piece_list = [[frozen_value_weight] * zz.nq, swapped + spread_round(over[1][1:])]
    crossed = [gather_shifts(over[d][0], "sub", ns) for d in range(2, last)]
    piece_list[1], crossed = tie(piece_list[1], crossed)
    base.append(product(piece_list[1]).astype(bf16))
    base[1], end, over[2:last], pays = tie(base[1], end, over[2:last], pays)

    behind = gather_shifts(end, "parts", np_)
    got = [shifted(pays[d], "dp", nd, d) for d in range(nd)]
    piece_list += [crossed[d - 2] + spread_round(over[d][1:]) for d in range(2, last)]

    slots = []

    def finish(values):
        base.append(values.astype(bf16))
        due = len(base) - 1 - (nd - m)
        if due >= 0:
            made = []
            for g in range(nt):
                picked = base[-1]
                for k in range(due, len(base) - 1):
                    picked = jnp.where(arrivals[g][due] == k, base[k], picked)
                made.append(shifted(picked, "tensor", nt, g))
            slots.append(made)

    for d in range(2, last):
        finish(product(piece_list[d]))
    base[-1], got = tie(base[-1], got)
    mine, theirs = tables_of(zz, sc, own_tokens, own_grad, unfold, job_of, got)
    theirs = shifted(theirs, "sub", ns, 1)
    ahead = gather_shifts(end, "sub", ns)
    ahead, mine = tie(ahead, mine)
    begun = product(ahead)
    begun, behind, slots = tie(begun, behind, slots)
    tail = spread_round(behind[1:])
    piece_list.append(ahead + tail)
    finish(begun + product(tail, len(ahead)))
    base[-1], mine, theirs, grads = tie(base[-1], mine, theirs, grads)

    summed = (mine + theirs).reshape(nd, jobs_dev * r2, -1)
    sending = [summed[d].astype(bf16) for d in range(nd)]
    tables = [sending[0]] + [shifted(sending[d], "dp", nd, -d) for d in range(1, nd)]

    half = zz.nq // 2
    gradient = token_gradient_of(zz, sc, grads, maps, sums, unfold, job_of, piece_list, list(range(half)), None)
    given = [slots[j][d] for d in range(nt) for j in range(m)]
    gradient, given = tie(gradient, given)
    layer = layer_of(zz, sc, sums, maps, unfold, job_of, given)
    layer, gradient, tables = tie(layer, gradient, tables)
    landed = [shifted(layer[d], "dp", nd, d) for d in range(nd)]
    total = sum(x.astype(f32) for x in tables)
    counts = lax.dynamic_slice_in_dim(tokens_per_job, z * jobs_dev, jobs_dev).astype(f32)
    total = total.reshape(jobs_dev, r2, -1) * (adapter_scale / counts)[:, None, None]
    halves = gather_shifts(total, "sub", ns)
    gradient, halves = tie(gradient, halves)
    owned = jnp.concatenate(
        [sum(jnp.where((s - h) % ns == k, x, 0.0) for k, x in enumerate(halves)) for h in range(ns)], axis=1
    )
    grad_down, grad_up = owned[:, :, :width], owned[:, :, width:]
    gradient = token_gradient_of(
        zz, sc, grads, maps, sums, unfold, job_of, piece_list, list(range(half, zz.nq)), gradient
    )
    gradient, grad_down, grad_up, landed = tie(gradient, grad_down, grad_up, landed)
    layer_output = place(zz, sc, landed)
    return (
        layer_output.reshape(1, blocks, halved, heads),
        gradient.reshape(1, blocks, halved, width),
        grad_down,
        grad_up,
    )


def solution(mesh):
    return jax.shard_map(
        body,
        mesh=mesh,
        in_specs=(
            P(("parts", "dp"), None, "sub", "tensor"),
            P(("parts", "dp"), None, "sub", "tensor"),
            P("tensor", "dp"),
            P(("parts", "dp"), None, "tensor"),
            P(("parts", "dp"), None, "tensor"),
            P("parts"),
            P("parts", None),
        ),
        out_specs=(
            P(("parts", "dp"), None, "sub", "tensor"),
            P(("parts", "dp"), None, "sub", "tensor"),
            P(("parts", "dp"), None, "tensor"),
            P(("parts", "dp"), None, "tensor"),
        ),
        check_vma=False,
    )
```

```python
import functools

import jax
import jax.numpy as jnp
from jax import lax
from jax.experimental import pallas as pl
from jax.experimental.pallas import tpu as pltpu
from jax.sharding import PartitionSpec as P

adapter_scale = 2.0
f32, bf16, i32 = jnp.float32, jnp.bfloat16, jnp.int32
MIB = 1 << 20
TOKEN_LIMIT = 16 * MIB


def block_facts(tokens_per_job, block_ids, block_rows):
    job_total = tokens_per_job.shape[0]
    blocks = (tokens_per_job + (block_rows - 1)) // block_rows
    block_ends = jnp.cumsum(blocks, dtype=jnp.int32)
    starts = block_ends - blocks
    job_index = jnp.sum(
        (block_ends[None, :] <= block_ids[:, None]).astype(jnp.int32), axis=1, dtype=jnp.int32
    )
    chosen = job_index[:, None] == jnp.arange(job_total, dtype=jnp.int32)[None, :]
    job_count = jnp.sum(jnp.where(chosen, tokens_per_job[None, :], 0), axis=1, dtype=jnp.int32)
    first_block = jnp.sum(jnp.where(chosen, starts[None, :], 0), axis=1, dtype=jnp.int32)
    valid_rows = jnp.clip(job_count - block_rows * (block_ids - first_block), 0, block_rows)
    return job_index, valid_rows


def shifted(values, axis, count, step):
    if step % count == 0:
        return values
    return lax.ppermute(values, axis, [(i, (i + step) % count) for i in range(count)])


def gather_shifts(values, axis, count):
    return [shifted(values, axis, count, d) for d in range(count)]


def dot(a, b, dims, precision=None):
    return lax.dot_general(a, b, (dims, ((), ())), precision=precision, preferred_element_type=f32)


def tie(*values):
    return lax.optimization_barrier(values)


class Sizes:
    def __init__(self, nd, nt, ns, np_, blocks, halved, width, heads, jobs_dev, rank, columns):
        self.nd, self.nt, self.ns, self.np_ = nd, nt, ns, np_
        self.blocks, self.halved, self.width, self.heads = blocks, halved, width, heads
        self.jobs, self.jobs_dev, self.rank, self.columns = nd * jobs_dev, jobs_dev, rank, columns
        self.wide = self.jobs * rank
        self.rows = blocks * halved
        self.cap = -(-blocks // nd)
        self.slots = nd * self.cap
        self.nq = np_ * ns
        self.fq = width // self.nq
        self.per_head = nd // nt
        at, self.at = 0, {}
        for name, count in (
            ("out_pos", self.slots), ("in_pos", self.slots), ("out_fill", self.slots), ("in_fill", self.slots),
            ("out_rel", blocks), ("in_rel", blocks), ("out_valid", blocks), ("in_valid", blocks),
            ("quarter", self.nq), ("shard", nd), ("head", self.per_head),
            ("pick", self.per_head * nt),
        ):
            self.at[name] = at
            at += count

    def get(self, ref, name, index):
        return ref[self.at[name] + index]


def call(kernel, name, grid, scalars, inputs, in_specs, out_shape, out_specs, flops, moved, limit, scratch=(), alias=None):
    return pl.pallas_call(
        kernel,
        out_shape=out_shape,
        grid_spec=pltpu.PrefetchScalarGridSpec(
            num_scalar_prefetch=1, grid=grid, in_specs=in_specs, out_specs=out_specs, scratch_shapes=list(scratch)
        ),
        input_output_aliases=alias or {},
        compiler_params=pltpu.CompilerParams(vmem_limit_bytes=limit),
        cost_estimate=pl.CostEstimate(flops=flops, bytes_accessed=moved, transcendentals=0),
        name=name,
    )(scalars, *inputs)


ANY = pl.BlockSpec(memory_space=pl.ANY)


def whole(x):
    return pl.BlockSpec(x.shape, lambda *_: (0,) * len(x.shape))


def rows_of(index, z):
    return pl.ds(pl.multiple_of(index * z.halved, z.halved), z.halved)


def row_mask(valid, z, lanes):
    return lax.broadcasted_iota(i32, (z.halved, lanes), 0) < valid


def widen(values, rel, unfold, job_of, z):
    wide = dot(values, unfold, ((1,), (0,)))
    return jnp.where(job_of == rel, wide, 0.0).astype(bf16)


def products_kernel(z, n, sc, tokens, grad, maps, fold, job_of, out, held, sems):
    many = z.blocks // n
    copies = [
        pltpu.make_async_copy(tokens.at[pl.ds(k * n * z.halved, n * z.halved), :], held.at[k], sems.at[k])
        for k in range(many)
    ]
    for copy in copies:
        copy.start()
    back = dot(grad[...], maps[:, z.width :], ((1,), (1,)))
    for block in range(z.blocks):
        own = slice(block * z.halved, (block + 1) * z.halved)
        picked = jnp.where(job_of[...] == z.get(sc, "in_rel", block), back[own], 0.0)
        picked = jnp.where(row_mask(z.get(sc, "in_valid", block), z, z.wide), picked, 0.0)
        out[own, z.rank :] = dot(picked, fold[...], ((1,), (0,)), lax.Precision.HIGHEST).astype(bf16)
    for k in range(many):
        copies[k].wait()
        down = dot(held[k], maps[:, : z.width], ((1,), (1,)))
        for r in range(n):
            block = k * n + r
            own = slice(block * z.halved, (block + 1) * z.halved)
            mine = slice(r * z.halved, (r + 1) * z.halved)
            picked = jnp.where(job_of[...] == z.get(sc, "out_rel", block), down[mine], 0.0)
            out[own, : z.rank] = dot(picked, fold[...], ((1,), (0,)), lax.Precision.HIGHEST).astype(bf16)


def products(z, sc, tokens, grad, maps, fold, job_of):
    n = 2
    shape = jax.ShapeDtypeStruct((z.rows, 2 * z.rank), bf16)
    return call(
        functools.partial(products_kernel, z, n), "adapter_products", (1,), sc,
        (tokens, grad, maps, fold, job_of),
        [ANY, whole(grad), whole(maps), whole(fold), whole(job_of)],
        shape, whole(shape), 1000, 1000, TOKEN_LIMIT,
        scratch=(
            pltpu.VMEM((z.blocks // n, n * z.halved, z.width), bf16),
            pltpu.SemaphoreType.DMA((z.blocks // n,)),
        ),
    )


def sums_kernel(z, sc, *refs):
    parts, outs = refs[: z.nt], refs[z.nt :]
    sums, pays = outs[0], outs[1:]
    total = parts[0][...].astype(f32)
    for part in parts[1:]:
        total = total + part[...].astype(f32)
    sums[...] = total.astype(bf16)
    for d in range(z.nd):
        back = (z.nd - d) % z.nd
        for r in range(z.cap):
            own = slice(r * z.halved, (r + 1) * z.halved)
            picked = sums[rows_of(z.get(sc, "out_pos", d * z.cap + r), z), : z.rank]
            pays[d][own, : z.rank] = jnp.where(z.get(sc, "out_fill", d * z.cap + r) > 0, picked, 0)
            picked = sums[rows_of(z.get(sc, "in_pos", back * z.cap + r), z), z.rank :]
            pays[d][own, z.rank :] = jnp.where(z.get(sc, "in_fill", back * z.cap + r) > 0, picked, 0)


def sums_of(z, sc, parts):
    shapes = [jax.ShapeDtypeStruct((z.rows, 2 * z.rank), bf16)]
    shapes += [jax.ShapeDtypeStruct((z.cap * z.halved, 2 * z.rank), bf16)] * z.nd
    return call(
        functools.partial(sums_kernel, z), "adapter_sums", (1,), sc, parts, [whole(x) for x in parts],
        tuple(shapes), tuple(whole(x) for x in shapes), 1000, 1000, 8 * MIB,
    )


def table_kernel(z, tiles, sc, tokens, grad, unfold, job_of, *refs):
    got, (mine, theirs, back, down, back_t, down_t, held, sems) = refs[: z.nd], refs[z.nd :]
    half = mine.shape[0]
    part = z.width // tiles
    copies = [
        pltpu.make_async_copy(tokens.at[:, pl.ds(k * part, part)], held.at[k], sems.at[k]) for k in range(tiles)
    ]
    for copy in copies:
        copy.start()
    for d in range(z.nd):
        for r in range(z.cap):
            slot = d * z.cap + r
            own = slice(r * z.halved, (r + 1) * z.halved)

            @pl.when(z.get(sc, "out_fill", slot) > 0)
            def _():
                at = z.get(sc, "out_pos", slot)
                values = got[(z.nd - d) % z.nd][own, z.rank :]
                back[rows_of(at, z), :] = widen(values, z.get(sc, "out_rel", at), unfold[...], job_of[...], z)

            @pl.when(z.get(sc, "in_fill", slot) > 0)
            def _():
                at = z.get(sc, "in_pos", slot)
                values = widen(got[d][own, : z.rank], z.get(sc, "in_rel", at), unfold[...], job_of[...], z)
                mask = row_mask(z.get(sc, "in_valid", at), z, z.wide)
                down[rows_of(at, z), :] = jnp.where(mask, values, 0).astype(bf16)

    same = lax.broadcasted_iota(i32, (z.rows, z.rows), 0) == lax.broadcasted_iota(i32, (z.rows, z.rows), 1)
    unit = jnp.where(same, 1.0, 0.0).astype(bf16)
    back_t[...] = dot(back[...], unit, ((0,), (0,))).astype(bf16)
    down_t[...] = dot(down[...], unit, ((0,), (0,))).astype(bf16)
    total = dot(down_t[...], grad[...], ((1,), (0,)))
    mine[:, z.width :] = total[:half]
    theirs[:, z.width :] = total[half:].astype(bf16)
    for k in range(tiles):
        copies[k].wait()
        total = dot(back_t[...], held[k], ((1,), (0,)))
        mine[:, k * part : (k + 1) * part] = total[:half]
        theirs[:, k * part : (k + 1) * part] = total[half:].astype(bf16)


def tables_of(z, sc, tokens, grad, unfold, job_of, got):
    tiles = 4
    shape = jax.ShapeDtypeStruct((z.wide // z.ns, z.width + z.heads), f32)
    sent = jax.ShapeDtypeStruct(shape.shape, bf16)
    return call(
        functools.partial(table_kernel, z, tiles), "job_tables", (1,), sc,
        (tokens, grad, unfold, job_of, *got),
        [ANY, whole(grad), whole(unfold), whole(job_of)] + [whole(x) for x in got],
        (shape, sent), (whole(shape), whole(sent)), 1000, 1000, TOKEN_LIMIT,
        scratch=(pltpu.VMEM((z.rows, z.wide), bf16),) * 2
        + (pltpu.VMEM((z.wide, z.rows), bf16),) * 2
        + (pltpu.VMEM((tiles, z.rows, z.width // tiles), bf16), pltpu.SemaphoreType.DMA((tiles,))),
    )


def layer_kernel(z, sc, sums, maps, unfold, job_of, *refs):
    m = z.per_head
    given, (outs, frozen) = refs[: m * z.nt], (refs[m * z.nt : -1], refs[-1])
    for j in range(m):
        total = given[j][...].astype(f32)
        for d in range(1, z.nt):
            total = total + given[d * m + j][...].astype(f32)
        for i in range(m):

            @pl.when(z.get(sc, "head", j) == i)
            def _():
                frozen[:, i * z.columns : (i + 1) * z.columns] = total

    for d in range(z.nd):
        for r in range(z.cap):
            slot = d * z.cap + r
            at = z.get(sc, "out_pos", slot)
            valid = jnp.where(z.get(sc, "out_fill", slot) > 0, z.get(sc, "out_valid", at), 0)
            wide = widen(sums[rows_of(at, z), : z.rank], z.get(sc, "out_rel", at), unfold[...], job_of[...], z)
            adapter = dot(wide, maps[...], ((1,), (0,)))
            layer = frozen[rows_of(at, z), :] + adapter_scale * adapter
            layer = jnp.where(row_mask(valid, z, z.heads), layer, 0.0)
            outs[d][r * z.halved : (r + 1) * z.halved, :] = layer.astype(bf16)


def layer_of(z, sc, sums, maps, unfold, job_of, given):
    shapes = [jax.ShapeDtypeStruct((z.cap * z.halved, z.heads), bf16)] * z.nd
    at = z.width // z.heads
    return call(
        functools.partial(layer_kernel, z), "layer", (1,), sc, (sums, maps, unfold, job_of, *given),
        [whole(sums), pl.BlockSpec((z.wide, z.heads), lambda i, _: (0, at)), whole(unfold), whole(job_of)]
        + [whole(x) for x in given],
        tuple(shapes), tuple(whole(x) for x in shapes),
        2 * z.rows * z.wide * z.heads, 6 * z.rows * z.heads, 12 * MIB,
        scratch=(pltpu.VMEM((z.rows, z.heads), f32),),
    )


def place_kernel(z, sc, *refs):
    got, out = refs[: z.nd], refs[z.nd]
    for d in range(z.nd):
        for r in range(z.cap):
            slot = d * z.cap + r

            @pl.when(z.get(sc, "in_fill", slot) > 0)
            def _():
                out[rows_of(z.get(sc, "in_pos", slot), z), :] = got[d][r * z.halved : (r + 1) * z.halved, :]


def place(z, sc, got):
    shape = jax.ShapeDtypeStruct((z.rows, z.heads), bf16)
    return call(
        functools.partial(place_kernel, z), "place", (1,), sc, got, [whole(x) for x in got],
        shape, whole(shape), 1000, 4 * z.rows * z.heads, 8 * MIB,
    )


def gradient_kernel(z, count, per, aliased, sc, maps, sums, unfold, job_of, *refs):
    grads, refs = refs[: z.nt], refs[z.nt :]
    pieces, refs = refs[: z.nd * count], refs[z.nd * count :]
    out, grad, back = refs[1:] if aliased else refs
    step = pl.program_id(0)
    m = z.per_head

    @pl.when(step == 0)
    def _():
        for v in range(z.nt * m):
            grad[v] = grads[v // m][:, v % m * z.columns : (v % m + 1) * z.columns]
        for b in range(z.blocks):
            own = slice(b * z.halved, (b + 1) * z.halved)
            back[own, :] = widen(sums[own, z.rank :], z.get(sc, "in_rel", b), unfold[...], job_of[...], z)

    for k in range(count):

        @pl.when(step // per == k)
        def _():
            total = adapter_scale * dot(back[...], maps[...], ((1,), (0,)))
            for d in range(z.nd):
                total = total + dot(grad[z.get(sc, "shard", d)], pieces[d * count + k][...], ((1,), (1,)))
            for b in range(z.blocks):
                own = slice(b * z.halved, (b + 1) * z.halved)
                mask = row_mask(z.get(sc, "in_valid", b), z, total.shape[1])
                out[own, :] = jnp.where(mask, total[own], 0.0).astype(bf16)


def token_gradient_of(z, sc, grads, maps, sums, unfold, job_of, piece_list, quarters, before):
    tile = min(512, z.fq)
    per = z.fq // tile
    at = z.at["quarter"]
    first, count = quarters[0], len(quarters)
    block = lambda i, q: (0, q[at + first + i // per] * per + i % per)
    specs, flat = [], []
    for d in range(z.nd):
        for k, r in enumerate(quarters):
            inner = lambda i, k=k: jnp.clip(i - k * per, 0, per - 1)
            if d == 0:
                index = lambda i, q, r=r, inner=inner: (q[at + r] * per + inner(i), 0)
            else:
                index = lambda i, q, inner=inner: (inner(i), 0)
            specs.append(pl.BlockSpec((tile, z.columns), index))
            flat.append(piece_list[d][r])
    inputs = [maps, sums, unfold, job_of, *grads, *flat]
    in_specs = [pl.BlockSpec((z.wide, tile), block), whole(sums), whole(unfold), whole(job_of)]
    in_specs += [whole(x) for x in grads] + specs
    alias = None
    if before is not None:
        alias = {1 + len(inputs): 0}
        inputs.append(before)
        in_specs.append(pl.BlockSpec(memory_space=pl.ANY))
    return call(
        functools.partial(gradient_kernel, z, count, per, before is not None),
        "token_gradient_%d" % first, (count * per,), sc, inputs, in_specs,
        jax.ShapeDtypeStruct((z.rows, z.width), bf16), pl.BlockSpec((z.rows, tile), block),
        1000 if alias is None else 2 * z.rows * count * z.fq * (z.nd * z.columns + z.wide),
        1000 if alias is None else 2 * count * z.fq * (z.rows + z.nd * z.columns), 14 * MIB,
        scratch=(pltpu.VMEM((z.nd, z.rows, z.columns), bf16), pltpu.VMEM((z.rows, z.wide), bf16)),
        alias=alias,
    )


def body(
    tokens,
    cotangent,
    frozen_value_weight,
    adapter_down,
    adapter_up,
    tokens_per_job,
    packed_block_slots,
):
    nd, nt, ns, np_ = (lax.axis_size(a) for a in ("dp", "tensor", "sub", "parts"))
    z, t, s, p = (lax.axis_index(a) for a in ("dp", "tensor", "sub", "parts"))
    blocks, halved, width = tokens.shape[1:]
    heads = cotangent.shape[3]
    jobs_dev, rank, _ = adapter_down.shape
    columns = frozen_value_weight.shape[1]
    zz = Sizes(nd, nt, ns, np_, blocks, halved, width, heads, jobs_dev, rank, columns)
    rows, r2, m, cap = zz.rows, rank // ns, zz.per_head, zz.cap
    own_tokens = tokens.reshape(rows, width)
    own_grad = cotangent.reshape(rows, heads)

    quarters = jnp.stack([(p - a) % np_ * ns + (s - b) % ns for a in range(np_) for b in range(ns)]).astype(i32)
    moving = lax.dynamic_slice_in_dim(frozen_value_weight, (p * ns + s) * zz.fq, zz.fq, axis=0)

    maps = jnp.concatenate([adapter_down, adapter_up], axis=2).reshape(jobs_dev, ns, r2, width + heads)
    maps = lax.dynamic_index_in_dim(maps, s, 1, keepdims=False)
    maps, moving = tie(maps, moving)
    rounds = [None, shifted(moving, "dp", nd, 1)]
    token_quarters = [lax.dynamic_slice_in_dim(own_tokens, quarters[r] * zz.fq, zz.fq, 1) for r in range(zz.nq)]
    def arrival(index):
        found = (z - index * m - jnp.arange(m, dtype=i32)) % nd
        place_of = jnp.sum((found[None, :] < found[:, None]).astype(i32), axis=1)
        match = place_of[None, :] == jnp.arange(m, dtype=i32)[:, None]
        return jnp.sum(jnp.where(match, found[None, :], 0), axis=1, dtype=i32)

    arrivals = [arrival((t + g) % nt) for g in range(nt)]
    chosen = [[[x[j] == k for k in range(nd)] for j in range(m)] for x in arrivals]
    scale = adapter_scale / lax.dynamic_slice_in_dim(tokens_per_job, z * jobs_dev, jobs_dev).astype(f32)
    maps, rounds[1], token_quarters, chosen, scale = tie(
        gather_shifts(maps, "dp", nd), rounds[1], token_quarters, chosen, scale
    )
    maps = jnp.concatenate(maps, axis=0).reshape(zz.jobs * r2, -1)
    maps = jnp.concatenate(gather_shifts(maps, "sub", ns), axis=0)
    grads = gather_shifts(own_grad, "tensor", nt)

    positions = jnp.arange(blocks, dtype=i32)
    dest = packed_block_slots // blocks
    same = dest[:, :, None] == dest[:, None, :]
    earlier = positions[None, None, :] < positions[None, :, None]
    send_rank = jnp.sum((same & earlier).astype(i32), axis=2, dtype=i32)
    flat_slots = packed_block_slots.reshape(-1)
    flat_ids = jnp.arange(nd * blocks, dtype=i32)
    slot_owner = flat_slots[None, :] == (z * blocks + positions)[:, None]
    block_ids = jnp.sum(jnp.where(slot_owner, flat_ids[None, :], 0), axis=1, dtype=i32)
    in_rank = jnp.sum(jnp.where(slot_owner, send_rank.reshape(-1)[None, :], 0), axis=1, dtype=i32)
    in_slot = (z - block_ids // blocks) % nd * cap + in_rank
    own_dest = lax.dynamic_index_in_dim(dest, z, 0, keepdims=False)
    own_rank = lax.dynamic_index_in_dim(send_rank, z, 0, keepdims=False)
    out_slot = (own_dest - z) % nd * cap + own_rank
    slot_range = jnp.arange(zz.slots, dtype=i32)

    def positions_of(slots):
        match = slots[None, :] == slot_range[:, None]
        return jnp.sum(jnp.where(match, positions[None, :], 0), axis=1, dtype=i32), jnp.any(match, axis=1)

    out_pos, out_fill = positions_of(out_slot)
    in_pos, in_fill = positions_of(in_slot)

    def facts(ids):
        job, valid = block_facts(tokens_per_job, ids, halved * ns)
        return (z - job // jobs_dev) % nd * jobs_dev + job % jobs_dev, valid - s * halved

    out_rel, out_valid = facts(z * blocks + positions)
    in_rel, in_valid = facts(block_ids)

    shard_of = (z - jnp.arange(nd, dtype=i32)) % nd
    shard_at = (t - shard_of // m) % nt * m + shard_of % m
    head_at = (z - arrivals[0]) % nd - t * m
    sc = jnp.concatenate(
        [
            x.astype(i32)
            for x in (out_pos, in_pos, out_fill, in_fill, out_rel, in_rel, out_valid, in_valid, quarters, shard_at, head_at, *arrivals)
        ]
    )
    column = jnp.arange(zz.wide, dtype=i32)
    job_of = (column // r2 % zz.jobs)[None, :]
    rank_of = column // (zz.jobs * r2) * r2 + column % r2
    unfold = (jnp.arange(rank, dtype=i32)[:, None] == rank_of[None, :]).astype(bf16)
    fold = unfold.astype(f32).T

    def product(pieces, first=0):
        return sum(dot(token_quarters[first + r], x, ((1,), (0,))) for r, x in enumerate(pieces))

    def spread_round(over_parts):
        return [x for y in over_parts for x in gather_shifts(y, "sub", ns)]

    last = nd - 1
    over = [None] * nd
    over[1] = gather_shifts(rounds[1], "parts", np_)
    for d in range(2, last):
        rounds.append(shifted(rounds[-1], "dp", nd, 1))
    swapped = gather_shifts(over[1][0], "sub", ns)
    maps, swapped = tie(maps, swapped)
    part = products(zz, sc, own_tokens, own_grad, maps, fold, job_of)
    parts = gather_shifts(part, "tensor", nt)
    late_weight, _ = tie(frozen_value_weight, part)
    base = [dot(own_tokens, late_weight, ((1,), (0,))).astype(bf16)]
    base[0], parts, grads = tie(base[0], parts, grads)
    sums, *pays = sums_of(zz, sc, parts)
    rounds[last - 1], over[1], sums = tie(rounds[last - 1], over[1], sums)

    end = shifted(rounds[last - 1], "dp", nd, 1)
    for d in range(2, last):
        over[d] = gather_shifts(rounds[d], "parts", np_)
    piece_list = [[frozen_value_weight] * zz.nq, swapped + spread_round(over[1][1:])]
    crossed = [gather_shifts(over[d][0], "sub", ns) for d in range(2, last)]
    piece_list[1], crossed = tie(piece_list[1], crossed)
    base.append(product(piece_list[1]).astype(bf16))
    base[1], end, over[2:last], pays = tie(base[1], end, over[2:last], pays)

    behind = gather_shifts(end, "parts", np_)
    got = [shifted(pays[d], "dp", nd, d) for d in range(nd)]
    piece_list += [crossed[d - 2] + spread_round(over[d][1:]) for d in range(2, last)]

    slots = []

    def finish(values):
        base.append(values.astype(bf16))
        due = len(base) - 1 - (nd - m)
        if due >= 0:
            made = []
            for g in range(nt):
                picked = base[-1]
                for k in range(due, len(base) - 1):
                    picked = jnp.where(chosen[g][due][k], base[k], picked)
                made.append(shifted(picked, "tensor", nt, g))
            slots.append(made)

    for d in range(2, last):
        finish(product(piece_list[d]))
    base[-1], got = tie(base[-1], got)
    mine, theirs = tables_of(zz, sc, own_tokens, own_grad, unfold, job_of, got)
    theirs = shifted(theirs, "sub", ns, 1)
    ahead = gather_shifts(end, "sub", ns)
    ahead, mine = tie(ahead, mine)
    begun = product(ahead)
    begun, behind, slots = tie(begun, behind, slots)
    tail = spread_round(behind[1:])
    piece_list.append(ahead + tail)
    finish(begun + product(tail, len(ahead)))
    base[-1], mine, theirs, grads = tie(base[-1], mine, theirs, grads)

    summed = (mine + theirs).reshape(nd, jobs_dev * r2, -1)
    sending = [summed[d].astype(bf16) for d in range(nd)]
    tables = [sending[0]] + [shifted(sending[d], "dp", nd, -d) for d in range(1, nd)]

    half = zz.nq // 2
    gradient = token_gradient_of(zz, sc, grads, maps, sums, unfold, job_of, piece_list, list(range(half)), None)
    given = [slots[j][d] for d in range(nt) for j in range(m)]
    gradient, given = tie(gradient, given)
    layer = layer_of(zz, sc, sums, maps, unfold, job_of, given)
    layer, gradient, tables = tie(layer, gradient, tables)
    landed = [shifted(layer[d], "dp", nd, d) for d in range(nd)]
    total = sum(x.astype(f32) for x in tables)
    total = total.reshape(jobs_dev, r2, -1) * scale[:, None, None]
    halves = gather_shifts(total, "sub", ns)
    gradient, halves = tie(gradient, halves)
    owned = jnp.concatenate(
        [sum(jnp.where((s - h) % ns == k, x, 0.0) for k, x in enumerate(halves)) for h in range(ns)], axis=1
    )
    grad_down, grad_up = owned[:, :, :width], owned[:, :, width:]
    gradient = token_gradient_of(
        zz, sc, grads, maps, sums, unfold, job_of, piece_list, list(range(half, zz.nq)), gradient
    )
    gradient, grad_down, grad_up, landed = tie(gradient, grad_down, grad_up, landed)
    layer_output = place(zz, sc, landed)
    return (
        layer_output.reshape(1, blocks, halved, heads),
        gradient.reshape(1, blocks, halved, width),
        grad_down,
        grad_up,
    )


def solution(mesh):
    return jax.shard_map(
        body,
        mesh=mesh,
        in_specs=(
            P(("parts", "dp"), None, "sub", "tensor"),
            P(("parts", "dp"), None, "sub", "tensor"),
            P("tensor", "dp"),
            P(("parts", "dp"), None, "tensor"),
            P(("parts", "dp"), None, "tensor"),
            P("parts"),
            P("parts", None),
        ),
        out_specs=(
            P(("parts", "dp"), None, "sub", "tensor"),
            P(("parts", "dp"), None, "sub", "tensor"),
            P(("parts", "dp"), None, "tensor"),
            P(("parts", "dp"), None, "tensor"),
        ),
        check_vma=False,
    )
```

```python
import functools

import jax
import jax.numpy as jnp
from jax import lax
from jax.experimental import pallas as pl
from jax.experimental.pallas import tpu as pltpu
from jax.sharding import PartitionSpec as P

adapter_scale = 2.0
f32, bf16, i32 = jnp.float32, jnp.bfloat16, jnp.int32
MIB = 1 << 20
TOKEN_LIMIT = 16 * MIB


def block_facts(tokens_per_job, block_ids, block_rows):
    job_total = tokens_per_job.shape[0]
    blocks = (tokens_per_job + (block_rows - 1)) // block_rows
    block_ends = jnp.cumsum(blocks, dtype=jnp.int32)
    starts = block_ends - blocks
    job_index = jnp.sum(
        (block_ends[None, :] <= block_ids[:, None]).astype(jnp.int32), axis=1, dtype=jnp.int32
    )
    chosen = job_index[:, None] == jnp.arange(job_total, dtype=jnp.int32)[None, :]
    job_count = jnp.sum(jnp.where(chosen, tokens_per_job[None, :], 0), axis=1, dtype=jnp.int32)
    first_block = jnp.sum(jnp.where(chosen, starts[None, :], 0), axis=1, dtype=jnp.int32)
    valid_rows = jnp.clip(job_count - block_rows * (block_ids - first_block), 0, block_rows)
    return job_index, valid_rows


def shifted(values, axis, count, step):
    if step % count == 0:
        return values
    return lax.ppermute(values, axis, [(i, (i + step) % count) for i in range(count)])


def gather_shifts(values, axis, count):
    return [shifted(values, axis, count, d) for d in range(count)]


def dot(a, b, dims, precision=None):
    return lax.dot_general(a, b, (dims, ((), ())), precision=precision, preferred_element_type=f32)


def tie(*values):
    return lax.optimization_barrier(values)


class Sizes:
    def __init__(self, nd, nt, ns, np_, blocks, halved, width, heads, jobs_dev, rank, columns):
        self.nd, self.nt, self.ns, self.np_ = nd, nt, ns, np_
        self.blocks, self.halved, self.width, self.heads = blocks, halved, width, heads
        self.jobs, self.jobs_dev, self.rank, self.columns = nd * jobs_dev, jobs_dev, rank, columns
        self.wide = self.jobs * rank
        self.rows = blocks * halved
        self.cap = -(-blocks // nd)
        self.slots = nd * self.cap
        self.nq = np_ * ns
        self.fq = width // self.nq
        self.per_head = nd // nt
        at, self.at = 0, {}
        for name, count in (
            ("out_pos", self.slots), ("in_pos", self.slots), ("out_fill", self.slots), ("in_fill", self.slots),
            ("out_rel", blocks), ("in_rel", blocks), ("out_valid", blocks), ("in_valid", blocks),
            ("quarter", self.nq), ("shard", nd), ("head", self.per_head),
            ("pick", self.per_head * nt),
        ):
            self.at[name] = at
            at += count

    def get(self, ref, name, index):
        return ref[self.at[name] + index]


def call(kernel, name, grid, scalars, inputs, in_specs, out_shape, out_specs, flops, moved, limit, scratch=(), alias=None):
    return pl.pallas_call(
        kernel,
        out_shape=out_shape,
        grid_spec=pltpu.PrefetchScalarGridSpec(
            num_scalar_prefetch=1, grid=grid, in_specs=in_specs, out_specs=out_specs, scratch_shapes=list(scratch)
        ),
        input_output_aliases=alias or {},
        compiler_params=pltpu.CompilerParams(vmem_limit_bytes=limit),
        cost_estimate=pl.CostEstimate(flops=flops, bytes_accessed=moved, transcendentals=0),
        name=name,
    )(scalars, *inputs)


ANY = pl.BlockSpec(memory_space=pl.ANY)


def whole(x):
    return pl.BlockSpec(x.shape, lambda *_: (0,) * len(x.shape))


def rows_of(index, z):
    return pl.ds(pl.multiple_of(index * z.halved, z.halved), z.halved)


def row_mask(valid, z, lanes):
    return lax.broadcasted_iota(i32, (z.halved, lanes), 0) < valid


def widen(values, rel, unfold, job_of, z):
    wide = dot(values, unfold, ((1,), (0,)))
    return jnp.where(job_of == rel, wide, 0.0).astype(bf16)


def products_kernel(z, n, sc, tokens, grad, maps, fold, job_of, out, held, sems):
    many = z.blocks // n
    copies = [
        pltpu.make_async_copy(tokens.at[pl.ds(k * n * z.halved, n * z.halved), :], held.at[k], sems.at[k])
        for k in range(many)
    ]
    for copy in copies:
        copy.start()
    back = dot(grad[...], maps[:, z.width :], ((1,), (1,)))
    for block in range(z.blocks):
        own = slice(block * z.halved, (block + 1) * z.halved)
        picked = jnp.where(job_of[...] == z.get(sc, "in_rel", block), back[own], 0.0)
        picked = jnp.where(row_mask(z.get(sc, "in_valid", block), z, z.wide), picked, 0.0)
        out[own, z.rank :] = dot(picked, fold[...], ((1,), (0,)), lax.Precision.HIGHEST).astype(bf16)
    for k in range(many):
        copies[k].wait()
        down = dot(held[k], maps[:, : z.width], ((1,), (1,)))
        for r in range(n):
            block = k * n + r
            own = slice(block * z.halved, (block + 1) * z.halved)
            mine = slice(r * z.halved, (r + 1) * z.halved)
            picked = jnp.where(job_of[...] == z.get(sc, "out_rel", block), down[mine], 0.0)
            out[own, : z.rank] = dot(picked, fold[...], ((1,), (0,)), lax.Precision.HIGHEST).astype(bf16)


def products(z, sc, tokens, grad, maps, fold, job_of):
    n = 2
    shape = jax.ShapeDtypeStruct((z.rows, 2 * z.rank), bf16)
    return call(
        functools.partial(products_kernel, z, n), "adapter_products", (1,), sc,
        (tokens, grad, maps, fold, job_of),
        [ANY, whole(grad), whole(maps), whole(fold), whole(job_of)],
        shape, whole(shape), 1000, 1000, TOKEN_LIMIT,
        scratch=(
            pltpu.VMEM((z.blocks // n, n * z.halved, z.width), bf16),
            pltpu.SemaphoreType.DMA((z.blocks // n,)),
        ),
    )


def sums_kernel(z, sc, *refs):
    parts, outs = refs[: z.nt], refs[z.nt :]
    sums, pays = outs[0], outs[1:]
    total = parts[0][...].astype(f32)
    for part in parts[1:]:
        total = total + part[...].astype(f32)
    sums[...] = total.astype(bf16)
    for d in range(z.nd):
        back = (z.nd - d) % z.nd
        for r in range(z.cap):
            own = slice(r * z.halved, (r + 1) * z.halved)
            picked = sums[rows_of(z.get(sc, "out_pos", d * z.cap + r), z), : z.rank]
            pays[d][own, : z.rank] = jnp.where(z.get(sc, "out_fill", d * z.cap + r) > 0, picked, 0)
            picked = sums[rows_of(z.get(sc, "in_pos", back * z.cap + r), z), z.rank :]
            pays[d][own, z.rank :] = jnp.where(z.get(sc, "in_fill", back * z.cap + r) > 0, picked, 0)


def sums_of(z, sc, parts):
    shapes = [jax.ShapeDtypeStruct((z.rows, 2 * z.rank), bf16)]
    shapes += [jax.ShapeDtypeStruct((z.cap * z.halved, 2 * z.rank), bf16)] * z.nd
    return call(
        functools.partial(sums_kernel, z), "adapter_sums", (1,), sc, parts, [whole(x) for x in parts],
        tuple(shapes), tuple(whole(x) for x in shapes), 1000, 1000, 8 * MIB,
    )


def table_kernel(z, tiles, sc, tokens, grad, unfold, job_of, *refs):
    got, (mine, theirs, back, down, back_t, down_t, held, sems) = refs[: z.nd], refs[z.nd :]
    half = mine.shape[0]
    part = z.width // tiles
    copies = [
        pltpu.make_async_copy(tokens.at[:, pl.ds(k * part, part)], held.at[k], sems.at[k]) for k in range(tiles)
    ]
    for copy in copies:
        copy.start()
    for d in range(z.nd):
        for r in range(z.cap):
            slot = d * z.cap + r
            own = slice(r * z.halved, (r + 1) * z.halved)

            @pl.when(z.get(sc, "out_fill", slot) > 0)
            def _():
                at = z.get(sc, "out_pos", slot)
                values = got[(z.nd - d) % z.nd][own, z.rank :]
                back[rows_of(at, z), :] = widen(values, z.get(sc, "out_rel", at), unfold[...], job_of[...], z)

            @pl.when(z.get(sc, "in_fill", slot) > 0)
            def _():
                at = z.get(sc, "in_pos", slot)
                values = widen(got[d][own, : z.rank], z.get(sc, "in_rel", at), unfold[...], job_of[...], z)
                mask = row_mask(z.get(sc, "in_valid", at), z, z.wide)
                down[rows_of(at, z), :] = jnp.where(mask, values, 0).astype(bf16)

    same = lax.broadcasted_iota(i32, (z.rows, z.rows), 0) == lax.broadcasted_iota(i32, (z.rows, z.rows), 1)
    unit = jnp.where(same, 1.0, 0.0).astype(bf16)
    back_t[...] = dot(back[...], unit, ((0,), (0,))).astype(bf16)
    down_t[...] = dot(down[...], unit, ((0,), (0,))).astype(bf16)
    total = dot(down_t[...], grad[...], ((1,), (0,)))
    mine[:, z.width :] = total[:half]
    theirs[:, z.width :] = total[half:].astype(bf16)
    for k in range(tiles):
        copies[k].wait()
        total = dot(back_t[...], held[k], ((1,), (0,)))
        mine[:, k * part : (k + 1) * part] = total[:half]
        theirs[:, k * part : (k + 1) * part] = total[half:].astype(bf16)


def tables_of(z, sc, tokens, grad, unfold, job_of, got):
    tiles = 4
    shape = jax.ShapeDtypeStruct((z.wide // z.ns, z.width + z.heads), f32)
    sent = jax.ShapeDtypeStruct(shape.shape, bf16)
    return call(
        functools.partial(table_kernel, z, tiles), "job_tables", (1,), sc,
        (tokens, grad, unfold, job_of, *got),
        [ANY, whole(grad), whole(unfold), whole(job_of)] + [whole(x) for x in got],
        (shape, sent), (whole(shape), whole(sent)), 1000, 1000, TOKEN_LIMIT,
        scratch=(pltpu.VMEM((z.rows, z.wide), bf16),) * 2
        + (pltpu.VMEM((z.wide, z.rows), bf16),) * 2
        + (pltpu.VMEM((tiles, z.rows, z.width // tiles), bf16), pltpu.SemaphoreType.DMA((tiles,))),
    )


def layer_kernel(z, sc, sums, maps, unfold, job_of, *refs):
    m = z.per_head
    given, (outs, frozen) = refs[: m * z.nt], (refs[m * z.nt : -1], refs[-1])
    for j in range(m):
        total = given[j][...].astype(f32)
        for d in range(1, z.nt):
            total = total + given[d * m + j][...].astype(f32)
        for i in range(m):

            @pl.when(z.get(sc, "head", j) == i)
            def _():
                frozen[:, i * z.columns : (i + 1) * z.columns] = total

    for d in range(z.nd):
        for r in range(z.cap):
            slot = d * z.cap + r
            at = z.get(sc, "out_pos", slot)
            valid = jnp.where(z.get(sc, "out_fill", slot) > 0, z.get(sc, "out_valid", at), 0)
            wide = widen(sums[rows_of(at, z), : z.rank], z.get(sc, "out_rel", at), unfold[...], job_of[...], z)
            adapter = dot(wide, maps[...], ((1,), (0,)))
            layer = frozen[rows_of(at, z), :] + adapter_scale * adapter
            layer = jnp.where(row_mask(valid, z, z.heads), layer, 0.0)
            outs[d][r * z.halved : (r + 1) * z.halved, :] = layer.astype(bf16)


def layer_of(z, sc, sums, maps, unfold, job_of, given):
    shapes = [jax.ShapeDtypeStruct((z.cap * z.halved, z.heads), bf16)] * z.nd
    at = z.width // z.heads
    return call(
        functools.partial(layer_kernel, z), "layer", (1,), sc, (sums, maps, unfold, job_of, *given),
        [whole(sums), pl.BlockSpec((z.wide, z.heads), lambda i, _: (0, at)), whole(unfold), whole(job_of)]
        + [whole(x) for x in given],
        tuple(shapes), tuple(whole(x) for x in shapes),
        2 * z.rows * z.wide * z.heads, 6 * z.rows * z.heads, 12 * MIB,
        scratch=(pltpu.VMEM((z.rows, z.heads), f32),),
    )


def place_kernel(z, sc, *refs):
    got, out = refs[: z.nd], refs[z.nd]
    for d in range(z.nd):
        for r in range(z.cap):
            slot = d * z.cap + r

            @pl.when(z.get(sc, "in_fill", slot) > 0)
            def _():
                out[rows_of(z.get(sc, "in_pos", slot), z), :] = got[d][r * z.halved : (r + 1) * z.halved, :]


def place(z, sc, got):
    shape = jax.ShapeDtypeStruct((z.rows, z.heads), bf16)
    return call(
        functools.partial(place_kernel, z), "place", (1,), sc, got, [whole(x) for x in got],
        shape, whole(shape), 1000, 4 * z.rows * z.heads, 8 * MIB,
    )


def gradient_kernel(z, count, per, aliased, sc, maps, sums, unfold, job_of, *refs):
    grads, refs = refs[: z.nt], refs[z.nt :]
    pieces, refs = refs[: z.nd * count], refs[z.nd * count :]
    out, grad, back = refs[1:] if aliased else refs
    step = pl.program_id(0)
    m = z.per_head

    @pl.when(step == 0)
    def _():
        for v in range(z.nt * m):
            grad[v] = grads[v // m][:, v % m * z.columns : (v % m + 1) * z.columns]
        for b in range(z.blocks):
            own = slice(b * z.halved, (b + 1) * z.halved)
            back[own, :] = widen(sums[own, z.rank :], z.get(sc, "in_rel", b), unfold[...], job_of[...], z)

    for k in range(count):

        @pl.when(step // per == k)
        def _():
            total = adapter_scale * dot(back[...], maps[...], ((1,), (0,)))
            for d in range(z.nd):
                total = total + dot(grad[z.get(sc, "shard", d)], pieces[d * count + k][...], ((1,), (1,)))
            for b in range(z.blocks):
                own = slice(b * z.halved, (b + 1) * z.halved)
                mask = row_mask(z.get(sc, "in_valid", b), z, total.shape[1])
                out[own, :] = jnp.where(mask, total[own], 0.0).astype(bf16)


def token_gradient_of(z, sc, grads, maps, sums, unfold, job_of, piece_list, quarters, before):
    tile = min(512, z.fq)
    per = z.fq // tile
    at = z.at["quarter"]
    first, count = quarters[0], len(quarters)
    block = lambda i, q: (0, q[at + first + i // per] * per + i % per)
    specs, flat = [], []
    for d in range(z.nd):
        for k, r in enumerate(quarters):
            inner = lambda i, k=k: jnp.clip(i - k * per, 0, per - 1)
            if d == 0:
                index = lambda i, q, r=r, inner=inner: (q[at + r] * per + inner(i), 0)
            else:
                index = lambda i, q, inner=inner: (inner(i), 0)
            specs.append(pl.BlockSpec((tile, z.columns), index))
            flat.append(piece_list[d][r])
    inputs = [maps, sums, unfold, job_of, *grads, *flat]
    in_specs = [pl.BlockSpec((z.wide, tile), block), whole(sums), whole(unfold), whole(job_of)]
    in_specs += [whole(x) for x in grads] + specs
    alias = None
    if before is not None:
        alias = {1 + len(inputs): 0}
        inputs.append(before)
        in_specs.append(pl.BlockSpec(memory_space=pl.ANY))
    return call(
        functools.partial(gradient_kernel, z, count, per, before is not None),
        "token_gradient_%d" % first, (count * per,), sc, inputs, in_specs,
        jax.ShapeDtypeStruct((z.rows, z.width), bf16), pl.BlockSpec((z.rows, tile), block),
        1000 if alias is None else 2 * z.rows * count * z.fq * (z.nd * z.columns + z.wide),
        1000 if alias is None else 2 * count * z.fq * (z.rows + z.nd * z.columns),
        (14 if alias is None else 61) * MIB,
        scratch=(pltpu.VMEM((z.nd, z.rows, z.columns), bf16), pltpu.VMEM((z.rows, z.wide), bf16)),
        alias=alias,
    )


def body(
    tokens,
    cotangent,
    frozen_value_weight,
    adapter_down,
    adapter_up,
    tokens_per_job,
    packed_block_slots,
):
    nd, nt, ns, np_ = (lax.axis_size(a) for a in ("dp", "tensor", "sub", "parts"))
    z, t, s, p = (lax.axis_index(a) for a in ("dp", "tensor", "sub", "parts"))
    blocks, halved, width = tokens.shape[1:]
    heads = cotangent.shape[3]
    jobs_dev, rank, _ = adapter_down.shape
    columns = frozen_value_weight.shape[1]
    zz = Sizes(nd, nt, ns, np_, blocks, halved, width, heads, jobs_dev, rank, columns)
    rows, r2, m, cap = zz.rows, rank // ns, zz.per_head, zz.cap
    own_tokens = tokens.reshape(rows, width)
    own_grad = cotangent.reshape(rows, heads)

    quarters = jnp.stack([(p - a) % np_ * ns + (s - b) % ns for a in range(np_) for b in range(ns)]).astype(i32)
    moving = lax.dynamic_slice_in_dim(frozen_value_weight, (p * ns + s) * zz.fq, zz.fq, axis=0)

    maps = jnp.concatenate([adapter_down, adapter_up], axis=2).reshape(jobs_dev, ns, r2, width + heads)
    maps = lax.dynamic_index_in_dim(maps, s, 1, keepdims=False)
    maps, moving = tie(maps, moving)
    rounds = [None, shifted(moving, "dp", nd, 1)]
    token_quarters = [lax.dynamic_slice_in_dim(own_tokens, quarters[r] * zz.fq, zz.fq, 1) for r in range(zz.nq)]
    def arrival(index):
        found = (z - index * m - jnp.arange(m, dtype=i32)) % nd
        place_of = jnp.sum((found[None, :] < found[:, None]).astype(i32), axis=1)
        match = place_of[None, :] == jnp.arange(m, dtype=i32)[:, None]
        return jnp.sum(jnp.where(match, found[None, :], 0), axis=1, dtype=i32)

    arrivals = [arrival((t + g) % nt) for g in range(nt)]
    chosen = [[[x[j] == k for k in range(nd)] for j in range(m)] for x in arrivals]
    scale = adapter_scale / lax.dynamic_slice_in_dim(tokens_per_job, z * jobs_dev, jobs_dev).astype(f32)
    maps, rounds[1], token_quarters, chosen, scale = tie(
        gather_shifts(maps, "dp", nd), rounds[1], token_quarters, chosen, scale
    )
    maps = jnp.concatenate(maps, axis=0).reshape(zz.jobs * r2, -1)
    maps = jnp.concatenate(gather_shifts(maps, "sub", ns), axis=0)
    grads = gather_shifts(own_grad, "tensor", nt)

    positions = jnp.arange(blocks, dtype=i32)
    dest = packed_block_slots // blocks
    same = dest[:, :, None] == dest[:, None, :]
    earlier = positions[None, None, :] < positions[None, :, None]
    send_rank = jnp.sum((same & earlier).astype(i32), axis=2, dtype=i32)
    flat_slots = packed_block_slots.reshape(-1)
    flat_ids = jnp.arange(nd * blocks, dtype=i32)
    slot_owner = flat_slots[None, :] == (z * blocks + positions)[:, None]
    block_ids = jnp.sum(jnp.where(slot_owner, flat_ids[None, :], 0), axis=1, dtype=i32)
    in_rank = jnp.sum(jnp.where(slot_owner, send_rank.reshape(-1)[None, :], 0), axis=1, dtype=i32)
    in_slot = (z - block_ids // blocks) % nd * cap + in_rank
    own_dest = lax.dynamic_index_in_dim(dest, z, 0, keepdims=False)
    own_rank = lax.dynamic_index_in_dim(send_rank, z, 0, keepdims=False)
    out_slot = (own_dest - z) % nd * cap + own_rank
    slot_range = jnp.arange(zz.slots, dtype=i32)

    def positions_of(slots):
        match = slots[None, :] == slot_range[:, None]
        return jnp.sum(jnp.where(match, positions[None, :], 0), axis=1, dtype=i32), jnp.any(match, axis=1)

    out_pos, out_fill = positions_of(out_slot)
    in_pos, in_fill = positions_of(in_slot)

    def facts(ids):
        job, valid = block_facts(tokens_per_job, ids, halved * ns)
        return (z - job // jobs_dev) % nd * jobs_dev + job % jobs_dev, valid - s * halved

    out_rel, out_valid = facts(z * blocks + positions)
    in_rel, in_valid = facts(block_ids)

    shard_of = (z - jnp.arange(nd, dtype=i32)) % nd
    shard_at = (t - shard_of // m) % nt * m + shard_of % m
    head_at = (z - arrivals[0]) % nd - t * m
    sc = jnp.concatenate(
        [
            x.astype(i32)
            for x in (out_pos, in_pos, out_fill, in_fill, out_rel, in_rel, out_valid, in_valid, quarters, shard_at, head_at, *arrivals)
        ]
    )
    column = jnp.arange(zz.wide, dtype=i32)
    job_of = (column // r2 % zz.jobs)[None, :]
    rank_of = column // (zz.jobs * r2) * r2 + column % r2
    unfold = (jnp.arange(rank, dtype=i32)[:, None] == rank_of[None, :]).astype(bf16)
    fold = unfold.astype(f32).T

    def product(pieces, first=0):
        return sum(dot(token_quarters[first + r], x, ((1,), (0,))) for r, x in enumerate(pieces))

    def spread_round(over_parts):
        return [x for y in over_parts for x in gather_shifts(y, "sub", ns)]

    last = nd - 1
    over = [None] * nd
    over[1] = gather_shifts(rounds[1], "parts", np_)
    for d in range(2, last):
        rounds.append(shifted(rounds[-1], "dp", nd, 1))
    swapped = gather_shifts(over[1][0], "sub", ns)
    maps, swapped = tie(maps, swapped)
    part = products(zz, sc, own_tokens, own_grad, maps, fold, job_of)
    parts = gather_shifts(part, "tensor", nt)
    late_weight, _ = tie(frozen_value_weight, part)
    base = [dot(own_tokens, late_weight, ((1,), (0,))).astype(bf16)]
    base[0], parts, grads = tie(base[0], parts, grads)
    sums, *pays = sums_of(zz, sc, parts)
    rounds[last - 1], over[1], sums = tie(rounds[last - 1], over[1], sums)

    end = shifted(rounds[last - 1], "dp", nd, 1)
    for d in range(2, last):
        over[d] = gather_shifts(rounds[d], "parts", np_)
    piece_list = [[frozen_value_weight] * zz.nq, swapped + spread_round(over[1][1:])]
    crossed = [gather_shifts(over[d][0], "sub", ns) for d in range(2, last)]
    piece_list[1], crossed = tie(piece_list[1], crossed)
    base.append(product(piece_list[1]).astype(bf16))
    base[1], end, over[2:last], pays = tie(base[1], end, over[2:last], pays)

    behind = gather_shifts(end, "parts", np_)
    got = [shifted(pays[d], "dp", nd, d) for d in range(nd)]
    piece_list += [crossed[d - 2] + spread_round(over[d][1:]) for d in range(2, last)]

    slots = []

    def finish(values):
        base.append(values.astype(bf16))
        due = len(base) - 1 - (nd - m)
        if due >= 0:
            made = []
            for g in range(nt):
                picked = base[-1]
                for k in range(due, len(base) - 1):
                    picked = jnp.where(chosen[g][due][k], base[k], picked)
                made.append(shifted(picked, "tensor", nt, g))
            slots.append(made)

    for d in range(2, last):
        finish(product(piece_list[d]))
    base[-1], got = tie(base[-1], got)
    mine, theirs = tables_of(zz, sc, own_tokens, own_grad, unfold, job_of, got)
    theirs = shifted(theirs, "sub", ns, 1)
    ahead = gather_shifts(end, "sub", ns)
    ahead, mine = tie(ahead, mine)
    begun = product(ahead)
    begun, behind, slots = tie(begun, behind, slots)
    tail = spread_round(behind[1:])
    piece_list.append(ahead + tail)
    finish(begun + product(tail, len(ahead)))
    base[-1], mine, theirs, grads = tie(base[-1], mine, theirs, grads)

    summed = (mine + theirs).reshape(nd, jobs_dev * r2, -1)
    sending = [summed[d].astype(bf16) for d in range(nd)]
    tables = [sending[0]] + [shifted(sending[d], "dp", nd, -d) for d in range(1, nd)]

    half = zz.nq // 2
    gradient = token_gradient_of(zz, sc, grads, maps, sums, unfold, job_of, piece_list, list(range(half)), None)
    given = [slots[j][d] for d in range(nt) for j in range(m)]
    gradient, given = tie(gradient, given)
    layer = layer_of(zz, sc, sums, maps, unfold, job_of, given)
    layer, gradient, tables = tie(layer, gradient, tables)
    landed = [shifted(layer[d], "dp", nd, d) for d in range(nd)]
    total = sum(x.astype(f32) for x in tables)
    total = total.reshape(jobs_dev, r2, -1) * scale[:, None, None]
    halves = gather_shifts(total, "sub", ns)
    gradient, halves = tie(gradient, halves)
    owned = jnp.concatenate(
        [sum(jnp.where((s - h) % ns == k, x, 0.0) for k, x in enumerate(halves)) for h in range(ns)], axis=1
    )
    grad_down, grad_up = owned[:, :, :width], owned[:, :, width:]
    gradient, grad_down, grad_up = tie(gradient, grad_down, grad_up)
    gradient = token_gradient_of(
        zz, sc, grads, maps, sums, unfold, job_of, piece_list, list(range(half, zz.nq)), gradient
    )
    gradient, grad_down, grad_up, landed = tie(gradient, grad_down, grad_up, landed)
    layer_output = place(zz, sc, landed)
    return (
        layer_output.reshape(1, blocks, halved, heads),
        gradient.reshape(1, blocks, halved, width),
        grad_down,
        grad_up,
    )


def solution(mesh):
    return jax.shard_map(
        body,
        mesh=mesh,
        in_specs=(
            P(("parts", "dp"), None, "sub", "tensor"),
            P(("parts", "dp"), None, "sub", "tensor"),
            P("tensor", "dp"),
            P(("parts", "dp"), None, "tensor"),
            P(("parts", "dp"), None, "tensor"),
            P("parts"),
            P("parts", None),
        ),
        out_specs=(
            P(("parts", "dp"), None, "sub", "tensor"),
            P(("parts", "dp"), None, "sub", "tensor"),
            P(("parts", "dp"), None, "tensor"),
            P(("parts", "dp"), None, "tensor"),
        ),
        check_vma=False,
    )
```

```python
import functools

import jax
import jax.numpy as jnp
from jax import lax
from jax.experimental import pallas as pl
from jax.experimental.pallas import tpu as pltpu
from jax.sharding import PartitionSpec as P

adapter_scale = 2.0
f32, bf16, i32 = jnp.float32, jnp.bfloat16, jnp.int32
MIB = 1 << 20
TOKEN_LIMIT = 16 * MIB


def block_facts(tokens_per_job, block_ids, block_rows):
    job_total = tokens_per_job.shape[0]
    blocks = (tokens_per_job + (block_rows - 1)) // block_rows
    block_ends = jnp.cumsum(blocks, dtype=jnp.int32)
    starts = block_ends - blocks
    job_index = jnp.sum(
        (block_ends[None, :] <= block_ids[:, None]).astype(jnp.int32), axis=1, dtype=jnp.int32
    )
    chosen = job_index[:, None] == jnp.arange(job_total, dtype=jnp.int32)[None, :]
    job_count = jnp.sum(jnp.where(chosen, tokens_per_job[None, :], 0), axis=1, dtype=jnp.int32)
    first_block = jnp.sum(jnp.where(chosen, starts[None, :], 0), axis=1, dtype=jnp.int32)
    valid_rows = jnp.clip(job_count - block_rows * (block_ids - first_block), 0, block_rows)
    return job_index, valid_rows


def shifted(values, axis, count, step):
    if step % count == 0:
        return values
    return lax.ppermute(values, axis, [(i, (i + step) % count) for i in range(count)])


def gather_shifts(values, axis, count):
    return [shifted(values, axis, count, d) for d in range(count)]


def dot(a, b, dims, precision=None):
    return lax.dot_general(a, b, (dims, ((), ())), precision=precision, preferred_element_type=f32)


def tie(*values):
    return lax.optimization_barrier(values)


class Sizes:
    def __init__(self, nd, nt, ns, np_, blocks, halved, width, heads, jobs_dev, rank, columns):
        self.nd, self.nt, self.ns, self.np_ = nd, nt, ns, np_
        self.blocks, self.halved, self.width, self.heads = blocks, halved, width, heads
        self.jobs, self.jobs_dev, self.rank, self.columns = nd * jobs_dev, jobs_dev, rank, columns
        self.wide = self.jobs * rank
        self.rows = blocks * halved
        self.cap = -(-blocks // nd)
        self.slots = nd * self.cap
        self.nq = np_ * ns
        self.fq = width // self.nq
        self.per_head = nd // nt
        at, self.at = 0, {}
        for name, count in (
            ("out_pos", self.slots), ("in_pos", self.slots), ("out_fill", self.slots), ("in_fill", self.slots),
            ("out_rel", blocks), ("in_rel", blocks), ("out_valid", blocks), ("in_valid", blocks),
            ("quarter", self.nq), ("shard", nd), ("head", self.per_head),
            ("pick", self.per_head * nt),
        ):
            self.at[name] = at
            at += count

    def get(self, ref, name, index):
        return ref[self.at[name] + index]


def call(kernel, name, grid, scalars, inputs, in_specs, out_shape, out_specs, flops, moved, limit, scratch=(), alias=None):
    return pl.pallas_call(
        kernel,
        out_shape=out_shape,
        grid_spec=pltpu.PrefetchScalarGridSpec(
            num_scalar_prefetch=1, grid=grid, in_specs=in_specs, out_specs=out_specs, scratch_shapes=list(scratch)
        ),
        input_output_aliases=alias or {},
        compiler_params=pltpu.CompilerParams(vmem_limit_bytes=limit),
        cost_estimate=pl.CostEstimate(flops=flops, bytes_accessed=moved, transcendentals=0),
        name=name,
    )(scalars, *inputs)


ANY = pl.BlockSpec(memory_space=pl.ANY)


def whole(x):
    return pl.BlockSpec(x.shape, lambda *_: (0,) * len(x.shape))


def rows_of(index, z):
    return pl.ds(pl.multiple_of(index * z.halved, z.halved), z.halved)


def row_mask(valid, z, lanes):
    return lax.broadcasted_iota(i32, (z.halved, lanes), 0) < valid


def widen(values, rel, unfold, job_of, z):
    wide = dot(values, unfold, ((1,), (0,)))
    return jnp.where(job_of == rel, wide, 0.0).astype(bf16)


def products_kernel(z, n, sc, tokens, grad, maps, fold, job_of, out, held, sems):
    many = z.blocks // n
    copies = [
        pltpu.make_async_copy(tokens.at[pl.ds(k * n * z.halved, n * z.halved), :], held.at[k], sems.at[k])
        for k in range(many)
    ]
    for copy in copies:
        copy.start()
    back = dot(grad[...], maps[:, z.width :], ((1,), (1,)))
    for block in range(z.blocks):
        own = slice(block * z.halved, (block + 1) * z.halved)
        picked = jnp.where(job_of[...] == z.get(sc, "in_rel", block), back[own], 0.0)
        picked = jnp.where(row_mask(z.get(sc, "in_valid", block), z, z.wide), picked, 0.0)
        out[own, z.rank :] = dot(picked, fold[...], ((1,), (0,)), lax.Precision.HIGHEST).astype(bf16)
    for k in range(many):
        copies[k].wait()
        down = dot(held[k], maps[:, : z.width], ((1,), (1,)))
        for r in range(n):
            block = k * n + r
            own = slice(block * z.halved, (block + 1) * z.halved)
            mine = slice(r * z.halved, (r + 1) * z.halved)
            picked = jnp.where(job_of[...] == z.get(sc, "out_rel", block), down[mine], 0.0)
            out[own, : z.rank] = dot(picked, fold[...], ((1,), (0,)), lax.Precision.HIGHEST).astype(bf16)


def products(z, sc, tokens, grad, maps, fold, job_of):
    n = 2
    shape = jax.ShapeDtypeStruct((z.rows, 2 * z.rank), bf16)
    return call(
        functools.partial(products_kernel, z, n), "adapter_products", (1,), sc,
        (tokens, grad, maps, fold, job_of),
        [ANY, whole(grad), whole(maps), whole(fold), whole(job_of)],
        shape, whole(shape), 1000, 1000, TOKEN_LIMIT,
        scratch=(
            pltpu.VMEM((z.blocks // n, n * z.halved, z.width), bf16),
            pltpu.SemaphoreType.DMA((z.blocks // n,)),
        ),
    )


def sums_kernel(z, sc, *refs):
    parts, outs = refs[: z.nt], refs[z.nt :]
    sums, pays = outs[0], outs[1:]
    total = parts[0][...].astype(f32)
    for part in parts[1:]:
        total = total + part[...].astype(f32)
    sums[...] = total.astype(bf16)
    for d in range(z.nd):
        back = (z.nd - d) % z.nd
        for r in range(z.cap):
            own = slice(r * z.halved, (r + 1) * z.halved)
            picked = sums[rows_of(z.get(sc, "out_pos", d * z.cap + r), z), : z.rank]
            pays[d][own, : z.rank] = jnp.where(z.get(sc, "out_fill", d * z.cap + r) > 0, picked, 0)
            picked = sums[rows_of(z.get(sc, "in_pos", back * z.cap + r), z), z.rank :]
            pays[d][own, z.rank :] = jnp.where(z.get(sc, "in_fill", back * z.cap + r) > 0, picked, 0)


def sums_of(z, sc, parts):
    shapes = [jax.ShapeDtypeStruct((z.rows, 2 * z.rank), bf16)]
    shapes += [jax.ShapeDtypeStruct((z.cap * z.halved, 2 * z.rank), bf16)] * z.nd
    return call(
        functools.partial(sums_kernel, z), "adapter_sums", (1,), sc, parts, [whole(x) for x in parts],
        tuple(shapes), tuple(whole(x) for x in shapes), 1000, 1000, 8 * MIB,
    )


def table_kernel(z, tiles, sc, tokens, grad, unfold, job_of, *refs):
    got, (mine, theirs, back, down, back_t, down_t, held, sems) = refs[: z.nd], refs[z.nd :]
    half = mine.shape[0]
    part = z.width // tiles
    copies = [
        pltpu.make_async_copy(tokens.at[:, pl.ds(k * part, part)], held.at[k], sems.at[k]) for k in range(tiles)
    ]
    for copy in copies:
        copy.start()
    for d in range(z.nd):
        for r in range(z.cap):
            slot = d * z.cap + r
            own = slice(r * z.halved, (r + 1) * z.halved)

            @pl.when(z.get(sc, "out_fill", slot) > 0)
            def _():
                at = z.get(sc, "out_pos", slot)
                values = got[(z.nd - d) % z.nd][own, z.rank :]
                back[rows_of(at, z), :] = widen(values, z.get(sc, "out_rel", at), unfold[...], job_of[...], z)

            @pl.when(z.get(sc, "in_fill", slot) > 0)
            def _():
                at = z.get(sc, "in_pos", slot)
                values = widen(got[d][own, : z.rank], z.get(sc, "in_rel", at), unfold[...], job_of[...], z)
                mask = row_mask(z.get(sc, "in_valid", at), z, z.wide)
                down[rows_of(at, z), :] = jnp.where(mask, values, 0).astype(bf16)

    same = lax.broadcasted_iota(i32, (z.rows, z.rows), 0) == lax.broadcasted_iota(i32, (z.rows, z.rows), 1)
    unit = jnp.where(same, 1.0, 0.0).astype(bf16)
    back_t[...] = dot(back[...], unit, ((0,), (0,))).astype(bf16)
    down_t[...] = dot(down[...], unit, ((0,), (0,))).astype(bf16)
    total = dot(down_t[...], grad[...], ((1,), (0,)))
    mine[:, z.width :] = total[:half]
    theirs[:, z.width :] = total[half:].astype(bf16)
    for k in range(tiles):
        copies[k].wait()
        total = dot(back_t[...], held[k], ((1,), (0,)))
        mine[:, k * part : (k + 1) * part] = total[:half]
        theirs[:, k * part : (k + 1) * part] = total[half:].astype(bf16)


def tables_of(z, sc, tokens, grad, unfold, job_of, got):
    tiles = 4
    shape = jax.ShapeDtypeStruct((z.wide // z.ns, z.width + z.heads), f32)
    sent = jax.ShapeDtypeStruct(shape.shape, bf16)
    return call(
        functools.partial(table_kernel, z, tiles), "job_tables", (1,), sc,
        (tokens, grad, unfold, job_of, *got),
        [ANY, whole(grad), whole(unfold), whole(job_of)] + [whole(x) for x in got],
        (shape, sent), (whole(shape), whole(sent)), 1000, 1000, TOKEN_LIMIT,
        scratch=(pltpu.VMEM((z.rows, z.wide), bf16),) * 2
        + (pltpu.VMEM((z.wide, z.rows), bf16),) * 2
        + (pltpu.VMEM((tiles, z.rows, z.width // tiles), bf16), pltpu.SemaphoreType.DMA((tiles,))),
    )


def layer_kernel(z, sc, sums, maps, unfold, job_of, *refs):
    m = z.per_head
    given, (outs, frozen) = refs[: m * z.nt], (refs[m * z.nt : -1], refs[-1])
    for j in range(m):
        total = given[j][...].astype(f32)
        for d in range(1, z.nt):
            total = total + given[d * m + j][...].astype(f32)
        for i in range(m):

            @pl.when(z.get(sc, "head", j) == i)
            def _():
                frozen[:, i * z.columns : (i + 1) * z.columns] = total

    for d in range(z.nd):
        for r in range(z.cap):
            slot = d * z.cap + r
            at = z.get(sc, "out_pos", slot)
            valid = jnp.where(z.get(sc, "out_fill", slot) > 0, z.get(sc, "out_valid", at), 0)
            wide = widen(sums[rows_of(at, z), : z.rank], z.get(sc, "out_rel", at), unfold[...], job_of[...], z)
            adapter = dot(wide, maps[...], ((1,), (0,)))
            layer = frozen[rows_of(at, z), :] + adapter_scale * adapter
            layer = jnp.where(row_mask(valid, z, z.heads), layer, 0.0)
            outs[d][r * z.halved : (r + 1) * z.halved, :] = layer.astype(bf16)


def layer_of(z, sc, sums, maps, unfold, job_of, given):
    shapes = [jax.ShapeDtypeStruct((z.cap * z.halved, z.heads), bf16)] * z.nd
    at = z.width // z.heads
    return call(
        functools.partial(layer_kernel, z), "layer", (1,), sc, (sums, maps, unfold, job_of, *given),
        [whole(sums), pl.BlockSpec((z.wide, z.heads), lambda i, _: (0, at)), whole(unfold), whole(job_of)]
        + [whole(x) for x in given],
        tuple(shapes), tuple(whole(x) for x in shapes),
        2 * z.rows * z.wide * z.heads, 6 * z.rows * z.heads, 12 * MIB,
        scratch=(pltpu.VMEM((z.rows, z.heads), f32),),
    )


def place_kernel(z, sc, *refs):
    got, out = refs[: z.nd], refs[z.nd]
    for d in range(z.nd):
        for r in range(z.cap):
            slot = d * z.cap + r

            @pl.when(z.get(sc, "in_fill", slot) > 0)
            def _():
                out[rows_of(z.get(sc, "in_pos", slot), z), :] = got[d][r * z.halved : (r + 1) * z.halved, :]


def place(z, sc, got):
    shape = jax.ShapeDtypeStruct((z.rows, z.heads), bf16)
    return call(
        functools.partial(place_kernel, z), "place", (1,), sc, got, [whole(x) for x in got],
        shape, whole(shape), 1000, 4 * z.rows * z.heads, 8 * MIB,
    )


def gradient_kernel(z, count, per, aliased, sc, maps, sums, unfold, job_of, *refs):
    grads, refs = refs[: z.nt], refs[z.nt :]
    pieces, refs = refs[: z.nd * count], refs[z.nd * count :]
    out, grad, back = refs[1:] if aliased else refs
    step = pl.program_id(0)
    m = z.per_head

    @pl.when(step == 0)
    def _():
        for v in range(z.nt * m):
            grad[v] = grads[v // m][:, v % m * z.columns : (v % m + 1) * z.columns]
        for b in range(z.blocks):
            own = slice(b * z.halved, (b + 1) * z.halved)
            back[own, :] = widen(sums[own, z.rank :], z.get(sc, "in_rel", b), unfold[...], job_of[...], z)

    for k in range(count):

        @pl.when(step // per == k)
        def _():
            total = adapter_scale * dot(back[...], maps[...], ((1,), (0,)))
            for d in range(z.nd):
                total = total + dot(grad[z.get(sc, "shard", d)], pieces[d * count + k][...], ((1,), (1,)))
            for b in range(z.blocks):
                own = slice(b * z.halved, (b + 1) * z.halved)
                mask = row_mask(z.get(sc, "in_valid", b), z, total.shape[1])
                out[own, :] = jnp.where(mask, total[own], 0.0).astype(bf16)


def token_gradient_of(z, sc, grads, maps, sums, unfold, job_of, piece_list, quarters, before):
    tile = min(256, z.fq)
    per = z.fq // tile
    at = z.at["quarter"]
    first, count = quarters[0], len(quarters)
    block = lambda i, q: (0, q[at + first + i // per] * per + i % per)
    specs, flat = [], []
    for d in range(z.nd):
        for k, r in enumerate(quarters):
            inner = lambda i, k=k: jnp.clip(i - k * per, 0, per - 1)
            if d == 0:
                index = lambda i, q, r=r, inner=inner: (q[at + r] * per + inner(i), 0)
            else:
                index = lambda i, q, inner=inner: (inner(i), 0)
            specs.append(pl.BlockSpec((tile, z.columns), index))
            flat.append(piece_list[d][r])
    inputs = [maps, sums, unfold, job_of, *grads, *flat]
    in_specs = [pl.BlockSpec((z.wide, tile), block), whole(sums), whole(unfold), whole(job_of)]
    in_specs += [whole(x) for x in grads] + specs
    alias = None
    if before is not None:
        alias = {1 + len(inputs): 0}
        inputs.append(before)
        in_specs.append(pl.BlockSpec(memory_space=pl.ANY))
    return call(
        functools.partial(gradient_kernel, z, count, per, before is not None),
        "token_gradient_%d" % first, (count * per,), sc, inputs, in_specs,
        jax.ShapeDtypeStruct((z.rows, z.width), bf16), pl.BlockSpec((z.rows, tile), block),
        1000 if alias is None else 2 * z.rows * count * z.fq * (z.nd * z.columns + z.wide),
        1000 if alias is None else 2 * count * z.fq * (z.rows + z.nd * z.columns),
        (14 if alias is None else 61) * MIB,
        scratch=(pltpu.VMEM((z.nd, z.rows, z.columns), bf16), pltpu.VMEM((z.rows, z.wide), bf16)),
        alias=alias,
    )


def body(
    tokens,
    cotangent,
    frozen_value_weight,
    adapter_down,
    adapter_up,
    tokens_per_job,
    packed_block_slots,
):
    nd, nt, ns, np_ = (lax.axis_size(a) for a in ("dp", "tensor", "sub", "parts"))
    z, t, s, p = (lax.axis_index(a) for a in ("dp", "tensor", "sub", "parts"))
    blocks, halved, width = tokens.shape[1:]
    heads = cotangent.shape[3]
    jobs_dev, rank, _ = adapter_down.shape
    columns = frozen_value_weight.shape[1]
    zz = Sizes(nd, nt, ns, np_, blocks, halved, width, heads, jobs_dev, rank, columns)
    rows, r2, m, cap = zz.rows, rank // ns, zz.per_head, zz.cap
    own_tokens = tokens.reshape(rows, width)
    own_grad = cotangent.reshape(rows, heads)

    quarters = jnp.stack([(p - a) % np_ * ns + (s - b) % ns for a in range(np_) for b in range(ns)]).astype(i32)
    moving = lax.dynamic_slice_in_dim(frozen_value_weight, (p * ns + s) * zz.fq, zz.fq, axis=0)

    maps = jnp.concatenate([adapter_down, adapter_up], axis=2).reshape(jobs_dev, ns, r2, width + heads)
    maps = lax.dynamic_index_in_dim(maps, s, 1, keepdims=False)
    maps, moving = tie(maps, moving)
    rounds = [None, shifted(moving, "dp", nd, 1)]
    token_quarters = [lax.dynamic_slice_in_dim(own_tokens, quarters[r] * zz.fq, zz.fq, 1) for r in range(zz.nq)]
    def arrival(index):
        found = (z - index * m - jnp.arange(m, dtype=i32)) % nd
        place_of = jnp.sum((found[None, :] < found[:, None]).astype(i32), axis=1)
        match = place_of[None, :] == jnp.arange(m, dtype=i32)[:, None]
        return jnp.sum(jnp.where(match, found[None, :], 0), axis=1, dtype=i32)

    arrivals = [arrival((t + g) % nt) for g in range(nt)]
    chosen = [[[x[j] == k for k in range(nd)] for j in range(m)] for x in arrivals]
    scale = adapter_scale / lax.dynamic_slice_in_dim(tokens_per_job, z * jobs_dev, jobs_dev).astype(f32)
    maps, rounds[1], token_quarters, chosen, scale = tie(
        gather_shifts(maps, "dp", nd), rounds[1], token_quarters, chosen, scale
    )
    maps = jnp.concatenate(maps, axis=0).reshape(zz.jobs * r2, -1)
    maps = jnp.concatenate(gather_shifts(maps, "sub", ns), axis=0)
    grads = gather_shifts(own_grad, "tensor", nt)

    positions = jnp.arange(blocks, dtype=i32)
    dest = packed_block_slots // blocks
    same = dest[:, :, None] == dest[:, None, :]
    earlier = positions[None, None, :] < positions[None, :, None]
    send_rank = jnp.sum((same & earlier).astype(i32), axis=2, dtype=i32)
    flat_slots = packed_block_slots.reshape(-1)
    flat_ids = jnp.arange(nd * blocks, dtype=i32)
    slot_owner = flat_slots[None, :] == (z * blocks + positions)[:, None]
    block_ids = jnp.sum(jnp.where(slot_owner, flat_ids[None, :], 0), axis=1, dtype=i32)
    in_rank = jnp.sum(jnp.where(slot_owner, send_rank.reshape(-1)[None, :], 0), axis=1, dtype=i32)
    in_slot = (z - block_ids // blocks) % nd * cap + in_rank
    own_dest = lax.dynamic_index_in_dim(dest, z, 0, keepdims=False)
    own_rank = lax.dynamic_index_in_dim(send_rank, z, 0, keepdims=False)
    out_slot = (own_dest - z) % nd * cap + own_rank
    slot_range = jnp.arange(zz.slots, dtype=i32)

    def positions_of(slots):
        match = slots[None, :] == slot_range[:, None]
        return jnp.sum(jnp.where(match, positions[None, :], 0), axis=1, dtype=i32), jnp.any(match, axis=1)

    out_pos, out_fill = positions_of(out_slot)
    in_pos, in_fill = positions_of(in_slot)

    def facts(ids):
        job, valid = block_facts(tokens_per_job, ids, halved * ns)
        return (z - job // jobs_dev) % nd * jobs_dev + job % jobs_dev, valid - s * halved

    out_rel, out_valid = facts(z * blocks + positions)
    in_rel, in_valid = facts(block_ids)

    shard_of = (z - jnp.arange(nd, dtype=i32)) % nd
    shard_at = (t - shard_of // m) % nt * m + shard_of % m
    head_at = (z - arrivals[0]) % nd - t * m
    sc = jnp.concatenate(
        [
            x.astype(i32)
            for x in (out_pos, in_pos, out_fill, in_fill, out_rel, in_rel, out_valid, in_valid, quarters, shard_at, head_at, *arrivals)
        ]
    )
    column = jnp.arange(zz.wide, dtype=i32)
    job_of = (column // r2 % zz.jobs)[None, :]
    rank_of = column // (zz.jobs * r2) * r2 + column % r2
    unfold = (jnp.arange(rank, dtype=i32)[:, None] == rank_of[None, :]).astype(bf16)
    fold = unfold.astype(f32).T

    def product(pieces, first=0):
        return sum(dot(token_quarters[first + r], x, ((1,), (0,))) for r, x in enumerate(pieces))

    def spread_round(over_parts):
        return [x for y in over_parts for x in gather_shifts(y, "sub", ns)]

    last = nd - 1
    over = [None] * nd
    over[1] = gather_shifts(rounds[1], "parts", np_)
    for d in range(2, last):
        rounds.append(shifted(rounds[-1], "dp", nd, 1))
    swapped = gather_shifts(over[1][0], "sub", ns)
    maps, swapped = tie(maps, swapped)
    part = products(zz, sc, own_tokens, own_grad, maps, fold, job_of)
    parts = gather_shifts(part, "tensor", nt)
    late_weight, _ = tie(frozen_value_weight, part)
    base = [dot(own_tokens, late_weight, ((1,), (0,))).astype(bf16)]
    base[0], parts, grads = tie(base[0], parts, grads)
    sums, *pays = sums_of(zz, sc, parts)
    rounds[last - 1], over[1], sums = tie(rounds[last - 1], over[1], sums)

    end = shifted(rounds[last - 1], "dp", nd, 1)
    for d in range(2, last):
        over[d] = gather_shifts(rounds[d], "parts", np_)
    piece_list = [[frozen_value_weight] * zz.nq, swapped + spread_round(over[1][1:])]
    crossed = [gather_shifts(over[d][0], "sub", ns) for d in range(2, last)]
    piece_list[1], crossed = tie(piece_list[1], crossed)
    base.append(product(piece_list[1]).astype(bf16))
    base[1], end, over[2:last], pays = tie(base[1], end, over[2:last], pays)

    behind = gather_shifts(end, "parts", np_)
    got = [shifted(pays[d], "dp", nd, d) for d in range(nd)]
    piece_list += [crossed[d - 2] + spread_round(over[d][1:]) for d in range(2, last)]

    slots = []

    def finish(values):
        base.append(values.astype(bf16))
        due = len(base) - 1 - (nd - m)
        if due >= 0:
            made = []
            for g in range(nt):
                picked = base[-1]
                for k in range(due, len(base) - 1):
                    picked = jnp.where(chosen[g][due][k], base[k], picked)
                made.append(shifted(picked, "tensor", nt, g))
            slots.append(made)

    for d in range(2, last):
        finish(product(piece_list[d]))
    base[-1], got = tie(base[-1], got)
    mine, theirs = tables_of(zz, sc, own_tokens, own_grad, unfold, job_of, got)
    theirs = shifted(theirs, "sub", ns, 1)
    ahead = gather_shifts(end, "sub", ns)
    ahead, mine = tie(ahead, mine)
    begun = product(ahead)
    begun, behind, slots = tie(begun, behind, slots)
    tail = spread_round(behind[1:])
    piece_list.append(ahead + tail)
    finish(begun + product(tail, len(ahead)))
    base[-1], mine, theirs, grads = tie(base[-1], mine, theirs, grads)

    summed = (mine + theirs).reshape(nd, jobs_dev * r2, -1)
    sending = [summed[d].astype(bf16) for d in range(nd)]
    tables = [sending[0]] + [shifted(sending[d], "dp", nd, -d) for d in range(1, nd)]

    half = zz.nq // 2
    gradient = token_gradient_of(zz, sc, grads, maps, sums, unfold, job_of, piece_list, list(range(half)), None)
    given = [slots[j][d] for d in range(nt) for j in range(m)]
    gradient, given = tie(gradient, given)
    layer = layer_of(zz, sc, sums, maps, unfold, job_of, given)
    layer, gradient, tables = tie(layer, gradient, tables)
    landed = [shifted(layer[d], "dp", nd, d) for d in range(nd)]
    total = sum(x.astype(f32) for x in tables)
    total = total.reshape(jobs_dev, r2, -1) * scale[:, None, None]
    halves = gather_shifts(total, "sub", ns)
    gradient, halves = tie(gradient, halves)
    owned = jnp.concatenate(
        [sum(jnp.where((s - h) % ns == k, x, 0.0) for k, x in enumerate(halves)) for h in range(ns)], axis=1
    )
    grad_down, grad_up = owned[:, :, :width], owned[:, :, width:]
    gradient, grad_down, grad_up = tie(gradient, grad_down, grad_up)
    gradient = token_gradient_of(
        zz, sc, grads, maps, sums, unfold, job_of, piece_list, list(range(half, zz.nq)), gradient
    )
    gradient, grad_down, grad_up, landed = tie(gradient, grad_down, grad_up, landed)
    layer_output = place(zz, sc, landed)
    return (
        layer_output.reshape(1, blocks, halved, heads),
        gradient.reshape(1, blocks, halved, width),
        grad_down,
        grad_up,
    )


def solution(mesh):
    return jax.shard_map(
        body,
        mesh=mesh,
        in_specs=(
            P(("parts", "dp"), None, "sub", "tensor"),
            P(("parts", "dp"), None, "sub", "tensor"),
            P("tensor", "dp"),
            P(("parts", "dp"), None, "tensor"),
            P(("parts", "dp"), None, "tensor"),
            P("parts"),
            P("parts", None),
        ),
        out_specs=(
            P(("parts", "dp"), None, "sub", "tensor"),
            P(("parts", "dp"), None, "sub", "tensor"),
            P(("parts", "dp"), None, "tensor"),
            P(("parts", "dp"), None, "tensor"),
        ),
        check_vma=False,
    )
```

```python
import functools

import jax
import jax.numpy as jnp
from jax import lax
from jax.experimental import pallas as pl
from jax.experimental.pallas import tpu as pltpu
from jax.sharding import PartitionSpec as P

adapter_scale = 2.0
f32, bf16, i32 = jnp.float32, jnp.bfloat16, jnp.int32
MIB = 1 << 20
TOKEN_LIMIT = 16 * MIB


def block_facts(tokens_per_job, block_ids, block_rows):
    job_total = tokens_per_job.shape[0]
    blocks = (tokens_per_job + (block_rows - 1)) // block_rows
    block_ends = jnp.cumsum(blocks, dtype=jnp.int32)
    starts = block_ends - blocks
    job_index = jnp.sum(
        (block_ends[None, :] <= block_ids[:, None]).astype(jnp.int32), axis=1, dtype=jnp.int32
    )
    chosen = job_index[:, None] == jnp.arange(job_total, dtype=jnp.int32)[None, :]
    job_count = jnp.sum(jnp.where(chosen, tokens_per_job[None, :], 0), axis=1, dtype=jnp.int32)
    first_block = jnp.sum(jnp.where(chosen, starts[None, :], 0), axis=1, dtype=jnp.int32)
    valid_rows = jnp.clip(job_count - block_rows * (block_ids - first_block), 0, block_rows)
    return job_index, valid_rows


def shifted(values, axis, count, step):
    if step % count == 0:
        return values
    return lax.ppermute(values, axis, [(i, (i + step) % count) for i in range(count)])


def gather_shifts(values, axis, count):
    return [shifted(values, axis, count, d) for d in range(count)]


def dot(a, b, dims, precision=None):
    return lax.dot_general(a, b, (dims, ((), ())), precision=precision, preferred_element_type=f32)


def tie(*values):
    return lax.optimization_barrier(values)


class Sizes:
    def __init__(self, nd, nt, ns, np_, blocks, halved, width, heads, jobs_dev, rank, columns):
        self.nd, self.nt, self.ns, self.np_ = nd, nt, ns, np_
        self.blocks, self.halved, self.width, self.heads = blocks, halved, width, heads
        self.jobs, self.jobs_dev, self.rank, self.columns = nd * jobs_dev, jobs_dev, rank, columns
        self.wide = self.jobs * rank
        self.rows = blocks * halved
        self.cap = -(-blocks // nd)
        self.slots = nd * self.cap
        self.nq = np_ * ns
        self.fq = width // self.nq
        self.per_head = nd // nt
        at, self.at = 0, {}
        for name, count in (
            ("out_pos", self.slots), ("in_pos", self.slots), ("out_fill", self.slots), ("in_fill", self.slots),
            ("out_rel", blocks), ("in_rel", blocks), ("out_valid", blocks), ("in_valid", blocks),
            ("quarter", self.nq), ("shard", nd), ("head", self.per_head),
            ("pick", self.per_head * nt),
        ):
            self.at[name] = at
            at += count

    def get(self, ref, name, index):
        return ref[self.at[name] + index]


def call(kernel, name, grid, scalars, inputs, in_specs, out_shape, out_specs, flops, moved, limit, scratch=(), alias=None):
    return pl.pallas_call(
        kernel,
        out_shape=out_shape,
        grid_spec=pltpu.PrefetchScalarGridSpec(
            num_scalar_prefetch=1, grid=grid, in_specs=in_specs, out_specs=out_specs, scratch_shapes=list(scratch)
        ),
        input_output_aliases=alias or {},
        compiler_params=pltpu.CompilerParams(vmem_limit_bytes=limit),
        cost_estimate=pl.CostEstimate(flops=flops, bytes_accessed=moved, transcendentals=0),
        name=name,
    )(scalars, *inputs)


ANY = pl.BlockSpec(memory_space=pl.ANY)


def whole(x):
    return pl.BlockSpec(x.shape, lambda *_: (0,) * len(x.shape))


def rows_of(index, z):
    return pl.ds(pl.multiple_of(index * z.halved, z.halved), z.halved)


def row_mask(valid, z, lanes):
    return lax.broadcasted_iota(i32, (z.halved, lanes), 0) < valid


def widen(values, rel, unfold, job_of, z):
    wide = dot(values, unfold, ((1,), (0,)))
    return jnp.where(job_of == rel, wide, 0.0).astype(bf16)


def products_kernel(z, n, sc, tokens, grad, maps, fold, job_of, out, held, sems):
    many = z.blocks // n
    copies = [
        pltpu.make_async_copy(tokens.at[pl.ds(k * n * z.halved, n * z.halved), :], held.at[k], sems.at[k])
        for k in range(many)
    ]
    for copy in copies:
        copy.start()
    back = dot(grad[...], maps[:, z.width :], ((1,), (1,)))
    for block in range(z.blocks):
        own = slice(block * z.halved, (block + 1) * z.halved)
        picked = jnp.where(job_of[...] == z.get(sc, "in_rel", block), back[own], 0.0)
        picked = jnp.where(row_mask(z.get(sc, "in_valid", block), z, z.wide), picked, 0.0)
        out[own, z.rank :] = dot(picked, fold[...], ((1,), (0,)), lax.Precision.HIGHEST).astype(bf16)
    for k in range(many):
        copies[k].wait()
        down = dot(held[k], maps[:, : z.width], ((1,), (1,)))
        for r in range(n):
            block = k * n + r
            own = slice(block * z.halved, (block + 1) * z.halved)
            mine = slice(r * z.halved, (r + 1) * z.halved)
            picked = jnp.where(job_of[...] == z.get(sc, "out_rel", block), down[mine], 0.0)
            out[own, : z.rank] = dot(picked, fold[...], ((1,), (0,)), lax.Precision.HIGHEST).astype(bf16)


def products(z, sc, tokens, grad, maps, fold, job_of):
    n = 2
    shape = jax.ShapeDtypeStruct((z.rows, 2 * z.rank), bf16)
    return call(
        functools.partial(products_kernel, z, n), "adapter_products", (1,), sc,
        (tokens, grad, maps, fold, job_of),
        [ANY, whole(grad), whole(maps), whole(fold), whole(job_of)],
        shape, whole(shape), 1000, 1000, TOKEN_LIMIT,
        scratch=(
            pltpu.VMEM((z.blocks // n, n * z.halved, z.width), bf16),
            pltpu.SemaphoreType.DMA((z.blocks // n,)),
        ),
    )


def sums_kernel(z, sc, *refs):
    parts, outs = refs[: z.nt], refs[z.nt :]
    sums, pays = outs[0], outs[1:]
    total = parts[0][...].astype(f32)
    for part in parts[1:]:
        total = total + part[...].astype(f32)
    sums[...] = total.astype(bf16)
    for d in range(z.nd):
        back = (z.nd - d) % z.nd
        for r in range(z.cap):
            own = slice(r * z.halved, (r + 1) * z.halved)
            picked = sums[rows_of(z.get(sc, "out_pos", d * z.cap + r), z), : z.rank]
            pays[d][own, : z.rank] = jnp.where(z.get(sc, "out_fill", d * z.cap + r) > 0, picked, 0)
            picked = sums[rows_of(z.get(sc, "in_pos", back * z.cap + r), z), z.rank :]
            pays[d][own, z.rank :] = jnp.where(z.get(sc, "in_fill", back * z.cap + r) > 0, picked, 0)


def sums_of(z, sc, parts):
    shapes = [jax.ShapeDtypeStruct((z.rows, 2 * z.rank), bf16)]
    shapes += [jax.ShapeDtypeStruct((z.cap * z.halved, 2 * z.rank), bf16)] * z.nd
    return call(
        functools.partial(sums_kernel, z), "adapter_sums", (1,), sc, parts, [whole(x) for x in parts],
        tuple(shapes), tuple(whole(x) for x in shapes), 1000, 1000, 8 * MIB,
    )


def table_kernel(z, tiles, sc, tokens, grad, unfold, job_of, *refs):
    got, (mine, theirs, back, down, back_t, down_t, held, sems) = refs[: z.nd], refs[z.nd :]
    half = mine.shape[0]
    part = z.width // tiles
    copies = [
        pltpu.make_async_copy(tokens.at[:, pl.ds(k * part, part)], held.at[k], sems.at[k]) for k in range(tiles)
    ]
    for copy in copies:
        copy.start()
    for d in range(z.nd):
        for r in range(z.cap):
            slot = d * z.cap + r
            own = slice(r * z.halved, (r + 1) * z.halved)

            @pl.when(z.get(sc, "out_fill", slot) > 0)
            def _():
                at = z.get(sc, "out_pos", slot)
                values = got[(z.nd - d) % z.nd][own, z.rank :]
                back[rows_of(at, z), :] = widen(values, z.get(sc, "out_rel", at), unfold[...], job_of[...], z)

            @pl.when(z.get(sc, "in_fill", slot) > 0)
            def _():
                at = z.get(sc, "in_pos", slot)
                values = widen(got[d][own, : z.rank], z.get(sc, "in_rel", at), unfold[...], job_of[...], z)
                mask = row_mask(z.get(sc, "in_valid", at), z, z.wide)
                down[rows_of(at, z), :] = jnp.where(mask, values, 0).astype(bf16)

    same = lax.broadcasted_iota(i32, (z.rows, z.rows), 0) == lax.broadcasted_iota(i32, (z.rows, z.rows), 1)
    unit = jnp.where(same, 1.0, 0.0).astype(bf16)
    back_t[...] = dot(back[...], unit, ((0,), (0,))).astype(bf16)
    down_t[...] = dot(down[...], unit, ((0,), (0,))).astype(bf16)
    total = dot(down_t[...], grad[...], ((1,), (0,)))
    mine[:, z.width :] = total[:half]
    theirs[:, z.width :] = total[half:].astype(bf16)
    for k in range(tiles):
        copies[k].wait()
        total = dot(back_t[...], held[k], ((1,), (0,)))
        mine[:, k * part : (k + 1) * part] = total[:half]
        theirs[:, k * part : (k + 1) * part] = total[half:].astype(bf16)


def tables_of(z, sc, tokens, grad, unfold, job_of, got):
    tiles = 4
    shape = jax.ShapeDtypeStruct((z.wide // z.ns, z.width + z.heads), f32)
    sent = jax.ShapeDtypeStruct(shape.shape, bf16)
    return call(
        functools.partial(table_kernel, z, tiles), "job_tables", (1,), sc,
        (tokens, grad, unfold, job_of, *got),
        [ANY, whole(grad), whole(unfold), whole(job_of)] + [whole(x) for x in got],
        (shape, sent), (whole(shape), whole(sent)), 1000, 1000, TOKEN_LIMIT,
        scratch=(pltpu.VMEM((z.rows, z.wide), bf16),) * 2
        + (pltpu.VMEM((z.wide, z.rows), bf16),) * 2
        + (pltpu.VMEM((tiles, z.rows, z.width // tiles), bf16), pltpu.SemaphoreType.DMA((tiles,))),
    )


def layer_kernel(z, sc, sums, maps, unfold, job_of, *refs):
    m = z.per_head
    given, (outs, frozen) = refs[: m * z.nt], (refs[m * z.nt : -1], refs[-1])
    for j in range(m):
        total = given[j][...].astype(f32)
        for d in range(1, z.nt):
            total = total + given[d * m + j][...].astype(f32)
        for i in range(m):

            @pl.when(z.get(sc, "head", j) == i)
            def _():
                frozen[:, i * z.columns : (i + 1) * z.columns] = total

    for d in range(z.nd):
        for r in range(z.cap):
            slot = d * z.cap + r
            at = z.get(sc, "out_pos", slot)
            valid = jnp.where(z.get(sc, "out_fill", slot) > 0, z.get(sc, "out_valid", at), 0)
            wide = widen(sums[rows_of(at, z), : z.rank], z.get(sc, "out_rel", at), unfold[...], job_of[...], z)
            adapter = dot(wide, maps[...], ((1,), (0,)))
            layer = frozen[rows_of(at, z), :] + adapter_scale * adapter
            layer = jnp.where(row_mask(valid, z, z.heads), layer, 0.0)
            outs[d][r * z.halved : (r + 1) * z.halved, :] = layer.astype(bf16)


def layer_of(z, sc, sums, maps, unfold, job_of, given):
    shapes = [jax.ShapeDtypeStruct((z.cap * z.halved, z.heads), bf16)] * z.nd
    at = z.width // z.heads
    return call(
        functools.partial(layer_kernel, z), "layer", (1,), sc, (sums, maps, unfold, job_of, *given),
        [whole(sums), pl.BlockSpec((z.wide, z.heads), lambda i, _: (0, at)), whole(unfold), whole(job_of)]
        + [whole(x) for x in given],
        tuple(shapes), tuple(whole(x) for x in shapes),
        2 * z.rows * z.wide * z.heads, 6 * z.rows * z.heads, 12 * MIB,
        scratch=(pltpu.VMEM((z.rows, z.heads), f32),),
    )


def place_kernel(z, sc, *refs):
    got, out = refs[: z.nd], refs[z.nd]
    for d in range(z.nd):
        for r in range(z.cap):
            slot = d * z.cap + r

            @pl.when(z.get(sc, "in_fill", slot) > 0)
            def _():
                out[rows_of(z.get(sc, "in_pos", slot), z), :] = got[d][r * z.halved : (r + 1) * z.halved, :]


def place(z, sc, got):
    shape = jax.ShapeDtypeStruct((z.rows, z.heads), bf16)
    return call(
        functools.partial(place_kernel, z), "place", (1,), sc, got, [whole(x) for x in got],
        shape, whole(shape), 1000, 4 * z.rows * z.heads, 8 * MIB,
    )


def gradient_kernel(z, count, per, aliased, sc, maps, sums, unfold, job_of, *refs):
    grads, refs = refs[: z.nt], refs[z.nt :]
    pieces, refs = refs[: z.nd * count], refs[z.nd * count :]
    out, grad, back = refs[1:] if aliased else refs
    step = pl.program_id(0)
    m = z.per_head

    @pl.when(step == 0)
    def _():
        for v in range(z.nt * m):
            grad[v] = grads[v // m][:, v % m * z.columns : (v % m + 1) * z.columns]
        for b in range(z.blocks):
            own = slice(b * z.halved, (b + 1) * z.halved)
            back[own, :] = widen(sums[own, z.rank :], z.get(sc, "in_rel", b), unfold[...], job_of[...], z)

    for k in range(count):

        @pl.when(step // per == k)
        def _():
            total = adapter_scale * dot(back[...], maps[...], ((1,), (0,)))
            for d in range(z.nd):
                total = total + dot(grad[z.get(sc, "shard", d)], pieces[d * count + k][...], ((1,), (1,)))
            for b in range(z.blocks):
                own = slice(b * z.halved, (b + 1) * z.halved)
                mask = row_mask(z.get(sc, "in_valid", b), z, total.shape[1])
                out[own, :] = jnp.where(mask, total[own], 0.0).astype(bf16)


def token_gradient_of(z, sc, grads, maps, sums, unfold, job_of, piece_list, quarters, before):
    tile = min(1024, z.fq)
    per = z.fq // tile
    at = z.at["quarter"]
    first, count = quarters[0], len(quarters)
    block = lambda i, q: (0, q[at + first + i // per] * per + i % per)
    specs, flat = [], []
    for d in range(z.nd):
        for k, r in enumerate(quarters):
            inner = lambda i, k=k: jnp.clip(i - k * per, 0, per - 1)
            if d == 0:
                index = lambda i, q, r=r, inner=inner: (q[at + r] * per + inner(i), 0)
            else:
                index = lambda i, q, inner=inner: (inner(i), 0)
            specs.append(pl.BlockSpec((tile, z.columns), index))
            flat.append(piece_list[d][r])
    inputs = [maps, sums, unfold, job_of, *grads, *flat]
    in_specs = [pl.BlockSpec((z.wide, tile), block), whole(sums), whole(unfold), whole(job_of)]
    in_specs += [whole(x) for x in grads] + specs
    alias = None
    if before is not None:
        alias = {1 + len(inputs): 0}
        inputs.append(before)
        in_specs.append(pl.BlockSpec(memory_space=pl.ANY))
    return call(
        functools.partial(gradient_kernel, z, count, per, before is not None),
        "token_gradient_%d" % first, (count * per,), sc, inputs, in_specs,
        jax.ShapeDtypeStruct((z.rows, z.width), bf16), pl.BlockSpec((z.rows, tile), block),
        1000 if alias is None else 2 * z.rows * count * z.fq * (z.nd * z.columns + z.wide),
        1000 if alias is None else 2 * count * z.fq * (z.rows + z.nd * z.columns),
        (20 if alias is None else 61) * MIB,
        scratch=(pltpu.VMEM((z.nd, z.rows, z.columns), bf16), pltpu.VMEM((z.rows, z.wide), bf16)),
        alias=alias,
    )


def body(
    tokens,
    cotangent,
    frozen_value_weight,
    adapter_down,
    adapter_up,
    tokens_per_job,
    packed_block_slots,
):
    nd, nt, ns, np_ = (lax.axis_size(a) for a in ("dp", "tensor", "sub", "parts"))
    z, t, s, p = (lax.axis_index(a) for a in ("dp", "tensor", "sub", "parts"))
    blocks, halved, width = tokens.shape[1:]
    heads = cotangent.shape[3]
    jobs_dev, rank, _ = adapter_down.shape
    columns = frozen_value_weight.shape[1]
    zz = Sizes(nd, nt, ns, np_, blocks, halved, width, heads, jobs_dev, rank, columns)
    rows, r2, m, cap = zz.rows, rank // ns, zz.per_head, zz.cap
    own_tokens = tokens.reshape(rows, width)
    own_grad = cotangent.reshape(rows, heads)

    quarters = jnp.stack([(p - a) % np_ * ns + (s - b) % ns for a in range(np_) for b in range(ns)]).astype(i32)
    moving = lax.dynamic_slice_in_dim(frozen_value_weight, (p * ns + s) * zz.fq, zz.fq, axis=0)

    maps = jnp.concatenate([adapter_down, adapter_up], axis=2).reshape(jobs_dev, ns, r2, width + heads)
    maps = lax.dynamic_index_in_dim(maps, s, 1, keepdims=False)
    maps, moving = tie(maps, moving)
    rounds = [None, shifted(moving, "dp", nd, 1)]
    token_quarters = [lax.dynamic_slice_in_dim(own_tokens, quarters[r] * zz.fq, zz.fq, 1) for r in range(zz.nq)]
    def arrival(index):
        found = (z - index * m - jnp.arange(m, dtype=i32)) % nd
        place_of = jnp.sum((found[None, :] < found[:, None]).astype(i32), axis=1)
        match = place_of[None, :] == jnp.arange(m, dtype=i32)[:, None]
        return jnp.sum(jnp.where(match, found[None, :], 0), axis=1, dtype=i32)

    arrivals = [arrival((t + g) % nt) for g in range(nt)]
    chosen = [[[x[j] == k for k in range(nd)] for j in range(m)] for x in arrivals]
    scale = adapter_scale / lax.dynamic_slice_in_dim(tokens_per_job, z * jobs_dev, jobs_dev).astype(f32)
    maps, rounds[1], token_quarters, chosen, scale = tie(
        gather_shifts(maps, "dp", nd), rounds[1], token_quarters, chosen, scale
    )
    maps = jnp.concatenate(maps, axis=0).reshape(zz.jobs * r2, -1)
    maps = jnp.concatenate(gather_shifts(maps, "sub", ns), axis=0)
    grads = gather_shifts(own_grad, "tensor", nt)

    positions = jnp.arange(blocks, dtype=i32)
    dest = packed_block_slots // blocks
    same = dest[:, :, None] == dest[:, None, :]
    earlier = positions[None, None, :] < positions[None, :, None]
    send_rank = jnp.sum((same & earlier).astype(i32), axis=2, dtype=i32)
    flat_slots = packed_block_slots.reshape(-1)
    flat_ids = jnp.arange(nd * blocks, dtype=i32)
    slot_owner = flat_slots[None, :] == (z * blocks + positions)[:, None]
    block_ids = jnp.sum(jnp.where(slot_owner, flat_ids[None, :], 0), axis=1, dtype=i32)
    in_rank = jnp.sum(jnp.where(slot_owner, send_rank.reshape(-1)[None, :], 0), axis=1, dtype=i32)
    in_slot = (z - block_ids // blocks) % nd * cap + in_rank
    own_dest = lax.dynamic_index_in_dim(dest, z, 0, keepdims=False)
    own_rank = lax.dynamic_index_in_dim(send_rank, z, 0, keepdims=False)
    out_slot = (own_dest - z) % nd * cap + own_rank
    slot_range = jnp.arange(zz.slots, dtype=i32)

    def positions_of(slots):
        match = slots[None, :] == slot_range[:, None]
        return jnp.sum(jnp.where(match, positions[None, :], 0), axis=1, dtype=i32), jnp.any(match, axis=1)

    out_pos, out_fill = positions_of(out_slot)
    in_pos, in_fill = positions_of(in_slot)

    def facts(ids):
        job, valid = block_facts(tokens_per_job, ids, halved * ns)
        return (z - job // jobs_dev) % nd * jobs_dev + job % jobs_dev, valid - s * halved

    out_rel, out_valid = facts(z * blocks + positions)
    in_rel, in_valid = facts(block_ids)

    shard_of = (z - jnp.arange(nd, dtype=i32)) % nd
    shard_at = (t - shard_of // m) % nt * m + shard_of % m
    head_at = (z - arrivals[0]) % nd - t * m
    sc = jnp.concatenate(
        [
            x.astype(i32)
            for x in (out_pos, in_pos, out_fill, in_fill, out_rel, in_rel, out_valid, in_valid, quarters, shard_at, head_at, *arrivals)
        ]
    )
    column = jnp.arange(zz.wide, dtype=i32)
    job_of = (column // r2 % zz.jobs)[None, :]
    rank_of = column // (zz.jobs * r2) * r2 + column % r2
    unfold = (jnp.arange(rank, dtype=i32)[:, None] == rank_of[None, :]).astype(bf16)
    fold = unfold.astype(f32).T

    def product(pieces, first=0):
        return sum(dot(token_quarters[first + r], x, ((1,), (0,))) for r, x in enumerate(pieces))

    def spread_round(over_parts):
        return [x for y in over_parts for x in gather_shifts(y, "sub", ns)]

    last = nd - 1
    over = [None] * nd
    over[1] = gather_shifts(rounds[1], "parts", np_)
    for d in range(2, last):
        rounds.append(shifted(rounds[-1], "dp", nd, 1))
    swapped = gather_shifts(over[1][0], "sub", ns)
    maps, swapped = tie(maps, swapped)
    part = products(zz, sc, own_tokens, own_grad, maps, fold, job_of)
    parts = gather_shifts(part, "tensor", nt)
    late_weight, _ = tie(frozen_value_weight, part)
    base = [dot(own_tokens, late_weight, ((1,), (0,))).astype(bf16)]
    base[0], parts, grads = tie(base[0], parts, grads)
    sums, *pays = sums_of(zz, sc, parts)
    rounds[last - 1], over[1], sums = tie(rounds[last - 1], over[1], sums)

    end = shifted(rounds[last - 1], "dp", nd, 1)
    for d in range(2, last):
        over[d] = gather_shifts(rounds[d], "parts", np_)
    piece_list = [[frozen_value_weight] * zz.nq, swapped + spread_round(over[1][1:])]
    crossed = [gather_shifts(over[d][0], "sub", ns) for d in range(2, last)]
    piece_list[1], crossed = tie(piece_list[1], crossed)
    base.append(product(piece_list[1]).astype(bf16))
    base[1], end, over[2:last], pays = tie(base[1], end, over[2:last], pays)

    behind = gather_shifts(end, "parts", np_)
    got = [shifted(pays[d], "dp", nd, d) for d in range(nd)]
    piece_list += [crossed[d - 2] + spread_round(over[d][1:]) for d in range(2, last)]

    slots = []

    def finish(values):
        base.append(values.astype(bf16))
        due = len(base) - 1 - (nd - m)
        if due >= 0:
            made = []
            for g in range(nt):
                picked = base[-1]
                for k in range(due, len(base) - 1):
                    picked = jnp.where(chosen[g][due][k], base[k], picked)
                made.append(shifted(picked, "tensor", nt, g))
            slots.append(made)

    for d in range(2, last):
        finish(product(piece_list[d]))
    base[-1], got = tie(base[-1], got)
    mine, theirs = tables_of(zz, sc, own_tokens, own_grad, unfold, job_of, got)
    theirs = shifted(theirs, "sub", ns, 1)
    ahead = gather_shifts(end, "sub", ns)
    ahead, mine = tie(ahead, mine)
    begun = product(ahead)
    begun, behind, slots = tie(begun, behind, slots)
    tail = spread_round(behind[1:])
    piece_list.append(ahead + tail)
    finish(begun + product(tail, len(ahead)))
    base[-1], mine, theirs, grads = tie(base[-1], mine, theirs, grads)

    summed = (mine + theirs).reshape(nd, jobs_dev * r2, -1)
    sending = [summed[d].astype(bf16) for d in range(nd)]
    tables = [sending[0]] + [shifted(sending[d], "dp", nd, -d) for d in range(1, nd)]

    half = zz.nq // 2
    gradient = token_gradient_of(zz, sc, grads, maps, sums, unfold, job_of, piece_list, list(range(half)), None)
    given = [slots[j][d] for d in range(nt) for j in range(m)]
    gradient, given = tie(gradient, given)
    layer = layer_of(zz, sc, sums, maps, unfold, job_of, given)
    layer, gradient, tables = tie(layer, gradient, tables)
    landed = [shifted(layer[d], "dp", nd, d) for d in range(nd)]
    total = sum(x.astype(f32) for x in tables)
    total = total.reshape(jobs_dev, r2, -1) * scale[:, None, None]
    halves = gather_shifts(total, "sub", ns)
    gradient, halves = tie(gradient, halves)
    owned = jnp.concatenate(
        [sum(jnp.where((s - h) % ns == k, x, 0.0) for k, x in enumerate(halves)) for h in range(ns)], axis=1
    )
    grad_down, grad_up = owned[:, :, :width], owned[:, :, width:]
    gradient, grad_down, grad_up = tie(gradient, grad_down, grad_up)
    gradient = token_gradient_of(
        zz, sc, grads, maps, sums, unfold, job_of, piece_list, list(range(half, zz.nq)), gradient
    )
    gradient, grad_down, grad_up, landed = tie(gradient, grad_down, grad_up, landed)
    layer_output = place(zz, sc, landed)
    return (
        layer_output.reshape(1, blocks, halved, heads),
        gradient.reshape(1, blocks, halved, width),
        grad_down,
        grad_up,
    )


def solution(mesh):
    return jax.shard_map(
        body,
        mesh=mesh,
        in_specs=(
            P(("parts", "dp"), None, "sub", "tensor"),
            P(("parts", "dp"), None, "sub", "tensor"),
            P("tensor", "dp"),
            P(("parts", "dp"), None, "tensor"),
            P(("parts", "dp"), None, "tensor"),
            P("parts"),
            P("parts", None),
        ),
        out_specs=(
            P(("parts", "dp"), None, "sub", "tensor"),
            P(("parts", "dp"), None, "sub", "tensor"),
            P(("parts", "dp"), None, "tensor"),
            P(("parts", "dp"), None, "tensor"),
        ),
        check_vma=False,
    )
```
